32 devices in a mesh: dp: 8 (over z, x), head: 4 (over y, core).
Axes of the slice: x: 2, y: 2, z: 4, core: 2. Of those that a mesh axis runs over, the one named last changes fastest.
Arguments:
- frames: bfloat16 [6144, 1024], P(('dp', 'head')), may hold values from -6 to 6
- cotangent: bfloat16 [6144, 1024], P(('dp', 'head')), may hold values from -6 to 6
- lengths: int32 [8, 2], P('dp'), may hold values from 145 to 432, as said below
- norm_gains: bfloat16 [6, 1024], P(None, ('dp', 'head')), may hold values from 0.099609375 to 1.8984375
- position_bias: bfloat16 [1024], P(('dp', 'head')), may hold values from -4 to 4
- attend_weight: bfloat16 [1024, 3072], P(('dp', 'head')), may hold values from -0.1875 to 0.1875
- merge_weight: bfloat16 [1024, 1024], P(('dp', 'head')), may hold values from -1.5 to 1.5
- glu_weight: bfloat16 [1024, 2048], P(('dp', 'head')), may hold values from -0.1875 to 0.1875
- depth_weight: bfloat16 [31, 1024], P(None, ('dp', 'head')), may hold values from -1 to 1
- point_weight: bfloat16 [1024, 1024], P(('dp', 'head')), may hold values from -0.1875 to 0.1875
- inner_weight: bfloat16 [2, 1024, 4096], P(None, None, ('dp', 'head')), may hold values from -0.1875 to 0.1875
- outer_weight: bfloat16 [2, 4096, 1024], P(None, ('dp', 'head')), may hold values from -0.09375 to 0.09375
Outputs:
- layer_out: bfloat16 [6144, 1024], P(('dp', 'head'))
- frames_grad: float32 [6144, 1024], P(('dp', 'head'))
- gains_grad: float32 [6, 1024], P(None, ('dp', 'head'))
- position_grad: float32 [1024], P(('dp', 'head'))
- attend_grad: float32 [1024, 3072], P(('dp', 'head'))
- merge_grad: float32 [1024, 1024], P(('dp', 'head'))
- glu_grad: float32 [1024, 2048], P(('dp', 'head'))
- depth_grad: float32 [31, 1024], P(None, ('dp', 'head'))
- point_grad: float32 [1024, 1024], P(('dp', 'head'))
- inner_grad: float32 [2, 1024, 4096], P(None, None, ('dp', 'head'))
- outer_grad: float32 [2, 4096, 1024], P(None, ('dp', 'head'))
The draws below stay inside these ranges and needn't reach their ends.
Inputs may be any that keep to these rules, and one draw needn't show every extreme that they name: `lengths`: in every row the second utterance has exactly 432 frames; the first has fewer than 192 frames, and so has the third, which holds the rest of the group's frames. In some row the first utterance has the least number of frames.
All inputs are finite; a program needn't handle non-finite values.
Results may differ from the reference program's by a relative error of at most 0.017.
Values may be sent and summed in bfloat16 or wider, within the bound.
No kernel may reach another device: no remote copies, remote signals or barrier semaphores. Data moves between devices by JAX's collectives and lax.ppermute only.
A program may use at most 384 MiB of HBM per device.

```python
import jax
import jax.numpy as jnp
from jax import lax

D = 1024
HEADS = 16
HD = 64
FF = 4096
KERNEL = 31
NB = 64
TOK_DEV = 192
GROUPS = 8
GROUP_TOK = 768
TOKENS = 6144
SHORTS = 336
MAXLEN = 432


def draw_lengths(key, part):
    key = jax.random.fold_in(key, 7)
    lowest = SHORTS - TOK_DEV + 1
    leading = jax.random.randint(key, (GROUPS,), lowest, TOK_DEV).astype(jnp.int32)
    chosen = jax.random.randint(jax.random.fold_in(key, 11), (), 0, GROUPS).astype(jnp.int32)
    leading = jnp.where(jnp.arange(GROUPS, dtype=jnp.int32) == chosen, jnp.int32(lowest), leading).astype(jnp.int32)
    longest = jnp.full((GROUPS,), MAXLEN, jnp.int32)
    return jnp.stack([leading, longest], 1).astype(jnp.int32)


def block_levels(stream_key, dims, pieces, smallest, top_value):
    loudness, own = 1.0, jax.random.fold_in(stream_key, 6)
    for axis_at, blocks in pieces:
        steps = jnp.exp(jax.random.uniform(jax.random.fold_in(own, axis_at), (blocks,), jnp.float32, smallest / len(pieces), top_value / len(pieces)))
        loudness = loudness * jnp.repeat(steps, dims[axis_at] // blocks).reshape([-1 if axis == axis_at else 1 for axis in range(len(dims))])
    return loudness


def bell_draw(rng, extent, scale, bound, shards=(), held_as=jnp.bfloat16):
    array = scale * jax.random.normal(rng, extent, jnp.float32)
    if shards:
        array = array * block_levels(rng, extent, shards, -0.22, 0.18)
    return jnp.clip(array, -bound, bound).astype(held_as)


def setup_inputs(seed: int = 0) -> dict:
    key_list = jax.random.split(jax.random.key(seed), 13)
    return {
        "frames": bell_draw(key_list[0], (TOKENS, D), 1.0, 6.0, ((0, 32),)),
        "cotangent": bell_draw(key_list[1], (TOKENS, D), 1.0, 6.0, ((0, 32),)),
        "lengths": draw_lengths(jax.random.fold_in(key_list[12], 71), 0),
        "norm_gains": jnp.clip(1.0 + 0.18 * jax.random.normal(key_list[3], (6, D), jnp.float32), 0.099609375, 1.8984375).astype(jnp.bfloat16),
        "position_bias": bell_draw(key_list[4], (NB * HEADS,), 1.0, 4.0, ((0, 32),)),
        "attend_weight": bell_draw(key_list[5], (D, 3 * D), D ** -0.5, 0.1875, ((0, 32),)),
        "merge_weight": bell_draw(key_list[6], (D, D), (D // 64) ** -0.5, 1.5, ((0, 32),)),
        "glu_weight": bell_draw(key_list[7], (D, 2 * D), D ** -0.5, 0.1875, ((0, 32),)),
        "depth_weight": bell_draw(key_list[8], (KERNEL, D), KERNEL ** -0.5, 1.0, ((1, 32),)),
        "point_weight": bell_draw(key_list[9], (D, D), D ** -0.5, 0.1875, ((0, 32),)),
        "inner_weight": bell_draw(key_list[10], (2, D, FF), D ** -0.5, 0.1875, ((2, 32),)),
        "outer_weight": bell_draw(key_list[11], (2, FF, D), FF ** -0.5, 0.09375, ((1, 32),)),
    }


@jax.custom_vjp
def low(v):
    return lax.optimization_barrier(v.astype(jnp.bfloat16)).astype(jnp.float32)

@jax.custom_vjp
def low_back(v):
    return v

def low_keep(v):
    return (low(v), None)

def low_pass(kept, grad):
    return (grad,)

def back_keep(v):
    return (v, None)

def back_low(kept, grad):
    return (low(grad),)
low.defvjp(low_keep, low_pass)
low_back.defvjp(back_keep, back_low)
EPS = 1e-05

def matmul(left_in, right_in):
    return jnp.dot(left_in, right_in, precision=lax.Precision.HIGHEST)

def normalize(values, gain):
    average = lax.optimization_barrier(jnp.mean(values, axis=-1, keepdims=True))
    centred = values - average
    spread = lax.optimization_barrier(jnp.mean(centred * centred, axis=-1, keepdims=True))
    return centred * lax.rsqrt(spread + EPS) * gain

def segments_of(lengths_row, positions):
    first_end = lengths_row[0]
    second_end = first_end + lengths_row[1]
    return (positions >= first_end).astype(jnp.int32) + (positions >= second_end).astype(jnp.int32)

def buckets_of(query_pos, key_pos):
    offset = query_pos[:, None] - key_pos[None, :]
    distance = jnp.abs(offset)
    level = jnp.zeros_like(distance)
    for power in range(1, 14):
        level = level + (distance >= 2 ** power).astype(jnp.int32)
    plain = jnp.where(distance < 16, distance, jnp.minimum(12 + level, 31))
    return (plain + 32 * (offset < 0).astype(jnp.int32)).astype(jnp.int32)

def feed_half(hidden, gain, inner, outer):
    entry = low(normalize(hidden, gain))
    middle = low_back(matmul(entry, inner))
    activated = low(jax.nn.silu(middle))
    return hidden + 0.5 * low_back(matmul(activated, outer))

def group_layer(group_rows, lengths_row, params):
    gains, position_bias, attend_weight, merge_weight, glu_weight, depth_weight, point_weight, inner_weight, outer_weight = params
    positions = jnp.arange(GROUP_TOK, dtype=jnp.int32)
    segment = segments_of(lengths_row, positions)
    first = feed_half(group_rows, gains[0], inner_weight[0], outer_weight[0])
    att_entry = low(normalize(first, gains[1]))
    triple = low(low_back(matmul(att_entry, attend_weight))).reshape(GROUP_TOK, 3, HEADS, HD)
    table = position_bias.reshape(NB, HEADS).T
    bucket = buckets_of(positions, positions)
    same = segment[:, None] == segment[None, :]

    def one_head(items):
        queries, key_rows, value_rows, column = items
        raw = low_back(matmul(queries, key_rows.T))
        scores = jnp.where(same, raw * 0.125 + jnp.take(column, bucket), -1e+30)
        weights = low(jax.nn.softmax(scores, axis=-1))
        return low(low_back(matmul(weights, value_rows)))
    heads_out = lax.map(jax.checkpoint(one_head), (triple[:, 0].transpose(1, 0, 2), triple[:, 1].transpose(1, 0, 2), triple[:, 2].transpose(1, 0, 2), table))
    attended = heads_out.transpose(1, 0, 2).reshape(GROUP_TOK, D)
    second = first + low_back(matmul(attended, merge_weight))
    conv_entry = low(normalize(second, gains[2]))
    gate_up = low_back(matmul(conv_entry, glu_weight))
    glu_rows = low(gate_up[:, :D] * jax.nn.sigmoid(gate_up[:, D:]))
    margin = (KERNEL - 1) // 2
    padded = jnp.pad(glu_rows, ((margin, margin), (0, 0)))
    segment_pad = jnp.pad(segment, (margin, margin), constant_values=-1)
    mixed = jnp.zeros((GROUP_TOK, D), jnp.float32)
    for tap in range(KERNEL):
        match = (segment_pad[tap:tap + GROUP_TOK] == segment).astype(jnp.float32)[:, None]
        mixed = mixed + depth_weight[tap] * padded[tap:tap + GROUP_TOK] * match
    mixed = low_back(mixed)
    swish = low(jax.nn.silu(normalize(mixed, gains[3])))
    third = second + low_back(matmul(swish, point_weight))
    fourth = feed_half(third, gains[4], inner_weight[1], outer_weight[1])
    return normalize(fourth, gains[5])

def reference(frames, cotangent, lengths, norm_gains, position_bias, attend_weight, merge_weight, glu_weight, depth_weight, point_weight, inner_weight, outer_weight):
    params = tuple((item.astype(jnp.float32) for item in (norm_gains, position_bias, attend_weight, merge_weight, glu_weight, depth_weight, point_weight, inner_weight, outer_weight)))
    inputs = frames.astype(jnp.float32).reshape(GROUPS, GROUP_TOK, D)

    def whole(values, weights):
        layer = jax.checkpoint(group_layer)
        return lax.map(lambda items: layer(items[0], items[1], weights), (values, lengths))
    result, pull = jax.vjp(whole, inputs, params)
    input_grad, weight_grads = pull(cotangent.astype(jnp.float32).reshape(GROUPS, GROUP_TOK, D))
    return (result.reshape(TOKENS, D).astype(jnp.bfloat16), input_grad.reshape(TOKENS, D), weight_grads[0], weight_grads[1], weight_grads[2], weight_grads[3], weight_grads[4], weight_grads[5], weight_grads[6], weight_grads[7], weight_grads[8])
```

```python
import jax
import jax.numpy as jnp
from jax import lax
from jax.experimental import pallas as pl
from jax.experimental.pallas import tpu as pltpu
from jax.sharding import Mesh
from jax.sharding import PartitionSpec as P

HEADS = 16
HD = 64
NB = 64
ROWS = 128
VMEM = 50 * 1024 * 1024


def matmul_in(left, right, dims):
    return lax.dot_general(left, right, (dims, ((), ())), preferred_element_type=jnp.float32)


def spread_bias(info_ref, bias_ref, spread_ref):
    width = spread_ref.shape[1]
    row = jnp.broadcast_to(bias_ref[0], (ROWS, width))
    spread_ref[...] = pltpu.roll(row, 0, 1, stride=1, stride_axis=0)


def half_mask(rows):
    lane = lax.broadcasted_iota(jnp.int32, (rows, 2 * HD), 1)
    start = lax.rem(pl.program_id(0), 2) * HD
    return (lane >= start) & (lane < start + HD)


def segment_at(position, first_end, second_end):
    return (position >= first_end).astype(jnp.int32) + (position >= second_end).astype(jnp.int32)


def weights_of(info_ref, spread_ref, query, keys, number):
    group = keys.shape[0]
    first_end, second_end, start = info_ref[0], info_ref[1], info_ref[2]
    raw = matmul_in(query, keys, ((1,), (1,)))
    shift = pl.multiple_of(group - start - number * ROWS, ROWS)
    bias = spread_ref[:, pl.ds(shift, group)]
    row = start + number * ROWS + lax.broadcasted_iota(jnp.int32, (ROWS, 1), 0)
    column = lax.broadcasted_iota(jnp.int32, (1, group), 1)
    same = segment_at(row, first_end, second_end) == segment_at(column, first_end, second_end)
    scores = jnp.where(same, raw * 0.125 + bias, -1e30)
    raised = jnp.exp(scores - jnp.max(scores, axis=1, keepdims=True))
    return raised * (1.0 / jnp.sum(raised, axis=1, keepdims=True))


def attend_kernel(info_ref, bias_ref, query_ref, key_ref, value_ref, out_ref, spread_ref):
    spread_bias(info_ref, bias_ref, spread_ref)
    mask = half_mask(ROWS)
    first = lax.rem(pl.program_id(0), 2) == 0
    for number in range(query_ref.shape[0] // ROWS):
        rows = pl.ds(number * ROWS, ROWS)
        query = jnp.where(mask, query_ref[rows, :], jnp.bfloat16(0))
        weights = weights_of(info_ref, spread_ref, query, key_ref[...], number)
        out = matmul_in(weights.astype(jnp.bfloat16), value_ref[...], ((1,), (0,)))
        out = out.astype(jnp.bfloat16)
        kept = jnp.where(first, out, out_ref[rows, :])
        out_ref[rows, :] = jnp.where(mask, out, kept)


def attend_back_kernel(
    info_ref,
    bias_ref,
    query_ref,
    key_ref,
    value_ref,
    grad_ref,
    query_grad_ref,
    key_grad_ref,
    value_grad_ref,
    sums_ref,
    spread_ref,
    diag_ref,
    weight_ref,
    score_ref,
    query_mid_ref,
    grad_mid_ref,
):
    spread_bias(info_ref, bias_ref, spread_ref)
    mask = half_mask(ROWS)
    group, width = key_ref.shape[0], spread_ref.shape[1]
    first = lax.rem(pl.program_id(0), 2) == 0
    diag_ref[...] = jnp.zeros(diag_ref.shape, jnp.float32)
    for number in range(query_ref.shape[0] // ROWS):
        rows = pl.ds(number * ROWS, ROWS)
        query = jnp.where(mask, query_ref[rows, :], jnp.bfloat16(0))
        grad = jnp.where(mask, grad_ref[rows, :], jnp.bfloat16(0))
        query_mid_ref[rows, :] = query
        grad_mid_ref[rows, :] = grad
        weights = weights_of(info_ref, spread_ref, query, key_ref[...], number)
        weight_ref[rows, :] = weights.astype(jnp.bfloat16)
        weight_grad = matmul_in(grad, value_ref[...], ((1,), (1,)))
        inner = jnp.sum(weights * weight_grad, axis=1, keepdims=True)
        score_grad = weights * (weight_grad - inner)
        shift = pl.multiple_of(group - info_ref[2] - number * ROWS, ROWS)
        diag_ref[:, pl.ds(shift, group)] += score_grad
        raw_grad = (score_grad * 0.125).astype(jnp.bfloat16)
        score_ref[rows, :] = raw_grad
        out = matmul_in(raw_grad, key_ref[...], ((1,), (0,))).astype(jnp.bfloat16)
        kept = jnp.where(first, out, query_grad_ref[rows, :])
        query_grad_ref[rows, :] = jnp.where(mask, out, kept)
    key_grad = matmul_in(score_ref[...], query_mid_ref[...], ((0,), (0,)))
    value_grad = matmul_in(weight_ref[...], grad_mid_ref[...], ((0,), (0,)))

    @pl.when(first)
    def _():
        key_grad_ref[...] = key_grad
        value_grad_ref[...] = value_grad

    @pl.when(jnp.logical_not(first))
    def _():
        key_grad_ref[...] += key_grad
        value_grad_ref[...] += value_grad

    total = diag_ref[...]
    size = ROWS // 2
    while size >= 8:
        total = total[:size] + pltpu.roll(total[size:], width - size, 1)
        size //= 2
    for size in (4, 2, 1):
        total = total + pltpu.roll(pltpu.roll(total, 8 - size, 0), width - size, 1)
    sums_ref[0] = total[0:1]


def attend_specs(rows, group, width, pairs):
    return [
        pl.BlockSpec(memory_space=pltpu.SMEM),
        pl.BlockSpec((1, 1, width), lambda h: (h, 0, 0)),
        pl.BlockSpec((rows, 2 * HD), lambda h: (0, h // 2)),
        pl.BlockSpec((group, 2 * HD), lambda h: (0, h // 2)),
        pl.BlockSpec((group, 2 * HD), lambda h: (0, pairs + h // 2)),
    ]


def attend(info, bias, query, both):
    heads, _, width = bias.shape
    rows, group = query.shape[0], both.shape[0]
    pairs = heads // 2
    return pl.pallas_call(
        attend_kernel,
        grid=(heads,),
        in_specs=attend_specs(rows, group, width, pairs),
        out_specs=pl.BlockSpec((rows, 2 * HD), lambda h: (0, h // 2)),
        out_shape=jax.ShapeDtypeStruct((rows, heads * HD), jnp.bfloat16),
        scratch_shapes=[pltpu.VMEM((ROWS, width), jnp.float32)],
        compiler_params=pltpu.CompilerParams(vmem_limit_bytes=VMEM),
        name="attend",
    )(info, bias, query, both, both)


def attend_back(info, bias, query, both, grad):
    heads, _, width = bias.shape
    rows, group = query.shape[0], both.shape[0]
    pairs = heads // 2
    pair_block = pl.BlockSpec((rows, 2 * HD), lambda h: (0, h // 2))
    group_block = pl.BlockSpec((group, 2 * HD), lambda h: (0, h // 2))
    return pl.pallas_call(
        attend_back_kernel,
        grid=(heads,),
        in_specs=attend_specs(rows, group, width, pairs) + [pair_block],
        out_specs=[pair_block, group_block, group_block, pl.BlockSpec((1, 1, width), lambda h: (h, 0, 0))],
        out_shape=[
            jax.ShapeDtypeStruct((rows, heads * HD), jnp.bfloat16),
            jax.ShapeDtypeStruct((group, heads * HD), jnp.float32),
            jax.ShapeDtypeStruct((group, heads * HD), jnp.float32),
            jax.ShapeDtypeStruct((heads, 1, width), jnp.float32),
        ],
        scratch_shapes=[
            pltpu.VMEM((ROWS, width), jnp.float32),
            pltpu.VMEM((ROWS, width), jnp.float32),
            pltpu.VMEM((rows, group), jnp.bfloat16),
            pltpu.VMEM((rows, group), jnp.bfloat16),
            pltpu.VMEM((rows, 2 * HD), jnp.bfloat16),
            pltpu.VMEM((rows, 2 * HD), jnp.bfloat16),
        ],
        compiler_params=pltpu.CompilerParams(vmem_limit_bytes=VMEM),
        name="attend_back",
    )(info, bias, query, both, both, grad)


LANES = 128
EDGE = 16


def reach_of(info_ref, rows, group):
    position = info_ref[2] + lax.broadcasted_iota(jnp.int32, (rows, LANES), 0)
    first_end, second_end = info_ref[0], info_ref[1]
    low = jnp.where(position >= second_end, second_end, jnp.where(position >= first_end, first_end, 0))
    high = jnp.where(position < first_end, first_end, jnp.where(position < second_end, second_end, group))
    return (low - position, high - position)


def within(reach, shift):
    if shift < 0:
        return reach[0] <= shift
    return reach[1] > shift


def fill(pad_ref, low_ref, mid_ref, high_ref):
    rows = mid_ref.shape[0]
    pad_ref[0:EDGE, :] = low_ref[...].astype(jnp.float32)
    pad_ref[EDGE : EDGE + rows, :] = mid_ref[...].astype(jnp.float32)
    pad_ref[EDGE + rows :, :] = high_ref[...].astype(jnp.float32)


def taps_of(pad_ref, depth_ref, reach, base, rows, taps, mirror):
    margin = (taps - 1) // 2
    total = jnp.zeros((rows, LANES), jnp.float32)
    for tap in range(taps):
        shift = margin - tap if mirror else tap - margin
        piece = pad_ref[EDGE + base + shift : EDGE + base + shift + rows, :] * depth_ref[tap : tap + 1, :]
        if shift:
            piece = jnp.where(within(reach, shift), piece, 0.0)
        total = total + piece
    return total


def conv_kernel(group, taps, info_ref, low_ref, mid_ref, high_ref, depth_ref, out_ref, pad_ref):
    fill(pad_ref, low_ref, mid_ref, high_ref)
    low, high = reach_of(info_ref, mid_ref.shape[0], group)
    for base in range(0, mid_ref.shape[0], STEP):
        reach = (low[base : base + STEP], high[base : base + STEP])
        out_ref[base : base + STEP, :] = taps_of(pad_ref, depth_ref, reach, base, STEP, taps, False)


STEP = 64


def conv_back_kernel(
    group,
    taps,
    info_ref,
    low_ref,
    mid_ref,
    high_ref,
    grad_low_ref,
    grad_mid_ref,
    grad_high_ref,
    depth_ref,
    out_ref,
    depth_grad_ref,
    pad_ref,
    grad_pad_ref,
    sum_ref,
):
    fill(pad_ref, low_ref, mid_ref, high_ref)
    fill(grad_pad_ref, grad_low_ref, grad_mid_ref, grad_high_ref)
    low, high = reach_of(info_ref, mid_ref.shape[0], group)
    margin = (taps - 1) // 2
    sum_ref[...] = jnp.zeros(sum_ref.shape, jnp.float32)
    for base in range(0, mid_ref.shape[0], STEP):
        reach = (low[base : base + STEP], high[base : base + STEP])
        out_ref[base : base + STEP, :] = taps_of(grad_pad_ref, depth_ref, reach, base, STEP, taps, True)
        grad = grad_pad_ref[EDGE + base : EDGE + base + STEP, :]
        for tap in range(taps):
            shift = tap - margin
            piece = pad_ref[EDGE + base + shift : EDGE + base + shift + STEP, :] * grad
            if shift:
                piece = jnp.where(within(reach, shift), piece, 0.0)
            sum_ref[8 * tap : 8 * tap + 8, :] += jnp.sum(piece.reshape(STEP // 8, 8, LANES), axis=0)
    for tap in range(taps):
        depth_grad_ref[tap : tap + 1, :] = jnp.sum(sum_ref[8 * tap : 8 * tap + 8, :], axis=0, keepdims=True)


def lane_block(rows):
    return pl.BlockSpec((rows, LANES), lambda i: (0, i))


def conv(info, low, mid, high, depth, group):
    rows, width = mid.shape
    taps = depth.shape[0]
    return pl.pallas_call(
        lambda *refs: conv_kernel(group, taps, *refs),
        grid=(width // LANES,),
        in_specs=[pl.BlockSpec(memory_space=pltpu.SMEM)]
        + [lane_block(EDGE), lane_block(rows), lane_block(EDGE), lane_block(taps)],
        out_specs=lane_block(rows),
        out_shape=jax.ShapeDtypeStruct((rows, width), jnp.float32),
        scratch_shapes=[pltpu.VMEM((rows + 2 * EDGE, LANES), jnp.float32)],
        compiler_params=pltpu.CompilerParams(vmem_limit_bytes=VMEM),
        name="conv",
    )(info, low, mid, high, depth)


def conv_back(info, low, mid, high, grad_low, grad_mid, grad_high, depth, group):
    rows, width = mid.shape
    taps = depth.shape[0]
    return pl.pallas_call(
        lambda *refs: conv_back_kernel(group, taps, *refs),
        grid=(width // LANES,),
        in_specs=[pl.BlockSpec(memory_space=pltpu.SMEM)]
        + [lane_block(EDGE), lane_block(rows), lane_block(EDGE)] * 2
        + [lane_block(taps)],
        out_specs=[lane_block(rows), lane_block(taps)],
        out_shape=[
            jax.ShapeDtypeStruct((rows, width), jnp.float32),
            jax.ShapeDtypeStruct((taps, width), jnp.float32),
        ],
        scratch_shapes=[
            pltpu.VMEM((rows + 2 * EDGE, LANES), jnp.float32),
            pltpu.VMEM((rows + 2 * EDGE, LANES), jnp.float32),
            pltpu.VMEM((8 * taps, LANES), jnp.float32),
        ],
        compiler_params=pltpu.CompilerParams(vmem_limit_bytes=VMEM),
        name="conv_back",
    )(info, low, mid, high, grad_low, grad_mid, grad_high, depth)


EPS = 1e-05
CORES = [(0, 1), (1, 0)]


def low(values):
    return values.astype(jnp.bfloat16)


def product(left_in, right_in):
    return jnp.dot(left_in, right_in, preferred_element_type=jnp.float32)


def left_product(left_in, right_in):
    return jnp.einsum("nd,nf->df", left_in, right_in, preferred_element_type=jnp.float32)


def right_product(left_in, right_in):
    return jnp.einsum("nf,df->nd", left_in, right_in, preferred_element_type=jnp.float32)


def swap(values, axis="c"):
    return lax.ppermute(values, axis, CORES)


def ordered(mine, other, place, dim=0):
    first = place == 0
    return jnp.concatenate([jnp.where(first, mine, other), jnp.where(first, other, mine)], axis=dim)


def choose(values, place, dim):
    return lax.dynamic_index_in_dim(values, place, dim, keepdims=False)


def pair_rows(values):
    return ordered(values, swap(values), lax.axis_index("c"))


def pair_sum(partial):
    place = lax.axis_index("c")
    halves = partial.reshape(2, partial.shape[0] // 2, partial.shape[1])
    received = swap(low(choose(halves, 1 - place, 0)))
    return choose(halves, place, 0) + received.astype(jnp.float32)


def gather_axis(values, axis):
    if lax.axis_size(axis) == 2:
        return ordered(values, swap(values, axis), lax.axis_index(axis))
    return lax.all_gather(values, axis, axis=0, tiled=True)


def reduce_axis(values, axis, dim):
    if lax.axis_size(axis) == 2:
        place = lax.axis_index(axis)
        received = swap(choose(values, 1 - place, dim), axis)
        kept = choose(values, place, dim)
        return (kept.astype(jnp.float32) + received.astype(jnp.float32)).astype(values.dtype)
    return lax.psum_scatter(values, axis, scatter_dimension=dim, tiled=False)


def normalize(values):
    average = jnp.mean(values, axis=-1, keepdims=True)
    centred = values - average
    inverse = lax.rsqrt(jnp.mean(centred * centred, axis=-1, keepdims=True) + EPS)
    return (centred * inverse, inverse)


def norm_back(upstream, normed, inverse, gain):
    gain_grad = jnp.sum(upstream * normed, axis=0)
    scaled = upstream * gain
    back = inverse * (
        scaled
        - jnp.mean(scaled, axis=-1, keepdims=True)
        - normed * jnp.mean(scaled * normed, axis=-1, keepdims=True)
    )
    return (back, gain_grad)


def silu_slope(values):
    sigma = jax.nn.sigmoid(values)
    return sigma * (1.0 + values * (1.0 - sigma))


def split_normalize(values):
    width = values.shape[1]
    average = jnp.mean(values, axis=1)
    centred = values - average[:, None]
    spread = jnp.sum(centred * centred, axis=1)
    other = swap(jnp.stack([average, spread]))
    gap = average - other[0]
    whole = spread + other[1] + (0.5 * width) * gap * gap
    inverse = lax.rsqrt(whole / (2 * width) + EPS)
    middle = 0.5 * (average + other[0])
    return ((values - middle[:, None]) * inverse[:, None], inverse[:, None])


def split_norm_back(upstream, normed, inverse, gain):
    gain_grad = jnp.sum(upstream * normed, axis=0)
    scaled = upstream * gain
    sums = jnp.stack([jnp.sum(scaled, axis=1), jnp.sum(scaled * normed, axis=1)])
    means = (sums + swap(sums)) / (2 * scaled.shape[1])
    back = inverse * (scaled - means[0][:, None] - normed * means[1][:, None])
    return (back, gain_grad)


def feed_forward(hidden, gain, inner, outer):
    rows = hidden.shape[0]
    normed, inverse = normalize(hidden)
    entry = low(normed * gain)
    both = jnp.concatenate([entry, swap(entry)], axis=0)
    middle = right_product(both, inner)
    activated = low(jax.nn.silu(middle))
    partial = product(activated, outer)
    received = swap(low(partial[rows:]))
    result = hidden + 0.5 * (partial[:rows] + received.astype(jnp.float32))
    return (result, (normed, inverse, both, middle, activated))


def feed_back(upstream, gain, inner, outer, kept):
    normed, inverse, both, middle, activated = kept
    rows = upstream.shape[0]
    half = low(0.5 * upstream)
    half_both = jnp.concatenate([half, swap(half)], axis=0)
    outer_grad = low(left_product(activated, half_both))
    active_grad = right_product(half_both, outer)
    middle_grad = low(active_grad * silu_slope(middle))
    inner_grad = low(left_product(middle_grad, both))
    partial = product(middle_grad, inner)
    received = swap(low(partial[rows:]))
    entry_grad = partial[:rows] + received.astype(jnp.float32)
    back, gain_grad = norm_back(entry_grad, normed, inverse, gain)
    return (upstream + back, gain_grad, inner_grad, outer_grad)


def bucket_hits(group):
    offset = group - jnp.arange(2 * group, dtype=jnp.int32)
    distance = jnp.abs(offset)
    level = jnp.zeros_like(distance)
    for power in range(1, 14):
        level = level + (distance >= 2**power).astype(jnp.int32)
    plain = jnp.where(distance < 16, distance, jnp.minimum(12 + level, 31))
    bucket = plain + 32 * (offset < 0).astype(jnp.int32)
    return bucket[:, None] == jnp.arange(NB, dtype=jnp.int32)[None, :]


def halos(values):
    count = lax.axis_size("y")
    forward = [(i, i + 1) for i in range(count - 1)]
    backward = [(target, source) for source, target in forward]
    return (
        lax.ppermute(values[-EDGE:], "y", forward),
        lax.ppermute(values[:EDGE], "y", backward),
    )


CHIPS = ("p", "q", "y")


def on_device(
    frames,
    cotangent,
    lengths,
    norm_gains,
    position_bias,
    attend_weight,
    merge_weight,
    glu_weight,
    depth_weight,
    point_weight,
    inner_weight,
    outer_weight,
):
    core = lax.axis_index("c")
    grid = tuple(lax.axis_size(axis) for axis in CHIPS)
    chips = grid[0] * grid[1] * grid[2]
    rows, width = frames.shape
    pair = 2 * rows
    group = pair * grid[2]
    half = width // 2
    share = attend_weight.shape[0]
    units = inner_weight.shape[2]
    taps = depth_weight.shape[0]
    heads = HEADS // 2
    f32 = jnp.float32

    small = jnp.concatenate([norm_gains.reshape(-1), position_bias, depth_weight.reshape(-1)])
    count = small.shape[0]
    small_rows = -(-2 * count // (16 * width)) * 16
    small_both = ordered(small[None], swap(small[None]), core).reshape(-1)
    small_both = jnp.pad(small_both, (0, small_rows * width - 2 * count)).reshape(small_rows, width)

    def own_columns(weight, shape, dim):
        parts = weight.reshape((share,) + shape)
        mine = choose(parts, core, dim).reshape(share, -1)
        other = swap(choose(parts, 1 - core, dim).reshape(share, -1))
        return ordered(mine, other, core)

    attend_part = own_columns(attend_weight, (3, 2, half), 2)
    glu_part = own_columns(glu_weight, (2, chips, 2, share), 3)
    mixed_pack = jnp.concatenate(
        [attend_part.reshape(-1, width), glu_part, merge_weight, point_weight, small_both], axis=0
    )

    def feed_pack(number):
        return jnp.concatenate([inner_weight[number].T, outer_weight[number]], axis=0)

    def feed_gather(number):
        whole = lax.all_gather(feed_pack(number), CHIPS, axis=0)
        return (
            whole[:, :units].reshape(chips * units, width),
            whole[:, units:].reshape(chips * units, width),
        )

    inner_one, outer_one = feed_gather(0)
    mixed = lax.all_gather(mixed_pack, CHIPS, axis=0)
    inner_two, outer_two = feed_gather(1)

    marks = [0]
    for size in (3 * share, 2 * share, share, share, small_rows):
        marks.append(marks[-1] + size)
    attend_full = mixed[:, marks[0] : marks[1]].reshape(width, 3 * half)
    glu_full = mixed[:, marks[1] : marks[2]].reshape(width, width)
    merge_half = mixed[:, marks[2] : marks[3]]
    point_full = mixed[:, marks[3] : marks[4]].reshape(half, width)
    small_full = mixed[:, marks[4] :].reshape(chips, -1)[:, : 2 * count].reshape(chips, 2, count)
    sides = merge_half.reshape(2, chips // 2, share, width)
    merge_full = ordered(
        choose(sides, core, 0)[:, None], swap(choose(sides, 1 - core, 0))[:, None], core, 1
    ).reshape(half, width)

    gain_size = norm_gains.size
    gains = small_full[..., :gain_size].reshape(chips, 2, 6, -1).astype(f32)
    gain_table = gains.transpose(2, 0, 1, 3).reshape(6, width)
    gain_mid = choose(gains[:, :, 3], core, 1).reshape(half)
    bias_table = small_full[..., gain_size : gain_size + position_bias.size].reshape(NB, 2, heads)
    bias_table = choose(bias_table, core, 1)
    depth = choose(small_full[..., gain_size + position_bias.size :], core, 1)
    depth = depth.reshape(chips, taps, share).transpose(1, 0, 2).reshape(taps, half).astype(f32)

    start = lax.axis_index("y") * pair
    info = jnp.stack([lengths[0, 0], lengths[0, 0] + lengths[0, 1], start.astype(jnp.int32)])
    hits = bucket_hits(group)
    bias = jnp.einsum("bh,wb->hw", bias_table, hits.astype(jnp.bfloat16), preferred_element_type=f32)
    bias = bias[:, None, :]

    hidden = frames.astype(f32)
    first, first_kept = feed_forward(hidden, gain_table[0], inner_one, outer_one)
    normed_att, inverse_att = normalize(first)
    att_entry = pair_rows(low(normed_att * gain_table[1]))
    triple = low(product(att_entry, attend_full))
    query = triple[:, :half]
    both = gather_axis(triple[:, half:], "y")
    attended = attend(info, bias, query, both)
    second = first + pair_sum(product(attended, merge_full))
    normed_conv, inverse_conv = normalize(second)
    conv_entry = pair_rows(low(normed_conv * gain_table[2]))
    gate_up = product(conv_entry, glu_full)
    gate_sig = jax.nn.sigmoid(gate_up[:, half:])
    glu_rows = low(gate_up[:, :half] * gate_sig)
    glu_low, glu_high = halos(glu_rows)
    mixed_rows = conv(info, glu_low, glu_rows, glu_high, depth, group)
    normed_mid, inverse_mid = split_normalize(mixed_rows)
    activated = normed_mid * gain_mid
    swish = low(jax.nn.silu(activated))
    third = second + pair_sum(product(swish, point_full))
    fourth, fourth_kept = feed_forward(third, gain_table[4], inner_two, outer_two)
    normed_last, inverse_last = normalize(fourth)
    result = low(normed_last * gain_table[5])

    def by_chip(values):
        return values.reshape(grid + (values.shape[0] // chips, values.shape[1]))

    def lane(values, order):
        names = list(CHIPS)
        for axis in order:
            dim = names.index(axis)
            values = reduce_axis(values, axis, dim)
            names.pop(dim)
        return values

    def last_sum(parts):
        return lax.psum_scatter(jnp.concatenate(parts, axis=1), "p", scatter_dimension=0, tiled=False)

    grad_fourth, gain_five = norm_back(
        cotangent.astype(f32), normed_last, inverse_last, gain_table[5]
    )
    grad_third, gain_four, inner_grad, outer_grad = feed_back(
        grad_fourth, gain_table[4], inner_two, outer_two, fourth_kept
    )
    feed_two = last_sum([lane(by_chip(inner_grad), "yq"), lane(by_chip(outer_grad), "qy")])

    conv_out_grad = pair_rows(low(grad_third))
    point_grad = low(left_product(swish, conv_out_grad))
    swish_grad = right_product(conv_out_grad, point_full)
    act_grad = swish_grad * silu_slope(activated)
    mixed_grad, gain_three = split_norm_back(act_grad, normed_mid, inverse_mid, gain_mid)
    mixed_low = low(mixed_grad)
    grad_low, grad_high = halos(mixed_low)
    glu_back, depth_grad = conv_back(
        info, glu_low, glu_rows, glu_high, grad_low, mixed_low, grad_high, depth, group
    )
    value_part = gate_up[:, :half]
    gate_grad = low(
        jnp.concatenate(
            [glu_back * gate_sig, glu_back * value_part * gate_sig * (1.0 - gate_sig)], axis=1
        )
    )
    glu_grad = low(left_product(conv_entry, gate_grad))
    conv_entry_grad = pair_sum(right_product(gate_grad, glu_full))
    conv_sum = last_sum([lane(by_chip(glu_grad), "qy"), lane(by_chip(point_grad), "yq")])
    back_conv, gain_two = norm_back(conv_entry_grad, normed_conv, inverse_conv, gain_table[2])
    grad_second = grad_third + back_conv

    att_out_grad = pair_rows(low(grad_second))
    merge_grad = low(left_product(attended, att_out_grad)).reshape(chips // 2, 2, share, width)
    merge_grad = ordered(
        choose(merge_grad, core, 1)[None], swap(choose(merge_grad, 1 - core, 1))[None], core
    ).reshape(chips * share, width)
    attended_grad = low(right_product(att_out_grad, merge_full))
    query_grad, key_grad, value_grad, table_sums = attend_back(info, bias, query, both, attended_grad)
    both_grad = jnp.concatenate([key_grad, value_grad], axis=1).reshape(grid[2], pair, width)
    if grid[2] == 2:
        place = lax.axis_index("y")
        received = swap(low(choose(both_grad, 1 - place, 0)), "y")
        both_grad = low(choose(both_grad, place, 0) + received.astype(f32))
    else:
        both_grad = low(lax.psum_scatter(both_grad, "y", scatter_dimension=0, tiled=False))
    triple_grad = jnp.concatenate([query_grad, both_grad], axis=1)
    attend_grad = low(left_product(att_entry, triple_grad))
    att_entry_grad = pair_sum(right_product(triple_grad, attend_full))
    attend_sum = last_sum(
        [
            lane(by_chip(attend_grad).reshape(grid + (3 * share, width)), "yq"),
            lane(by_chip(merge_grad), "qy"),
        ]
    )
    back_att, gain_one = norm_back(att_entry_grad, normed_att, inverse_att, gain_table[1])
    grad_first = grad_second + back_att
    input_grad, gain_zero, inner_grad, outer_grad = feed_back(
        grad_first, gain_table[0], inner_one, outer_one, first_kept
    )

    table_grad = jnp.einsum(
        "hw,wb->bh", table_sums[:, 0], hits.astype(f32), precision=lax.Precision.HIGHEST
    )

    def of_core(values, dim):
        empty = jnp.zeros_like(values)
        return jnp.stack(
            [jnp.where(core == 0, values, empty), jnp.where(core == 1, values, empty)], axis=dim
        )

    gain_three = of_core(gain_three.reshape(chips, share), 1).reshape(width)
    gain_grads = jnp.stack([gain_zero, gain_one, gain_two, gain_three, gain_four, gain_five])
    small_grads = jnp.concatenate(
        [
            gain_grads.reshape(6, chips, 2, share).transpose(1, 2, 0, 3).reshape(chips, 2, -1),
            of_core(table_grad, 1).reshape(chips, 2, -1),
            of_core(depth_grad.reshape(taps, chips, share).transpose(1, 0, 2), 1).reshape(
                chips, 2, -1
            ),
        ],
        axis=2,
    )
    small_sum = choose(small_grads, core, 1) + swap(choose(small_grads, 1 - core, 1))
    small_sum = lane(small_sum.reshape(grid + (count,)), "yq")
    one_rows = -(-count // (16 * width)) * 16
    small_sum = jnp.pad(low(small_sum), ((0, 0), (0, one_rows * width - count)))
    small_sum = small_sum.reshape(grid[0], one_rows, width)

    feed_one = last_sum(
        [lane(by_chip(inner_grad), "yq"), lane(by_chip(outer_grad), "qy"), small_sum]
    )

    def whole_columns(values, shape, dim):
        parts = values.reshape(2, share, -1)
        mine = choose(parts, core, 0)
        other = swap(choose(parts, 1 - core, 0))
        joined = ordered(
            jnp.expand_dims(mine.reshape((share,) + shape), dim),
            jnp.expand_dims(other.reshape((share,) + shape), dim),
            core,
            dim,
        )
        return joined.reshape(share, -1).astype(f32)

    attend_out = whole_columns(attend_sum[: 3 * share].reshape(2 * share, -1), (3, half), 2)
    merge_out = attend_sum[3 * share :].astype(f32)
    glu_out = whole_columns(conv_sum[: 2 * share], (2, chips, share), 3)
    point_out = conv_sum[2 * share :].astype(f32)
    inner_out = jnp.stack([feed_one[:units].T, feed_two[:units].T]).astype(f32)
    outer_out = jnp.stack([feed_one[units : 2 * units], feed_two[units:]]).astype(f32)
    small_out = feed_one[2 * units :].reshape(-1)[:count].astype(f32)
    gains_out = small_out[:gain_size].reshape(norm_gains.shape)
    position_out = small_out[gain_size : gain_size + position_bias.size]
    depth_out = small_out[gain_size + position_bias.size :].reshape(taps, share)
    return (
        result,
        input_grad,
        gains_out,
        position_out,
        attend_out,
        merge_out,
        glu_out,
        depth_out,
        point_out,
        inner_out,
        outer_out,
    )


def solution(mesh):
    across, along = mesh.shape["dp"], mesh.shape["head"]
    fine = Mesh(mesh.devices.reshape(4, across // 4, along // 2, 2), ("p", "q", "y", "c"))
    every = ("p", "q", "y", "c")
    in_specs = (
        P(every, None),
        P(every, None),
        P(("p", "q"), None),
        P(None, every),
        P(every),
        P(every, None),
        P(every, None),
        P(every, None),
        P(None, every),
        P(every, None),
        P(None, None, every),
        P(None, every, None),
    )
    out_specs = (
        P(every, None),
        P(every, None),
        P(None, every),
        P(every),
        P(every, None),
        P(every, None),
        P(every, None),
        P(None, every),
        P(every, None),
        P(None, None, every),
        P(None, every, None),
    )
    return jax.shard_map(
        on_device, mesh=fine, in_specs=in_specs, out_specs=out_specs, check_vma=False
    )
```

```python
import jax
import jax.numpy as jnp
from jax import lax
from jax.experimental import pallas as pl
from jax.experimental.pallas import tpu as pltpu
from jax.sharding import Mesh
from jax.sharding import PartitionSpec as P

HEADS = 16
HD = 64
NB = 64
ROWS = 128
VMEM = 50 * 1024 * 1024


def matmul_in(left, right, dims):
    return lax.dot_general(left, right, (dims, ((), ())), preferred_element_type=jnp.float32)


def spread_bias(info_ref, bias_ref, spread_ref):
    width = spread_ref.shape[1]
    row = jnp.broadcast_to(bias_ref[0], (ROWS, width))
    spread_ref[...] = pltpu.roll(row, 0, 1, stride=1, stride_axis=0)


def half_mask(rows):
    lane = lax.broadcasted_iota(jnp.int32, (rows, 2 * HD), 1)
    start = lax.rem(pl.program_id(0), 2) * HD
    return (lane >= start) & (lane < start + HD)


def segment_at(position, first_end, second_end):
    return (position >= first_end).astype(jnp.int32) + (position >= second_end).astype(jnp.int32)


def weights_of(info_ref, spread_ref, query, keys, number):
    group = keys.shape[0]
    first_end, second_end, start = info_ref[0], info_ref[1], info_ref[2]
    raw = matmul_in(query, keys, ((1,), (1,)))
    shift = pl.multiple_of(group - start - number * ROWS, ROWS)
    bias = spread_ref[:, pl.ds(shift, group)]
    row = start + number * ROWS + lax.broadcasted_iota(jnp.int32, (ROWS, 1), 0)
    column = lax.broadcasted_iota(jnp.int32, (1, group), 1)
    same = segment_at(row, first_end, second_end) == segment_at(column, first_end, second_end)
    scores = jnp.where(same, raw * 0.125 + bias, -1e30)
    raised = jnp.exp(scores - jnp.max(scores, axis=1, keepdims=True))
    return raised * (1.0 / jnp.sum(raised, axis=1, keepdims=True))


def attend_kernel(info_ref, bias_ref, query_ref, key_ref, value_ref, out_ref, spread_ref):
    spread_bias(info_ref, bias_ref, spread_ref)
    mask = half_mask(ROWS)
    first = lax.rem(pl.program_id(0), 2) == 0
    for number in range(query_ref.shape[0] // ROWS):
        rows = pl.ds(number * ROWS, ROWS)
        query = jnp.where(mask, query_ref[rows, :], jnp.bfloat16(0))
        weights = weights_of(info_ref, spread_ref, query, key_ref[...], number)
        out = matmul_in(weights.astype(jnp.bfloat16), value_ref[...], ((1,), (0,)))
        out = out.astype(jnp.bfloat16)
        kept = jnp.where(first, out, out_ref[rows, :])
        out_ref[rows, :] = jnp.where(mask, out, kept)


def attend_back_kernel(
    info_ref,
    bias_ref,
    query_ref,
    key_ref,
    value_ref,
    grad_ref,
    query_grad_ref,
    key_grad_ref,
    value_grad_ref,
    sums_ref,
    spread_ref,
    diag_ref,
    weight_ref,
    score_ref,
    query_mid_ref,
    grad_mid_ref,
):
    spread_bias(info_ref, bias_ref, spread_ref)
    mask = half_mask(ROWS)
    group, width = key_ref.shape[0], spread_ref.shape[1]
    first = lax.rem(pl.program_id(0), 2) == 0
    diag_ref[...] = jnp.zeros(diag_ref.shape, jnp.float32)
    for number in range(query_ref.shape[0] // ROWS):
        rows = pl.ds(number * ROWS, ROWS)
        query = jnp.where(mask, query_ref[rows, :], jnp.bfloat16(0))
        grad = jnp.where(mask, grad_ref[rows, :], jnp.bfloat16(0))
        query_mid_ref[rows, :] = query
        grad_mid_ref[rows, :] = grad
        weights = weights_of(info_ref, spread_ref, query, key_ref[...], number)
        weight_ref[rows, :] = weights.astype(jnp.bfloat16)
        weight_grad = matmul_in(grad, value_ref[...], ((1,), (1,)))
        inner = jnp.sum(weights * weight_grad, axis=1, keepdims=True)
        score_grad = weights * (weight_grad - inner)
        shift = pl.multiple_of(group - info_ref[2] - number * ROWS, ROWS)
        diag_ref[:, pl.ds(shift, group)] += score_grad
        raw_grad = (score_grad * 0.125).astype(jnp.bfloat16)
        score_ref[rows, :] = raw_grad
        out = matmul_in(raw_grad, key_ref[...], ((1,), (0,))).astype(jnp.bfloat16)
        kept = jnp.where(first, out, query_grad_ref[rows, :])
        query_grad_ref[rows, :] = jnp.where(mask, out, kept)
    key_grad = matmul_in(score_ref[...], query_mid_ref[...], ((0,), (0,)))
    value_grad = matmul_in(weight_ref[...], grad_mid_ref[...], ((0,), (0,)))

    @pl.when(first)
    def _():
        key_grad_ref[...] = key_grad
        value_grad_ref[...] = value_grad

    @pl.when(jnp.logical_not(first))
    def _():
        key_grad_ref[...] += key_grad
        value_grad_ref[...] += value_grad

    total = diag_ref[...]
    size = ROWS // 2
    while size >= 8:
        total = total[:size] + pltpu.roll(total[size:], width - size, 1)
        size //= 2
    for size in (4, 2, 1):
        total = total + pltpu.roll(pltpu.roll(total, 8 - size, 0), width - size, 1)
    sums_ref[0] = total[0:1]


def attend_specs(rows, group, width, pairs):
    return [
        pl.BlockSpec(memory_space=pltpu.SMEM),
        pl.BlockSpec((1, 1, width), lambda h: (h, 0, 0)),
        pl.BlockSpec((rows, 2 * HD), lambda h: (0, h // 2)),
        pl.BlockSpec((group, 2 * HD), lambda h: (0, h // 2)),
        pl.BlockSpec((group, 2 * HD), lambda h: (0, pairs + h // 2)),
    ]


def attend(info, bias, query, both):
    heads, _, width = bias.shape
    rows, group = query.shape[0], both.shape[0]
    pairs = heads // 2
    return pl.pallas_call(
        attend_kernel,
        grid=(heads,),
        in_specs=attend_specs(rows, group, width, pairs),
        out_specs=pl.BlockSpec((rows, 2 * HD), lambda h: (0, h // 2)),
        out_shape=jax.ShapeDtypeStruct((rows, heads * HD), jnp.bfloat16),
        scratch_shapes=[pltpu.VMEM((ROWS, width), jnp.float32)],
        compiler_params=pltpu.CompilerParams(vmem_limit_bytes=VMEM),
        name="attend",
    )(info, bias, query, both, both)


def attend_back(info, bias, query, both, grad):
    heads, _, width = bias.shape
    rows, group = query.shape[0], both.shape[0]
    pairs = heads // 2
    pair_block = pl.BlockSpec((rows, 2 * HD), lambda h: (0, h // 2))
    group_block = pl.BlockSpec((group, 2 * HD), lambda h: (0, h // 2))
    return pl.pallas_call(
        attend_back_kernel,
        grid=(heads,),
        in_specs=attend_specs(rows, group, width, pairs) + [pair_block],
        out_specs=[pair_block, group_block, group_block, pl.BlockSpec((1, 1, width), lambda h: (h, 0, 0))],
        out_shape=[
            jax.ShapeDtypeStruct((rows, heads * HD), jnp.bfloat16),
            jax.ShapeDtypeStruct((group, heads * HD), jnp.float32),
            jax.ShapeDtypeStruct((group, heads * HD), jnp.float32),
            jax.ShapeDtypeStruct((heads, 1, width), jnp.float32),
        ],
        scratch_shapes=[
            pltpu.VMEM((ROWS, width), jnp.float32),
            pltpu.VMEM((ROWS, width), jnp.float32),
            pltpu.VMEM((rows, group), jnp.bfloat16),
            pltpu.VMEM((rows, group), jnp.bfloat16),
            pltpu.VMEM((rows, 2 * HD), jnp.bfloat16),
            pltpu.VMEM((rows, 2 * HD), jnp.bfloat16),
        ],
        compiler_params=pltpu.CompilerParams(vmem_limit_bytes=VMEM),
        name="attend_back",
    )(info, bias, query, both, both, grad)


LANES = 128
EDGE = 16


def reach_of(info_ref, rows, group):
    position = info_ref[2] + lax.broadcasted_iota(jnp.int32, (rows, LANES), 0)
    first_end, second_end = info_ref[0], info_ref[1]
    low = jnp.where(position >= second_end, second_end, jnp.where(position >= first_end, first_end, 0))
    high = jnp.where(position < first_end, first_end, jnp.where(position < second_end, second_end, group))
    return (low - position, high - position)


def within(reach, shift):
    if shift < 0:
        return reach[0] <= shift
    return reach[1] > shift


def fill(pad_ref, low_ref, mid_ref, high_ref):
    rows = mid_ref.shape[0]
    pad_ref[0:EDGE, :] = low_ref[...].astype(jnp.float32)
    pad_ref[EDGE : EDGE + rows, :] = mid_ref[...].astype(jnp.float32)
    pad_ref[EDGE + rows :, :] = high_ref[...].astype(jnp.float32)


def taps_of(pad_ref, depth_ref, reach, base, rows, taps, mirror):
    margin = (taps - 1) // 2
    total = jnp.zeros((rows, LANES), jnp.float32)
    for tap in range(taps):
        shift = margin - tap if mirror else tap - margin
        piece = pad_ref[EDGE + base + shift : EDGE + base + shift + rows, :] * depth_ref[tap : tap + 1, :]
        if shift:
            piece = jnp.where(within(reach, shift), piece, 0.0)
        total = total + piece
    return total


def conv_kernel(group, taps, info_ref, low_ref, mid_ref, high_ref, depth_ref, out_ref, pad_ref):
    fill(pad_ref, low_ref, mid_ref, high_ref)
    low, high = reach_of(info_ref, mid_ref.shape[0], group)
    for base in range(0, mid_ref.shape[0], STEP):
        reach = (low[base : base + STEP], high[base : base + STEP])
        out_ref[base : base + STEP, :] = taps_of(pad_ref, depth_ref, reach, base, STEP, taps, False)


STEP = 64


def conv_back_kernel(
    group,
    taps,
    info_ref,
    low_ref,
    mid_ref,
    high_ref,
    grad_low_ref,
    grad_mid_ref,
    grad_high_ref,
    depth_ref,
    out_ref,
    depth_grad_ref,
    pad_ref,
    grad_pad_ref,
    sum_ref,
):
    fill(pad_ref, low_ref, mid_ref, high_ref)
    fill(grad_pad_ref, grad_low_ref, grad_mid_ref, grad_high_ref)
    low, high = reach_of(info_ref, mid_ref.shape[0], group)
    margin = (taps - 1) // 2
    sum_ref[...] = jnp.zeros(sum_ref.shape, jnp.float32)
    for base in range(0, mid_ref.shape[0], STEP):
        reach = (low[base : base + STEP], high[base : base + STEP])
        out_ref[base : base + STEP, :] = taps_of(grad_pad_ref, depth_ref, reach, base, STEP, taps, True)
        grad = grad_pad_ref[EDGE + base : EDGE + base + STEP, :]
        for tap in range(taps):
            shift = tap - margin
            piece = pad_ref[EDGE + base + shift : EDGE + base + shift + STEP, :] * grad
            if shift:
                piece = jnp.where(within(reach, shift), piece, 0.0)
            sum_ref[8 * tap : 8 * tap + 8, :] += jnp.sum(piece.reshape(STEP // 8, 8, LANES), axis=0)
    for tap in range(taps):
        depth_grad_ref[tap : tap + 1, :] = jnp.sum(sum_ref[8 * tap : 8 * tap + 8, :], axis=0, keepdims=True)


def lane_block(rows):
    return pl.BlockSpec((rows, LANES), lambda i: (0, i))


def conv(info, low, mid, high, depth, group):
    rows, width = mid.shape
    taps = depth.shape[0]
    return pl.pallas_call(
        lambda *refs: conv_kernel(group, taps, *refs),
        grid=(width // LANES,),
        in_specs=[pl.BlockSpec(memory_space=pltpu.SMEM)]
        + [lane_block(EDGE), lane_block(rows), lane_block(EDGE), lane_block(taps)],
        out_specs=lane_block(rows),
        out_shape=jax.ShapeDtypeStruct((rows, width), jnp.float32),
        scratch_shapes=[pltpu.VMEM((rows + 2 * EDGE, LANES), jnp.float32)],
        compiler_params=pltpu.CompilerParams(vmem_limit_bytes=VMEM),
        name="conv",
    )(info, low, mid, high, depth)


def conv_back(info, low, mid, high, grad_low, grad_mid, grad_high, depth, group):
    rows, width = mid.shape
    taps = depth.shape[0]
    return pl.pallas_call(
        lambda *refs: conv_back_kernel(group, taps, *refs),
        grid=(width // LANES,),
        in_specs=[pl.BlockSpec(memory_space=pltpu.SMEM)]
        + [lane_block(EDGE), lane_block(rows), lane_block(EDGE)] * 2
        + [lane_block(taps)],
        out_specs=[lane_block(rows), lane_block(taps)],
        out_shape=[
            jax.ShapeDtypeStruct((rows, width), jnp.float32),
            jax.ShapeDtypeStruct((taps, width), jnp.float32),
        ],
        scratch_shapes=[
            pltpu.VMEM((rows + 2 * EDGE, LANES), jnp.float32),
            pltpu.VMEM((rows + 2 * EDGE, LANES), jnp.float32),
            pltpu.VMEM((8 * taps, LANES), jnp.float32),
        ],
        compiler_params=pltpu.CompilerParams(vmem_limit_bytes=VMEM),
        name="conv_back",
    )(info, low, mid, high, grad_low, grad_mid, grad_high, depth)


EPS = 1e-05
CORES = [(0, 1), (1, 0)]


def low(values):
    return values.astype(jnp.bfloat16)


def product(left_in, right_in):
    return jnp.dot(left_in, right_in, preferred_element_type=jnp.float32)


def left_product(left_in, right_in):
    return jnp.einsum("nd,nf->df", left_in, right_in, preferred_element_type=jnp.float32)


def right_product(left_in, right_in):
    return jnp.einsum("nf,df->nd", left_in, right_in, preferred_element_type=jnp.float32)


def swap(values, axis="c"):
    return lax.ppermute(values, axis, CORES)


def ordered(mine, other, place, dim=0):
    first = place == 0
    return jnp.concatenate([jnp.where(first, mine, other), jnp.where(first, other, mine)], axis=dim)


def choose(values, place, dim):
    return lax.dynamic_index_in_dim(values, place, dim, keepdims=False)


def pair_rows(values):
    return ordered(values, swap(values), lax.axis_index("c"))


def pair_sum(partial):
    place = lax.axis_index("c")
    halves = partial.reshape(2, partial.shape[0] // 2, partial.shape[1])
    received = swap(low(choose(halves, 1 - place, 0)))
    return choose(halves, place, 0) + received.astype(jnp.float32)


def gather_axis(values, axis):
    if lax.axis_size(axis) == 2:
        return ordered(values, swap(values, axis), lax.axis_index(axis))
    return lax.all_gather(values, axis, axis=0, tiled=True)


def pick(values, axis, dim):
    return choose(values, 1 - lax.axis_index(axis), dim)


def send(values, axis, dim, *ties):
    if lax.axis_size(axis) == 2:
        return swap(after(pick(values, axis, dim), *ties), axis)
    return lax.psum_scatter(values, axis, scatter_dimension=dim, tiled=False)


def add(values, received, axis, dim):
    if lax.axis_size(axis) != 2:
        return received
    kept = choose(values, lax.axis_index(axis), dim)
    return (kept.astype(jnp.float32) + received.astype(jnp.float32)).astype(values.dtype)


def after(values, *tokens):
    if not tokens:
        return values
    return lax.optimization_barrier((values,) + tokens)[0]


def together(*values):
    return lax.optimization_barrier(values)


def placed(parts):
    own, across, both, along = parts
    q, y = lax.axis_index("q"), lax.axis_index("y")
    result = jnp.zeros((own.shape[0], 2, 2) + own.shape[1:], own.dtype)
    for part, at_q, at_y in ((own, q, y), (across, 1 - q, y), (both, 1 - q, 1 - y), (along, q, 1 - y)):
        at = (0, at_q, at_y) + (0,) * (own.ndim - 1)
        result = lax.dynamic_update_slice(result, part[:, None, None], at)
    return result


def normalize(values):
    average = jnp.mean(values, axis=-1, keepdims=True)
    centred = values - average
    inverse = lax.rsqrt(jnp.mean(centred * centred, axis=-1, keepdims=True) + EPS)
    return (centred * inverse, inverse)


def norm_back(upstream, normed, inverse, gain):
    gain_grad = jnp.sum(upstream * normed, axis=0)
    scaled = upstream * gain
    back = inverse * (
        scaled
        - jnp.mean(scaled, axis=-1, keepdims=True)
        - normed * jnp.mean(scaled * normed, axis=-1, keepdims=True)
    )
    return (back, gain_grad)


def silu_slope(values):
    sigma = jax.nn.sigmoid(values)
    return sigma * (1.0 + values * (1.0 - sigma))


def split_normalize(values):
    width = values.shape[1]
    average = jnp.mean(values, axis=1)
    centred = values - average[:, None]
    spread = jnp.sum(centred * centred, axis=1)
    other = swap(jnp.stack([average, spread]))
    gap = average - other[0]
    whole = spread + other[1] + (0.5 * width) * gap * gap
    inverse = lax.rsqrt(whole / (2 * width) + EPS)
    middle = 0.5 * (average + other[0])
    return ((values - middle[:, None]) * inverse[:, None], inverse[:, None])


def split_norm_back(upstream, normed, inverse, gain):
    gain_grad = jnp.sum(upstream * normed, axis=0)
    scaled = upstream * gain
    sums = jnp.stack([jnp.sum(scaled, axis=1), jnp.sum(scaled * normed, axis=1)])
    means = (sums + swap(sums)) / (2 * scaled.shape[1])
    back = inverse * (scaled - means[0][:, None] - normed * means[1][:, None])
    return (back, gain_grad)


def feed_forward(hidden, gain, inner, outer):
    rows = hidden.shape[0]
    normed, inverse = normalize(hidden)
    entry = low(normed * gain)
    both = jnp.concatenate([entry, swap(entry)], axis=0)
    middle = right_product(both, inner)
    activated = low(jax.nn.silu(middle))
    partial = product(activated, outer)
    received = swap(low(partial[rows:]))
    result = hidden + 0.5 * (partial[:rows] + received.astype(jnp.float32))
    return (result, (normed, inverse, both, middle, activated))


def feed_back(upstream, gain, inner, outer, kept):
    normed, inverse, both, middle, activated = kept
    rows = upstream.shape[0]
    half = low(0.5 * upstream)
    half_both = jnp.concatenate([half, swap(half)], axis=0)
    active_grad = right_product(half_both, outer)
    middle_grad = low(active_grad * silu_slope(middle))
    partial = product(middle_grad, inner)
    received = swap(low(partial[rows:]))
    entry_grad = partial[:rows] + received.astype(jnp.float32)
    back, gain_grad = norm_back(entry_grad, normed, inverse, gain)

    def inner_grad(low_row, high_row):
        return left_product(middle_grad[:, low_row:high_row], both)

    def outer_grad(low_row, high_row):
        return left_product(activated[:, low_row:high_row], half_both)

    return (upstream + back, gain_grad, inner_grad, outer_grad)


def bucket_hits(group):
    offset = group - jnp.arange(2 * group, dtype=jnp.int32)
    distance = jnp.abs(offset)
    level = jnp.zeros_like(distance)
    for power in range(1, 14):
        level = level + (distance >= 2**power).astype(jnp.int32)
    plain = jnp.where(distance < 16, distance, jnp.minimum(12 + level, 31))
    bucket = plain + 32 * (offset < 0).astype(jnp.int32)
    return bucket[:, None] == jnp.arange(NB, dtype=jnp.int32)[None, :]


def halos(values):
    count = lax.axis_size("y")
    forward = [(i, i + 1) for i in range(count - 1)]
    backward = [(target, source) for source, target in forward]
    return (
        lax.ppermute(values[-EDGE:], "y", forward),
        lax.ppermute(values[:EDGE], "y", backward),
    )


CHIPS = ("p", "q", "y")


def on_device(
    frames,
    cotangent,
    lengths,
    norm_gains,
    position_bias,
    attend_weight,
    merge_weight,
    glu_weight,
    depth_weight,
    point_weight,
    inner_weight,
    outer_weight,
):
    core = lax.axis_index("c")
    grid = tuple(lax.axis_size(axis) for axis in CHIPS)
    chips = grid[0] * grid[1] * grid[2]
    rows, width = frames.shape
    pair = 2 * rows
    group = pair * grid[2]
    half = width // 2
    share = attend_weight.shape[0]
    units = inner_weight.shape[2]
    taps = depth_weight.shape[0]
    heads = HEADS // 2
    f32 = jnp.float32

    small = jnp.concatenate([norm_gains.reshape(-1), position_bias, depth_weight.reshape(-1)])
    count = small.shape[0]
    small_rows = -(-2 * count // (16 * width)) * 16
    small_both = ordered(small[None], swap(small[None]), core).reshape(-1)
    small_both = jnp.pad(small_both, (0, small_rows * width - 2 * count)).reshape(small_rows, width)

    def feed_pack(number, *more):
        return jnp.concatenate([inner_weight[number].T, outer_weight[number], *more], axis=0)

    pack_one = feed_pack(0, small_both)
    pack_two = feed_pack(1)
    attend_weight, glu_weight = together(attend_weight, glu_weight, pack_one)[:2]

    def own_columns(weight, shape, dim):
        parts = weight.reshape((share,) + shape)
        mine = choose(parts, core, dim).reshape(share, -1)
        other = swap(choose(parts, 1 - core, dim).reshape(share, -1))
        return ordered(mine, other, core)

    attend_part = own_columns(attend_weight, (3, 2, half), 2)
    glu_part = own_columns(glu_weight, (2, chips, 2, share), 3)
    mixed_pack = jnp.concatenate(
        [attend_part.reshape(-1, width), glu_part, merge_weight, point_weight], axis=0
    )

    square = grid[1] == 2 and grid[2] == 2
    marks = [0]
    for size in (3 * share, 2 * share, share, share):
        marks.append(marks[-1] + size)

    def gather_p(values):
        return lax.all_gather(values, "p", axis=0)

    if square:
        whole_one = gather_p(pack_one)
        two_x, two_y = together(swap(pack_two, "q"), swap(pack_two, "y"))
        pack_two = jnp.stack([pack_two, two_x, swap(two_x, "y"), two_y])
        mixed = gather_p(after(mixed_pack, pack_one))
        inner = whole_one[:, :units].reshape(-1, width)
        outer = whole_one[:, units : 2 * units].reshape(-1, width)
        tiny = whole_one[:, 2 * units :]
        inner, outer, tiny, pack_two = together(inner, outer, tiny, pack_two)
        whole_two = gather_p(after(pack_two, mixed)).reshape(chips, 2 * units, width)
        tiny_x = swap(tiny, "q")
        inner_x, inner_y, outer_x, outer_y, tiny_x = together(
            swap(inner, "q"), swap(inner, "y"), swap(outer, "q"), swap(outer, "y"), tiny_x
        )
        inner_xy, outer_xy = swap(inner_x, "y"), swap(outer_y, "q")
        small_full = placed((tiny, tiny_x, swap(tiny_x, "y"), swap(tiny, "y")))
        small_full = small_full.reshape(chips, -1)
        inner_xy, outer_xy, mixed = together(inner_xy, outer_xy, mixed)
        inner_one = jnp.concatenate([inner, inner_x, inner_xy, inner_y], axis=0)
        outer_one = jnp.concatenate([outer, outer_x, outer_xy, outer_y], axis=0)
        attend_part = mixed[:, : marks[1]].reshape(grid[0], 2 * share, 3 * half)
        rest_part = mixed[:, marks[1] :]
        attend_part, rest_part = together(attend_part, rest_part)
        attend_x, attend_y = swap(attend_part, "q"), swap(attend_part, "y")
    else:
        whole_one = lax.all_gather(pack_one, CHIPS, axis=0)
        mixed = lax.all_gather(mixed_pack, CHIPS, axis=0)
        whole_two = lax.all_gather(pack_two, CHIPS, axis=0)
        inner_one = whole_one[:, :units].reshape(chips * units, width)
        outer_one = whole_one[:, units : 2 * units].reshape(chips * units, width)
        small_full = whole_one[:, 2 * units :].reshape(chips, -1)

    small_full = small_full[:, : 2 * count].reshape(chips, 2, count)
    gain_size = norm_gains.size
    gains = small_full[..., :gain_size].reshape(chips, 2, 6, -1).astype(f32)
    gain_table = gains.transpose(2, 0, 1, 3).reshape(6, width)
    gain_mid = choose(gains[:, :, 3], core, 1).reshape(half)
    bias_table = small_full[..., gain_size : gain_size + position_bias.size].reshape(NB, 2, heads)
    bias_table = choose(bias_table, core, 1)
    depth = choose(small_full[..., gain_size + position_bias.size :], core, 1)
    depth = depth.reshape(chips, taps, share).transpose(1, 0, 2).reshape(taps, half).astype(f32)

    start = lax.axis_index("y") * pair
    info = jnp.stack([lengths[0, 0], lengths[0, 0] + lengths[0, 1], start.astype(jnp.int32)])
    hits = bucket_hits(group)
    bias = jnp.einsum("bh,wb->hw", bias_table, hits.astype(jnp.bfloat16), preferred_element_type=f32)
    bias = bias[:, None, :]

    hidden = frames.astype(f32)
    first, first_kept = feed_forward(hidden, gain_table[0], inner_one, outer_one)
    if square:
        first, attend_x, attend_y = together(first, attend_x, attend_y)
        rest_y = swap(rest_part, "y")
        attend_full = placed((attend_part, attend_x, swap(attend_y, "q"), attend_y))
    else:
        attend_full = mixed[:, : marks[1]]
    attend_full = attend_full.reshape(width, 3 * half)
    normed_att, inverse_att = normalize(first)
    att_entry = pair_rows(low(normed_att * gain_table[1]))
    triple = low(product(att_entry, attend_full))
    query = triple[:, :half]
    key_value = triple[:, half:]
    if square:
        key_value, rest_part = together(key_value, rest_part)
        rest_x = swap(rest_part, "q")
    both = gather_axis(key_value, "y")
    if square:
        query, both, rest_x, rest_y = together(query, both, rest_x, rest_y)
        rest_xy = swap(rest_x, "y")
    attended = attend(info, bias, query, both)
    if square:
        attended, rest_xy = together(attended, rest_xy)
        rest = placed((rest_part, rest_x, rest_xy, rest_y)).reshape(chips, -1, width)
    else:
        rest = mixed[:, marks[1] :]
    marks = [mark - marks[1] for mark in marks]
    glu_full = rest[:, : marks[2]].reshape(width, width)
    merge_half = rest[:, marks[2] : marks[3]]
    point_full = rest[:, marks[3] : marks[4]].reshape(half, width)
    sides = merge_half.reshape(2, chips // 2, share, width)
    merge_full = ordered(
        choose(sides, core, 0)[:, None], swap(choose(sides, 1 - core, 0))[:, None], core, 1
    ).reshape(half, width)
    second = first + pair_sum(product(attended, merge_full))
    normed_conv, inverse_conv = normalize(second)
    conv_entry = pair_rows(low(normed_conv * gain_table[2]))
    gate_up = product(conv_entry, glu_full)
    gate_sig = jax.nn.sigmoid(gate_up[:, half:])
    glu_rows = low(gate_up[:, :half] * gate_sig)
    glu_low, glu_high = halos(glu_rows)
    mixed_rows = conv(info, glu_low, glu_rows, glu_high, depth, group)
    normed_mid, inverse_mid = split_normalize(mixed_rows)
    activated = normed_mid * gain_mid
    swish = low(jax.nn.silu(activated))
    third = second + pair_sum(product(swish, point_full))
    inner_two = whole_two[:, :units].reshape(chips * units, width)
    outer_two = whole_two[:, units:].reshape(chips * units, width)
    fourth, fourth_kept = feed_forward(third, gain_table[4], inner_two, outer_two)
    normed_last, inverse_last = normalize(fourth)
    result = low(normed_last * gain_table[5])

    def by_chip(values):
        return values.reshape(grid + (values.shape[0] // chips, values.shape[1]))

    def last_sum(values):
        return lax.psum_scatter(values, "p", scatter_dimension=0, tiled=False)

    size = grid[0] * units

    def early_sum(grad):
        values = low(grad(0, chips * units))
        if square:
            return last_sum(values.reshape(grid[0], 4, units, width))
        return last_sum(values.reshape(grid + (units, width)))

    grad_fourth, gain_five = norm_back(
        cotangent.astype(f32), normed_last, inverse_last, gain_table[5]
    )
    grad_third, gain_four, inner_two_grad, outer_two_grad = feed_back(
        grad_fourth, gain_table[4], inner_two, outer_two, fourth_kept
    )

    outer_two_sum = early_sum(outer_two_grad)
    inner_two_sum = early_sum(inner_two_grad)

    conv_out_grad = pair_rows(low(grad_third))
    swish_grad = right_product(conv_out_grad, point_full)
    act_grad = swish_grad * silu_slope(activated)
    mixed_grad, gain_three = split_norm_back(act_grad, normed_mid, inverse_mid, gain_mid)
    mixed_low = low(mixed_grad)
    grad_low, grad_high = halos(mixed_low)
    glu_back, depth_grad = conv_back(
        info, glu_low, glu_rows, glu_high, grad_low, mixed_low, grad_high, depth, group
    )
    value_part = gate_up[:, :half]
    gate_grad = low(
        jnp.concatenate(
            [glu_back * gate_sig, glu_back * value_part * gate_sig * (1.0 - gate_sig)], axis=1
        )
    )
    conv_entry_grad = pair_sum(right_product(gate_grad, glu_full))
    point_grad = by_chip(low(left_product(swish, conv_out_grad)))
    glu_grad = by_chip(low(left_product(conv_entry, gate_grad)))
    back_conv, gain_two = norm_back(conv_entry_grad, normed_conv, inverse_conv, gain_table[2])
    grad_second = grad_third + back_conv

    att_out_grad = pair_rows(low(grad_second))
    glu_a = send(glu_grad, "q", 1)
    point_a = send(point_grad, "y", 2)
    merge_grad = low(left_product(attended, att_out_grad)).reshape(chips // 2, 2, share, width)
    merge_grad = ordered(
        choose(merge_grad, core, 1)[None], swap(choose(merge_grad, 1 - core, 1))[None], core
    )
    merge_grad = by_chip(merge_grad.reshape(chips * share, width))
    attended_grad = low(right_product(att_out_grad, merge_full))
    query_grad, key_grad, value_grad, table_sums = attend_back(info, bias, query, both, attended_grad)
    query_grad, key_grad, value_grad, glu_a, point_a = together(
        query_grad, key_grad, value_grad, glu_a, point_a
    )
    both_grad = jnp.concatenate([key_grad, value_grad], axis=1).reshape(grid[2], pair, width)
    if grid[2] == 2:
        place = lax.axis_index("y")
        both_received = swap(low(choose(both_grad, 1 - place, 0)), "y")
        both_grad = low(choose(both_grad, place, 0) + both_received.astype(f32))
    else:
        both_received = low(lax.psum_scatter(both_grad, "y", scatter_dimension=0, tiled=False))
        both_grad = both_received
    triple_grad = jnp.concatenate([query_grad, both_grad], axis=1)
    attend_grad = low(left_product(att_entry, triple_grad))
    attend_grad = attend_grad.reshape(grid + (2 * share, 3 * half))
    att_entry_grad = pair_sum(right_product(triple_grad, attend_full))
    back_att, gain_one = norm_back(att_entry_grad, normed_att, inverse_att, gain_table[1])
    grad_first = grad_second + back_att
    glu_half = add(glu_grad, glu_a, "q", 1)
    point_half = add(point_grad, point_a, "y", 2)
    glu_b = send(glu_half, "y", 1, both_received)
    point_b = send(point_half, "q", 1, both_received)
    merge_a = send(merge_grad, "y", 2, both_received)
    attend_a = send(attend_grad, "q", 1)
    if square:
        grad_first, glu_b, point_b, merge_a = together(grad_first, glu_b, point_b, merge_a)
    input_grad, gain_zero, inner_one_grad, outer_one_grad = feed_back(
        grad_first, gain_table[0], inner_one, outer_one, first_kept
    )
    conv_sum = jnp.concatenate([add(glu_half, glu_b, "y", 1), add(point_half, point_b, "q", 1)], axis=1)
    merge_half = add(merge_grad, merge_a, "y", 2)
    merge_b = send(merge_half, "q", 1)
    if square:
        outer_one_a = swap(low(outer_one_grad(2 * size, 4 * size)), "y")
        inner_one_a = swap(low(inner_one_grad(size, 3 * size)), "q")
        two_sum = jnp.concatenate([inner_two_sum, outer_two_sum], axis=1)
        two_sum, input_grad = together(two_sum, input_grad)
        two_a = swap(two_sum[2:], "y")
        outer_one_a, inner_one_a, two_a, attend_a, merge_b = together(
            outer_one_a, inner_one_a, two_a, attend_a, merge_b
        )
    attend_half = add(attend_grad, attend_a, "q", 1)
    if square:
        last = together(
            low(outer_one_grad(size, 2 * size) + outer_one_a[:size].astype(f32)),
            low(inner_one_grad(3 * size, 4 * size) + inner_one_a[size:].astype(f32)),
            pick(attend_half, "y", 1),
            low(two_sum[1].astype(f32) + two_a[0].astype(f32)),
        )
        outer_one_b, inner_one_b, attend_b, two_b = [
            swap(part, axis) for part, axis in zip(last, "qyyq")
        ]
        two_sum = low(two_sum[0].astype(f32) + two_a[1].astype(f32) + two_b.astype(f32))
        inner_sum_two, outer_sum_two = two_sum[:units], two_sum[units:]
        outer_sum_one = outer_one_grad(0, size) + outer_one_a[size:].astype(f32)
        inner_sum_one = inner_one_grad(0, size) + inner_one_a[:size].astype(f32)
        outer_sum_one = low(outer_sum_one + outer_one_b.astype(f32)).reshape(grid[0], units, width)
        inner_sum_one = low(inner_sum_one + inner_one_b.astype(f32)).reshape(grid[0], units, width)
    else:
        attend_b = send(attend_half, "y", 1)
        inner_sum_one = by_chip(low(inner_one_grad(0, chips * units)))
        outer_sum_one = by_chip(low(outer_one_grad(0, chips * units)))
        inner_sum_one = send(send(inner_sum_one, "y", 2), "q", 1)
        outer_sum_one = send(send(outer_sum_one, "y", 2), "q", 1)
        inner_sum_two = send(send(inner_two_sum, "y", 1), "q", 0)
        outer_sum_two = send(send(outer_two_sum, "y", 1), "q", 0)
    attend_sum = add(attend_half, attend_b, "y", 1).reshape(grid[0], 3 * share, width)
    mixed_sum = last_sum(
        jnp.concatenate([attend_sum, conv_sum, add(merge_half, merge_b, "q", 1)], axis=1)
    )

    table_grad = jnp.einsum(
        "hw,wb->bh", table_sums[:, 0], hits.astype(f32), precision=lax.Precision.HIGHEST
    )

    def of_core(values, dim):
        empty = jnp.zeros_like(values)
        return jnp.stack(
            [jnp.where(core == 0, values, empty), jnp.where(core == 1, values, empty)], axis=dim
        )

    gain_three = of_core(gain_three.reshape(chips, share), 1).reshape(width)
    gain_grads = jnp.stack([gain_zero, gain_one, gain_two, gain_three, gain_four, gain_five])
    small_grads = jnp.concatenate(
        [
            gain_grads.reshape(6, chips, 2, share).transpose(1, 2, 0, 3).reshape(chips, 2, -1),
            of_core(table_grad, 1).reshape(chips, 2, -1),
            of_core(depth_grad.reshape(taps, chips, share).transpose(1, 0, 2), 1).reshape(
                chips, 2, -1
            ),
        ],
        axis=2,
    )
    small_sum = choose(small_grads, core, 1) + swap(choose(small_grads, 1 - core, 1))
    small_sum = small_sum.reshape(grid + (count,))
    small_sum = add(small_sum, send(small_sum, "y", 2), "y", 2)
    small_sum = add(small_sum, send(small_sum, "q", 1), "q", 1)
    one_rows = -(-count // (16 * width)) * 16
    small_sum = jnp.pad(low(small_sum), ((0, 0), (0, one_rows * width - count)))
    small_sum = small_sum.reshape(grid[0], one_rows, width)

    one_sum = last_sum(jnp.concatenate([inner_sum_one, outer_sum_one, small_sum], axis=1))

    def whole_columns(values, shape, dim):
        parts = values.reshape(2, share, -1)
        mine = choose(parts, core, 0)
        other = swap(choose(parts, 1 - core, 0))
        joined = ordered(
            jnp.expand_dims(mine.reshape((share,) + shape), dim),
            jnp.expand_dims(other.reshape((share,) + shape), dim),
            core,
            dim,
        )
        return joined.reshape(share, -1).astype(f32)

    attend_out = whole_columns(mixed_sum[: 3 * share].reshape(2 * share, -1), (3, half), 2)
    glu_out = whole_columns(mixed_sum[3 * share : 5 * share], (2, chips, share), 3)
    point_out = mixed_sum[5 * share : 6 * share].astype(f32)
    merge_out = mixed_sum[6 * share :].astype(f32)
    inner_out = jnp.stack([one_sum[:units].T, inner_sum_two.T]).astype(f32)
    outer_out = jnp.stack([one_sum[units : 2 * units], outer_sum_two]).astype(f32)
    small_out = one_sum[2 * units :].reshape(-1)[:count].astype(f32)
    gains_out = small_out[:gain_size].reshape(norm_gains.shape)
    position_out = small_out[gain_size : gain_size + position_bias.size]
    depth_out = small_out[gain_size + position_bias.size :].reshape(taps, share)
    return (
        result,
        input_grad,
        gains_out,
        position_out,
        attend_out,
        merge_out,
        glu_out,
        depth_out,
        point_out,
        inner_out,
        outer_out,
    )


def solution(mesh):
    across, along = mesh.shape["dp"], mesh.shape["head"]
    fine = Mesh(mesh.devices.reshape(4, across // 4, along // 2, 2), ("p", "q", "y", "c"))
    every = ("p", "q", "y", "c")
    in_specs = (
        P(every, None),
        P(every, None),
        P(("p", "q"), None),
        P(None, every),
        P(every),
        P(every, None),
        P(every, None),
        P(every, None),
        P(None, every),
        P(every, None),
        P(None, None, every),
        P(None, every, None),
    )
    out_specs = (
        P(every, None),
        P(every, None),
        P(None, every),
        P(every),
        P(every, None),
        P(every, None),
        P(every, None),
        P(None, every),
        P(every, None),
        P(None, None, every),
        P(None, every, None),
    )
    return jax.shard_map(
        on_device, mesh=fine, in_specs=in_specs, out_specs=out_specs, check_vma=False
    )
```

```python
import jax
import jax.numpy as jnp
from jax import lax
from jax.experimental import pallas as pl
from jax.experimental.pallas import tpu as pltpu
from jax.sharding import Mesh
from jax.sharding import PartitionSpec as P

HEADS = 16
HD = 64
NB = 64
ROWS = 128
VMEM = 50 * 1024 * 1024


def matmul_in(left, right, dims):
    return lax.dot_general(left, right, (dims, ((), ())), preferred_element_type=jnp.float32)


def spread_bias(info_ref, bias_ref, spread_ref):
    width = spread_ref.shape[1]
    row = jnp.broadcast_to(bias_ref[0], (ROWS, width))
    spread_ref[...] = pltpu.roll(row, 0, 1, stride=1, stride_axis=0)


def half_mask(rows):
    lane = lax.broadcasted_iota(jnp.int32, (rows, 2 * HD), 1)
    start = lax.rem(pl.program_id(0), 2) * HD
    return (lane >= start) & (lane < start + HD)


def segment_at(position, first_end, second_end):
    return (position >= first_end).astype(jnp.int32) + (position >= second_end).astype(jnp.int32)


def weights_of(info_ref, spread_ref, query, keys, number):
    group = keys.shape[0]
    first_end, second_end, start = info_ref[0], info_ref[1], info_ref[2]
    raw = matmul_in(query, keys, ((1,), (1,)))
    shift = pl.multiple_of(group - start - number * ROWS, ROWS)
    bias = spread_ref[:, pl.ds(shift, group)]
    row = start + number * ROWS + lax.broadcasted_iota(jnp.int32, (ROWS, 1), 0)
    column = lax.broadcasted_iota(jnp.int32, (1, group), 1)
    same = segment_at(row, first_end, second_end) == segment_at(column, first_end, second_end)
    scores = jnp.where(same, raw * 0.125 + bias, -1e30)
    raised = jnp.exp(scores - jnp.max(scores, axis=1, keepdims=True))
    return raised * (1.0 / jnp.sum(raised, axis=1, keepdims=True))


def attend_kernel(info_ref, bias_ref, query_ref, key_ref, value_ref, out_ref, spread_ref):
    spread_bias(info_ref, bias_ref, spread_ref)
    mask = half_mask(ROWS)
    first = lax.rem(pl.program_id(0), 2) == 0
    for number in range(query_ref.shape[0] // ROWS):
        rows = pl.ds(number * ROWS, ROWS)
        query = jnp.where(mask, query_ref[rows, :], jnp.bfloat16(0))
        weights = weights_of(info_ref, spread_ref, query, key_ref[...], number)
        out = matmul_in(weights.astype(jnp.bfloat16), value_ref[...], ((1,), (0,)))
        out = out.astype(jnp.bfloat16)
        kept = jnp.where(first, out, out_ref[rows, :])
        out_ref[rows, :] = jnp.where(mask, out, kept)


def attend_back_kernel(
    info_ref,
    bias_ref,
    query_ref,
    key_ref,
    value_ref,
    grad_ref,
    query_grad_ref,
    key_grad_ref,
    value_grad_ref,
    sums_ref,
    spread_ref,
    diag_ref,
    weight_ref,
    score_ref,
    query_mid_ref,
    grad_mid_ref,
):
    spread_bias(info_ref, bias_ref, spread_ref)
    mask = half_mask(ROWS)
    group, width = key_ref.shape[0], spread_ref.shape[1]
    first = lax.rem(pl.program_id(0), 2) == 0
    diag_ref[...] = jnp.zeros(diag_ref.shape, jnp.float32)
    for number in range(query_ref.shape[0] // ROWS):
        rows = pl.ds(number * ROWS, ROWS)
        query = jnp.where(mask, query_ref[rows, :], jnp.bfloat16(0))
        grad = jnp.where(mask, grad_ref[rows, :], jnp.bfloat16(0))
        query_mid_ref[rows, :] = query
        grad_mid_ref[rows, :] = grad
        weights = weights_of(info_ref, spread_ref, query, key_ref[...], number)
        weight_ref[rows, :] = weights.astype(jnp.bfloat16)
        weight_grad = matmul_in(grad, value_ref[...], ((1,), (1,)))
        inner = jnp.sum(weights * weight_grad, axis=1, keepdims=True)
        score_grad = weights * (weight_grad - inner)
        shift = pl.multiple_of(group - info_ref[2] - number * ROWS, ROWS)
        diag_ref[:, pl.ds(shift, group)] += score_grad
        raw_grad = (score_grad * 0.125).astype(jnp.bfloat16)
        score_ref[rows, :] = raw_grad
        out = matmul_in(raw_grad, key_ref[...], ((1,), (0,))).astype(jnp.bfloat16)
        kept = jnp.where(first, out, query_grad_ref[rows, :])
        query_grad_ref[rows, :] = jnp.where(mask, out, kept)
    key_grad = matmul_in(score_ref[...], query_mid_ref[...], ((0,), (0,)))
    value_grad = matmul_in(weight_ref[...], grad_mid_ref[...], ((0,), (0,)))

    @pl.when(first)
    def _():
        key_grad_ref[...] = key_grad
        value_grad_ref[...] = value_grad

    @pl.when(jnp.logical_not(first))
    def _():
        key_grad_ref[...] += key_grad
        value_grad_ref[...] += value_grad

    total = diag_ref[...]
    size = ROWS // 2
    while size >= 8:
        total = total[:size] + pltpu.roll(total[size:], width - size, 1)
        size //= 2
    for size in (4, 2, 1):
        total = total + pltpu.roll(pltpu.roll(total, 8 - size, 0), width - size, 1)
    sums_ref[0] = total[0:1]


def attend_specs(rows, group, width, pairs):
    return [
        pl.BlockSpec(memory_space=pltpu.SMEM),
        pl.BlockSpec((1, 1, width), lambda h: (h, 0, 0)),
        pl.BlockSpec((rows, 2 * HD), lambda h: (0, h // 2)),
        pl.BlockSpec((group, 2 * HD), lambda h: (0, h // 2)),
        pl.BlockSpec((group, 2 * HD), lambda h: (0, pairs + h // 2)),
    ]


def cost_of(heads, rows, group, products):
    return pl.CostEstimate(
        flops=2 * products * heads * rows * group * HD,
        bytes_accessed=4 * heads * HD * (rows + group),
        transcendentals=heads * rows * group,
    )


def attend(info, bias, query, both):
    heads, _, width = bias.shape
    rows, group = query.shape[0], both.shape[0]
    pairs = heads // 2
    return pl.pallas_call(
        attend_kernel,
        grid=(heads,),
        in_specs=attend_specs(rows, group, width, pairs),
        out_specs=pl.BlockSpec((rows, 2 * HD), lambda h: (0, h // 2)),
        out_shape=jax.ShapeDtypeStruct((rows, heads * HD), jnp.bfloat16),
        scratch_shapes=[pltpu.VMEM((ROWS, width), jnp.float32)],
        compiler_params=pltpu.CompilerParams(vmem_limit_bytes=VMEM),
        cost_estimate=cost_of(heads, rows, group, 2),
        name="attend",
    )(info, bias, query, both, both)


def attend_back(info, bias, query, both, grad):
    heads, _, width = bias.shape
    rows, group = query.shape[0], both.shape[0]
    pairs = heads // 2
    pair_block = pl.BlockSpec((rows, 2 * HD), lambda h: (0, h // 2))
    group_block = pl.BlockSpec((group, 2 * HD), lambda h: (0, h // 2))
    return pl.pallas_call(
        attend_back_kernel,
        grid=(heads,),
        in_specs=attend_specs(rows, group, width, pairs) + [pair_block],
        out_specs=[pair_block, group_block, group_block, pl.BlockSpec((1, 1, width), lambda h: (h, 0, 0))],
        out_shape=[
            jax.ShapeDtypeStruct((rows, heads * HD), jnp.bfloat16),
            jax.ShapeDtypeStruct((group, heads * HD), jnp.float32),
            jax.ShapeDtypeStruct((group, heads * HD), jnp.float32),
            jax.ShapeDtypeStruct((heads, 1, width), jnp.float32),
        ],
        scratch_shapes=[
            pltpu.VMEM((ROWS, width), jnp.float32),
            pltpu.VMEM((ROWS, width), jnp.float32),
            pltpu.VMEM((rows, group), jnp.bfloat16),
            pltpu.VMEM((rows, group), jnp.bfloat16),
            pltpu.VMEM((rows, 2 * HD), jnp.bfloat16),
            pltpu.VMEM((rows, 2 * HD), jnp.bfloat16),
        ],
        compiler_params=pltpu.CompilerParams(vmem_limit_bytes=VMEM),
        cost_estimate=cost_of(heads, rows, group, 5),
        name="attend_back",
    )(info, bias, query, both, both, grad)


LANES = 128
EDGE = 16


def reach_of(info_ref, rows, group):
    position = info_ref[2] + lax.broadcasted_iota(jnp.int32, (rows, LANES), 0)
    first_end, second_end = info_ref[0], info_ref[1]
    low = jnp.where(position >= second_end, second_end, jnp.where(position >= first_end, first_end, 0))
    high = jnp.where(position < first_end, first_end, jnp.where(position < second_end, second_end, group))
    return (low - position, high - position)


def within(reach, shift):
    if shift < 0:
        return reach[0] <= shift
    return reach[1] > shift


def fill(pad_ref, low_ref, mid_ref, high_ref):
    rows = mid_ref.shape[0]
    pad_ref[0:EDGE, :] = low_ref[...].astype(jnp.float32)
    pad_ref[EDGE : EDGE + rows, :] = mid_ref[...].astype(jnp.float32)
    pad_ref[EDGE + rows :, :] = high_ref[...].astype(jnp.float32)


def taps_of(pad_ref, depth_ref, reach, base, rows, taps, mirror):
    margin = (taps - 1) // 2
    total = jnp.zeros((rows, LANES), jnp.float32)
    for tap in range(taps):
        shift = margin - tap if mirror else tap - margin
        piece = pad_ref[EDGE + base + shift : EDGE + base + shift + rows, :] * depth_ref[tap : tap + 1, :]
        if shift:
            piece = jnp.where(within(reach, shift), piece, 0.0)
        total = total + piece
    return total


def conv_kernel(group, taps, info_ref, low_ref, mid_ref, high_ref, depth_ref, out_ref, pad_ref):
    fill(pad_ref, low_ref, mid_ref, high_ref)
    low, high = reach_of(info_ref, mid_ref.shape[0], group)
    for base in range(0, mid_ref.shape[0], STEP):
        reach = (low[base : base + STEP], high[base : base + STEP])
        out_ref[base : base + STEP, :] = taps_of(pad_ref, depth_ref, reach, base, STEP, taps, False)


STEP = 64


def conv_back_kernel(
    group,
    taps,
    info_ref,
    low_ref,
    mid_ref,
    high_ref,
    grad_low_ref,
    grad_mid_ref,
    grad_high_ref,
    depth_ref,
    out_ref,
    depth_grad_ref,
    pad_ref,
    grad_pad_ref,
    sum_ref,
):
    fill(pad_ref, low_ref, mid_ref, high_ref)
    fill(grad_pad_ref, grad_low_ref, grad_mid_ref, grad_high_ref)
    low, high = reach_of(info_ref, mid_ref.shape[0], group)
    margin = (taps - 1) // 2
    sum_ref[...] = jnp.zeros(sum_ref.shape, jnp.float32)
    for base in range(0, mid_ref.shape[0], STEP):
        reach = (low[base : base + STEP], high[base : base + STEP])
        out_ref[base : base + STEP, :] = taps_of(grad_pad_ref, depth_ref, reach, base, STEP, taps, True)
        grad = grad_pad_ref[EDGE + base : EDGE + base + STEP, :]
        for tap in range(taps):
            shift = tap - margin
            piece = pad_ref[EDGE + base + shift : EDGE + base + shift + STEP, :] * grad
            if shift:
                piece = jnp.where(within(reach, shift), piece, 0.0)
            sum_ref[8 * tap : 8 * tap + 8, :] += jnp.sum(piece.reshape(STEP // 8, 8, LANES), axis=0)
    for tap in range(taps):
        depth_grad_ref[tap : tap + 1, :] = jnp.sum(sum_ref[8 * tap : 8 * tap + 8, :], axis=0, keepdims=True)


def lane_block(rows):
    return pl.BlockSpec((rows, LANES), lambda i: (0, i))


def conv(info, low, mid, high, depth, group):
    rows, width = mid.shape
    taps = depth.shape[0]
    return pl.pallas_call(
        lambda *refs: conv_kernel(group, taps, *refs),
        grid=(width // LANES,),
        in_specs=[pl.BlockSpec(memory_space=pltpu.SMEM)]
        + [lane_block(EDGE), lane_block(rows), lane_block(EDGE), lane_block(taps)],
        out_specs=lane_block(rows),
        out_shape=jax.ShapeDtypeStruct((rows, width), jnp.float32),
        scratch_shapes=[pltpu.VMEM((rows + 2 * EDGE, LANES), jnp.float32)],
        compiler_params=pltpu.CompilerParams(vmem_limit_bytes=VMEM),
        cost_estimate=pl.CostEstimate(
            flops=2 * taps * rows * width, bytes_accessed=6 * rows * width, transcendentals=0
        ),
        name="conv",
    )(info, low, mid, high, depth)


def conv_back(info, low, mid, high, grad_low, grad_mid, grad_high, depth, group):
    rows, width = mid.shape
    taps = depth.shape[0]
    return pl.pallas_call(
        lambda *refs: conv_back_kernel(group, taps, *refs),
        grid=(width // LANES,),
        in_specs=[pl.BlockSpec(memory_space=pltpu.SMEM)]
        + [lane_block(EDGE), lane_block(rows), lane_block(EDGE)] * 2
        + [lane_block(taps)],
        out_specs=[lane_block(rows), lane_block(taps)],
        out_shape=[
            jax.ShapeDtypeStruct((rows, width), jnp.float32),
            jax.ShapeDtypeStruct((taps, width), jnp.float32),
        ],
        scratch_shapes=[
            pltpu.VMEM((rows + 2 * EDGE, LANES), jnp.float32),
            pltpu.VMEM((rows + 2 * EDGE, LANES), jnp.float32),
            pltpu.VMEM((8 * taps, LANES), jnp.float32),
        ],
        compiler_params=pltpu.CompilerParams(vmem_limit_bytes=VMEM),
        cost_estimate=pl.CostEstimate(
            flops=4 * taps * rows * width, bytes_accessed=8 * rows * width, transcendentals=0
        ),
        name="conv_back",
    )(info, low, mid, high, grad_low, grad_mid, grad_high, depth)


EPS = 1e-05
CORES = [(0, 1), (1, 0)]


def low(values):
    return values.astype(jnp.bfloat16)


def product(left_in, right_in):
    return jnp.dot(left_in, right_in, preferred_element_type=jnp.float32)


def left_product(left_in, right_in):
    return jnp.einsum("nd,nf->df", left_in, right_in, preferred_element_type=jnp.float32)


def right_product(left_in, right_in):
    return jnp.einsum("nf,df->nd", left_in, right_in, preferred_element_type=jnp.float32)


def swap(values, axis="c"):
    return lax.ppermute(values, axis, CORES)


def ordered(mine, other, place, dim=0):
    first = place == 0
    return jnp.concatenate([jnp.where(first, mine, other), jnp.where(first, other, mine)], axis=dim)


def choose(values, place, dim):
    return lax.dynamic_index_in_dim(values, place, dim, keepdims=False)


def pair_rows(values):
    return ordered(values, swap(values), lax.axis_index("c"))


def pair_sum(partial):
    place = lax.axis_index("c")
    halves = partial.reshape(2, partial.shape[0] // 2, partial.shape[1])
    received = swap(low(choose(halves, 1 - place, 0)))
    return choose(halves, place, 0) + received.astype(jnp.float32)


def gather_axis(values, axis):
    if lax.axis_size(axis) == 2:
        return ordered(values, swap(values, axis), lax.axis_index(axis))
    return lax.all_gather(values, axis, axis=0, tiled=True)


def pick(values, axis, dim):
    return choose(values, 1 - lax.axis_index(axis), dim)


def send(values, axis, dim):
    if lax.axis_size(axis) == 2:
        return swap(pick(values, axis, dim), axis)
    return lax.psum_scatter(values, axis, scatter_dimension=dim, tiled=False)


def add(values, received, axis, dim):
    if lax.axis_size(axis) != 2:
        return received
    kept = choose(values, lax.axis_index(axis), dim)
    return (kept.astype(jnp.float32) + received.astype(jnp.float32)).astype(values.dtype)


def together(*values):
    return lax.optimization_barrier(values)


def placed(parts):
    own, across, both, along = parts
    q, y = lax.axis_index("q"), lax.axis_index("y")
    result = jnp.zeros((own.shape[0], 2, 2) + own.shape[1:], own.dtype)
    for part, at_q, at_y in ((own, q, y), (across, 1 - q, y), (both, 1 - q, 1 - y), (along, q, 1 - y)):
        at = (0, at_q, at_y) + (0,) * (own.ndim - 1)
        result = lax.dynamic_update_slice(result, part[:, None, None], at)
    return result


def normalize(values):
    average = jnp.mean(values, axis=-1, keepdims=True)
    centred = values - average
    inverse = lax.rsqrt(jnp.mean(centred * centred, axis=-1, keepdims=True) + EPS)
    return (centred * inverse, inverse)


def norm_back(upstream, normed, inverse, gain):
    gain_grad = jnp.sum(upstream * normed, axis=0)
    scaled = upstream * gain
    back = inverse * (
        scaled
        - jnp.mean(scaled, axis=-1, keepdims=True)
        - normed * jnp.mean(scaled * normed, axis=-1, keepdims=True)
    )
    return (back, gain_grad)


def silu_slope(values):
    sigma = jax.nn.sigmoid(values)
    return sigma * (1.0 + values * (1.0 - sigma))


def split_normalize(values):
    width = values.shape[1]
    average = jnp.mean(values, axis=1)
    centred = values - average[:, None]
    spread = jnp.sum(centred * centred, axis=1)
    other = swap(jnp.stack([average, spread]))
    gap = average - other[0]
    whole = spread + other[1] + (0.5 * width) * gap * gap
    inverse = lax.rsqrt(whole / (2 * width) + EPS)
    middle = 0.5 * (average + other[0])
    return ((values - middle[:, None]) * inverse[:, None], inverse[:, None])


def split_norm_back(upstream, normed, inverse, gain):
    gain_grad = jnp.sum(upstream * normed, axis=0)
    scaled = upstream * gain
    sums = jnp.stack([jnp.sum(scaled, axis=1), jnp.sum(scaled * normed, axis=1)])
    means = (sums + swap(sums)) / (2 * scaled.shape[1])
    back = inverse * (scaled - means[0][:, None] - normed * means[1][:, None])
    return (back, gain_grad)


def feed_forward(hidden, gain, inner, outer):
    rows = hidden.shape[0]
    normed, inverse = normalize(hidden)
    entry = low(normed * gain)
    both = jnp.concatenate([entry, swap(entry)], axis=0)
    middle = right_product(both, inner)
    activated = low(jax.nn.silu(middle))
    partial = product(activated, outer)
    received = swap(low(partial[rows:]))
    result = hidden + 0.5 * (partial[:rows] + received.astype(jnp.float32))
    return (result, (normed, inverse, both, middle, activated))


def feed_back(upstream, gain, inner, outer, kept):
    normed, inverse, both, middle, activated = kept
    rows = upstream.shape[0]
    half = low(0.5 * upstream)
    half_both = jnp.concatenate([half, swap(half)], axis=0)
    active_grad = right_product(half_both, outer)
    middle_grad = low(active_grad * silu_slope(middle))
    partial = product(middle_grad, inner)
    received = swap(low(partial[rows:]))
    entry_grad = partial[:rows] + received.astype(jnp.float32)
    back, gain_grad = norm_back(entry_grad, normed, inverse, gain)

    eighth = middle.shape[1] // 8

    def inner_grad(first, end):
        return left_product(middle_grad[:, first * eighth : end * eighth], both)

    def outer_grad(first, end):
        return left_product(activated[:, first * eighth : end * eighth], half_both)

    return (upstream + back, gain_grad, inner_grad, outer_grad)


def bucket_hits(group):
    offset = group - jnp.arange(2 * group, dtype=jnp.int32)
    distance = jnp.abs(offset)
    level = jnp.zeros_like(distance)
    for power in range(1, 14):
        level = level + (distance >= 2**power).astype(jnp.int32)
    plain = jnp.where(distance < 16, distance, jnp.minimum(12 + level, 31))
    bucket = plain + 32 * (offset < 0).astype(jnp.int32)
    return bucket[:, None] == jnp.arange(NB, dtype=jnp.int32)[None, :]


def halos(values):
    count = lax.axis_size("y")
    forward = [(i, i + 1) for i in range(count - 1)]
    backward = [(target, source) for source, target in forward]
    return (
        lax.ppermute(values[-EDGE:], "y", forward),
        lax.ppermute(values[:EDGE], "y", backward),
    )


CHIPS = ("p", "q", "y")


def on_device(
    frames,
    cotangent,
    lengths,
    norm_gains,
    position_bias,
    attend_weight,
    merge_weight,
    glu_weight,
    depth_weight,
    point_weight,
    inner_weight,
    outer_weight,
):
    core = lax.axis_index("c")
    grid = tuple(lax.axis_size(axis) for axis in CHIPS)
    chips = grid[0] * grid[1] * grid[2]
    rows, width = frames.shape
    pair = 2 * rows
    group = pair * grid[2]
    half = width // 2
    share = attend_weight.shape[0]
    units = inner_weight.shape[2]
    taps = depth_weight.shape[0]
    heads = HEADS // 2
    f32 = jnp.float32

    small = jnp.concatenate([norm_gains.reshape(-1), position_bias, depth_weight.reshape(-1)])
    count = small.shape[0]
    small_rows = -(-2 * count // (16 * width)) * 16
    small_both = ordered(small[None], swap(small[None]), core).reshape(-1)
    small_both = jnp.pad(small_both, (0, small_rows * width - 2 * count)).reshape(small_rows, width)

    inner_pack = inner_weight[0].T
    outer_pack = jnp.concatenate([outer_weight[0], small_both], axis=0)
    pack_two = jnp.concatenate([inner_weight[1].T, outer_weight[1]], axis=0)
    attend_weight, glu_weight = together(attend_weight, glu_weight, outer_pack)[:2]

    def own_columns(weight, shape, dim):
        parts = weight.reshape((share,) + shape)
        mine = choose(parts, core, dim).reshape(share, -1)
        other = swap(choose(parts, 1 - core, dim).reshape(share, -1))
        return ordered(mine, other, core)

    attend_part = own_columns(attend_weight, (3, 2, half), 2)
    glu_part = own_columns(glu_weight, (2, chips, 2, share), 3)
    mixed_pack = jnp.concatenate(
        [attend_part.reshape(-1, width), glu_part, merge_weight, point_weight], axis=0
    )

    square = grid[1] == 2 and grid[2] == 2
    marks = [0]
    for size in (3 * share, 2 * share, share, share):
        marks.append(marks[-1] + size)

    def gather_p(values):
        return lax.all_gather(values, "p", axis=0)

    def in_halves(*parts):
        parts = [part.reshape(grid[0], units, width) for part in parts]
        near = [part[:, : units // 2].reshape(-1, width) for part in parts]
        far = [part[:, units // 2 :].reshape(-1, width) for part in parts]
        return jnp.concatenate(near + far, axis=0)

    if square:
        inner = gather_p(inner_pack)
        two_x, two_y = together(swap(pack_two, "q"), swap(pack_two, "y"))
        pack_two = jnp.stack([pack_two, two_x, swap(two_x, "y"), two_y])
        whole_one = gather_p(outer_pack)
        inner, pack_two = together(inner.reshape(-1, width), pack_two)
        inner_x, inner_y = together(swap(inner, "q"), swap(inner, "y"))
        mixed_pack, inner_x, inner_y = together(mixed_pack, inner_x, inner_y)
        mixed = gather_p(mixed_pack)
        inner_xy = swap(inner_y, "q")
        outer = whole_one[:, :units].reshape(-1, width)
        tiny = whole_one[:, units:]
        outer, tiny = together(outer, tiny)
        across = [(0, 3), (3, 0), (1, 2), (2, 1)]
        tiny_xy = lax.ppermute(tiny, ("q", "y"), across)
        outer_x, outer_y, tiny_x, tiny_y, tiny_xy = together(
            swap(outer, "q"), swap(outer, "y"), swap(tiny, "q"), swap(tiny, "y"), tiny_xy
        )
        small_full = placed((tiny, tiny_x, tiny_xy, tiny_y)).reshape(chips, -1)
        outer_xy = swap(outer_x, "y")
        mixed, pack_two = together(mixed, pack_two)
        whole_two = gather_p(pack_two).reshape(chips, 2 * units, width)
        attend_part = mixed[:, : marks[1]].reshape(grid[0], 2 * share, 3 * half)
        rest_part = mixed[:, marks[1] :]
        attend_part, rest_part = together(attend_part, rest_part)
        attend_x = swap(attend_part, "q")
        inner_xy, outer_xy, attend_x, attend_part, rest_part = together(
            inner_xy, outer_xy, attend_x, attend_part, rest_part
        )
        inner_one = in_halves(inner, inner_x, inner_xy, inner_y)
        outer_one = in_halves(outer, outer_x, outer_xy, outer_y)
        attend_y, rest_x = swap(attend_part, "y"), swap(rest_part, "q")
    else:
        inner_one = lax.all_gather(inner_pack, CHIPS, axis=0, tiled=True)
        whole_one = lax.all_gather(outer_pack, CHIPS, axis=0)
        mixed = lax.all_gather(mixed_pack, CHIPS, axis=0)
        whole_two = lax.all_gather(pack_two, CHIPS, axis=0)
        outer_one = whole_one[:, :units].reshape(chips * units, width)
        small_full = whole_one[:, units:].reshape(chips, -1)

    small_full = small_full[:, : 2 * count].reshape(chips, 2, count)
    gain_size = norm_gains.size
    gains = small_full[..., :gain_size].reshape(chips, 2, 6, -1).astype(f32)
    gain_table = gains.transpose(2, 0, 1, 3).reshape(6, width)
    gain_mid = choose(gains[:, :, 3], core, 1).reshape(half)
    bias_table = small_full[..., gain_size : gain_size + position_bias.size].reshape(NB, 2, heads)
    bias_table = choose(bias_table, core, 1)
    depth = choose(small_full[..., gain_size + position_bias.size :], core, 1)
    depth = depth.reshape(chips, taps, share).transpose(1, 0, 2).reshape(taps, half).astype(f32)

    start = lax.axis_index("y") * pair
    info = jnp.stack([lengths[0, 0], lengths[0, 0] + lengths[0, 1], start.astype(jnp.int32)])
    hits = bucket_hits(group)
    bias = jnp.einsum("bh,wb->hw", bias_table, hits.astype(jnp.bfloat16), preferred_element_type=f32)
    bias = bias[:, None, :]

    hidden = frames.astype(f32)
    first, first_kept = feed_forward(hidden, gain_table[0], inner_one, outer_one)
    if square:
        first, attend_y, rest_part = together(first, attend_y, rest_part)
        rest_y = swap(rest_part, "y")
        attend_full = placed((attend_part, attend_x, swap(attend_y, "q"), attend_y))
    else:
        attend_full = mixed[:, : marks[1]]
    attend_full = attend_full.reshape(width, 3 * half)
    normed_att, inverse_att = normalize(first)
    att_entry = pair_rows(low(normed_att * gain_table[1]))
    triple = low(product(att_entry, attend_full))
    query = triple[:, :half]
    key_value = triple[:, half:]
    if square:
        key_value, rest_x, rest_y = together(key_value, rest_x, rest_y)
        rest_xy = swap(rest_y, "q")
    both = gather_axis(key_value, "y")
    attended = attend(info, bias, query, both)
    if square:
        attended, rest_xy = together(attended, rest_xy)
        rest = placed((rest_part, rest_x, rest_xy, rest_y)).reshape(chips, -1, width)
    else:
        rest = mixed[:, marks[1] :]
    marks = [mark - marks[1] for mark in marks]
    glu_full = rest[:, : marks[2]].reshape(width, width)
    merge_half = rest[:, marks[2] : marks[3]]
    point_full = rest[:, marks[3] : marks[4]].reshape(half, width)
    sides = merge_half.reshape(2, chips // 2, share, width)
    merge_full = ordered(
        choose(sides, core, 0)[:, None], swap(choose(sides, 1 - core, 0))[:, None], core, 1
    ).reshape(half, width)
    second = first + pair_sum(product(attended, merge_full))
    normed_conv, inverse_conv = normalize(second)
    conv_entry = pair_rows(low(normed_conv * gain_table[2]))
    gate_up = product(conv_entry, glu_full)
    gate_sig = jax.nn.sigmoid(gate_up[:, half:])
    glu_rows = low(gate_up[:, :half] * gate_sig)
    glu_low, glu_high = halos(glu_rows)
    mixed_rows = conv(info, glu_low, glu_rows, glu_high, depth, group)
    normed_mid, inverse_mid = split_normalize(mixed_rows)
    activated = normed_mid * gain_mid
    swish = low(jax.nn.silu(activated))
    third = second + pair_sum(product(swish, point_full))
    inner_two = whole_two[:, :units].reshape(chips * units, width)
    outer_two = whole_two[:, units:].reshape(chips * units, width)
    fourth, fourth_kept = feed_forward(third, gain_table[4], inner_two, outer_two)
    normed_last, inverse_last = normalize(fourth)
    result = low(normed_last * gain_table[5])

    def by_chip(values):
        return values.reshape(grid + (values.shape[0] // chips, values.shape[1]))

    def last_sum(values):
        return lax.psum_scatter(values, "p", scatter_dimension=0, tiled=False)

    size = grid[0] * units // 2

    def early_sum(grad):
        shape = (grid[0], 4) if square else grid
        return last_sum(low(grad).reshape(shape + (units, width)))

    grad_fourth, gain_five = norm_back(
        cotangent.astype(f32), normed_last, inverse_last, gain_table[5]
    )
    grad_third, gain_four, inner_two_grad, outer_two_grad = feed_back(
        grad_fourth, gain_table[4], inner_two, outer_two, fourth_kept
    )

    outer_two_sum = early_sum(outer_two_grad(0, 8))

    conv_out_grad = pair_rows(low(grad_third))
    swish_grad = right_product(conv_out_grad, point_full)
    act_grad = swish_grad * silu_slope(activated)
    mixed_grad, gain_three = split_norm_back(act_grad, normed_mid, inverse_mid, gain_mid)
    mixed_low = low(mixed_grad)
    grad_low, grad_high = halos(mixed_low)
    if square:
        inner_two = low(inner_two_grad(0, 8)).reshape(grid[0], 4, units, width)
        inner_two_a, mixed_low = together(inner_two[:, 1:3], mixed_low)
        inner_two_a = swap(inner_two_a, "q")
    glu_back, depth_grad = conv_back(
        info, glu_low, glu_rows, glu_high, grad_low, mixed_low, grad_high, depth, group
    )
    value_part = gate_up[:, :half]
    gate_grad = low(
        jnp.concatenate(
            [glu_back * gate_sig, glu_back * value_part * gate_sig * (1.0 - gate_sig)], axis=1
        )
    )
    conv_entry_grad = pair_sum(right_product(gate_grad, glu_full))
    point_grad = by_chip(low(left_product(swish, conv_out_grad)))
    glu_grad = by_chip(low(left_product(conv_entry, gate_grad)))
    back_conv, gain_two = norm_back(conv_entry_grad, normed_conv, inverse_conv, gain_table[2])
    grad_second = grad_third + back_conv

    att_out_grad = pair_rows(low(grad_second))
    glu_sum = last_sum(glu_grad)
    point_a = send(point_grad, "y", 2)
    merge_grad = low(left_product(attended, att_out_grad)).reshape(chips // 2, 2, share, width)
    merge_grad = ordered(
        choose(merge_grad, core, 1)[None], swap(choose(merge_grad, 1 - core, 1))[None], core
    )
    merge_grad = by_chip(merge_grad.reshape(chips * share, width))
    attended_grad = low(right_product(att_out_grad, merge_full))
    merge_a = send(merge_grad, "y", 2)
    query_grad, key_grad, value_grad, table_sums = attend_back(info, bias, query, both, attended_grad)
    query_grad, key_grad, value_grad, point_a, merge_a = together(
        query_grad, key_grad, value_grad, point_a, merge_a
    )
    point_half = add(point_grad, point_a, "y", 2)
    merge_half = add(merge_grad, merge_a, "y", 2)
    both_grad = jnp.concatenate([key_grad, value_grad], axis=1).reshape(grid[2], pair, width)
    if grid[2] == 2:
        place = lax.axis_index("y")
        both_received = swap(low(choose(both_grad, 1 - place, 0)), "y")
        both_grad = low(choose(both_grad, place, 0) + both_received.astype(f32))
    else:
        both_received = low(lax.psum_scatter(both_grad, "y", scatter_dimension=0, tiled=False))
        both_grad = both_received
    if square:
        point_b, merge_b, outer_two_a, inner_two_a, both_grad = together(
            pick(point_half, "q", 1),
            pick(merge_half, "q", 1),
            outer_two_sum[1:3],
            inner_two_a,
            both_grad,
        )
        inner_two_b = low(inner_two[:, 3].astype(f32) + inner_two_a[:, 1].astype(f32))
        inner_two_b = swap(inner_two_b, "y")
        point_b, merge_b, outer_two_a = [swap(part, "q") for part in (point_b, merge_b, outer_two_a)]
    else:
        point_b, merge_b = send(point_half, "q", 1), send(merge_half, "q", 1)
        inner_two_sum = early_sum(inner_two_grad(0, 8))
    triple_grad = jnp.concatenate([query_grad, both_grad], axis=1)
    attend_grad = low(left_product(att_entry, triple_grad))
    attend_grad = attend_grad.reshape(grid + (2 * share, 3 * half))
    att_entry_grad = pair_sum(right_product(triple_grad, attend_full))
    back_att, gain_one = norm_back(att_entry_grad, normed_att, inverse_att, gain_table[1])
    grad_first = grad_second + back_att
    attend_grad, glu_sum = together(attend_grad, glu_sum)
    attend_sum = last_sum(attend_grad)
    if square:
        inner_two_sum = inner_two[:, 0].astype(f32) + inner_two_a[:, 0].astype(f32)
    input_grad, gain_zero, inner_one_grad, outer_one_grad = feed_back(
        grad_first, gain_table[0], inner_one, outer_one, first_kept
    )
    if square:
        near_o, near_i, point_b, merge_b, inner_two_b, glu_sum = together(
            low(outer_one_grad(1, 3)),
            low(inner_one_grad(2, 4)),
            point_b,
            merge_b,
            inner_two_b,
            glu_sum,
        )
        near_o, near_i = swap(near_o, "q"), swap(near_i, "y")
        inner_two_sum = low(inner_two_sum + inner_two_b.astype(f32))
    mixed_sum = jnp.concatenate(
        [
            add(point_half, point_b, "q", 1),
            add(merge_half, merge_b, "q", 1),
        ]
        + ([inner_two_sum] if square else []),
        axis=1,
    )
    if square:
        near_o, near_i, far_o, far_i, mixed_sum, outer_two_a, attend_sum = together(
            near_o,
            near_i,
            low(outer_one_grad(5, 7)),
            low(inner_one_grad(6, 8)),
            mixed_sum,
            outer_two_a,
            attend_sum,
        )
        glu_a = swap(pick(glu_sum, "q", 0), "q")
        far_o, far_i = swap(far_o, "q"), swap(far_i, "y")
        mixed_sum = last_sum(mixed_sum)

        def second(first, got_o, got_i):
            return together(
                low(outer_one_grad(first + 3, first + 4) + got_o[size:].astype(f32)),
                low(inner_one_grad(first + 1, first + 2) + got_i[:size].astype(f32)),
            )

        def third(first, got_o, got_i, end_o, end_i):
            sum_o = outer_one_grad(first, first + 1) + got_o[:size].astype(f32)
            sum_i = inner_one_grad(first, first + 1) + got_i[size:].astype(f32)
            sums = [low(sum_i + end_i.astype(f32)), low(sum_o + end_o.astype(f32))]
            return [part.reshape(grid[0], units // 2, width) for part in sums]

        near = second(0, near_o, near_i)
        near = together(swap(near[0], "y"), swap(near[1], "q"))
        near = jnp.concatenate(third(0, near_o, near_i, *near), axis=1)
        far_o, far_i, near, mixed_sum = together(far_o, far_i, near, mixed_sum)
        near_sum = last_sum(near)
        far = second(4, far_o, far_i)
        far = together(swap(far[0], "y"), swap(far[1], "q"))
        far = third(4, far_o, far_i, *far)
        outer_two_b = swap(low(outer_two_sum[3].astype(f32) + outer_two_a[1].astype(f32)), "y")
        outer_sum_two = outer_two_sum[0].astype(f32) + outer_two_a[0].astype(f32)
        outer_sum_two = low(outer_sum_two + outer_two_b.astype(f32))
        inner_sum_two = mixed_sum[2 * share :]
        glu_half = add(glu_sum, glu_a, "q", 0)
    else:
        mixed_sum = last_sum(mixed_sum)
        glu_half = send(glu_sum, "q", 0)
        inner_sum_one = by_chip(low(inner_one_grad(0, 8)))
        outer_sum_one = by_chip(low(outer_one_grad(0, 8)))
        inner_sum_one = send(send(inner_sum_one, "y", 2), "q", 1)
        outer_sum_one = send(send(outer_sum_one, "y", 2), "q", 1)
        inner_sum_two = send(send(inner_two_sum, "y", 1), "q", 0)
        outer_sum_two = send(send(outer_two_sum, "y", 1), "q", 0)
    glu_sum = add(glu_half, send(glu_half, "y", 0), "y", 0)
    attend_half = add(attend_sum, send(attend_sum, "q", 0), "q", 0)
    attend_sum = add(attend_half, send(attend_half, "y", 0), "y", 0)

    table_grad = jnp.einsum(
        "hw,wb->bh", table_sums[:, 0], hits.astype(f32), precision=lax.Precision.HIGHEST
    )

    def of_core(values, dim):
        empty = jnp.zeros_like(values)
        return jnp.stack(
            [jnp.where(core == 0, values, empty), jnp.where(core == 1, values, empty)], axis=dim
        )

    gain_three = of_core(gain_three.reshape(chips, share), 1).reshape(width)
    gain_grads = jnp.stack([gain_zero, gain_one, gain_two, gain_three, gain_four, gain_five])
    small_grads = jnp.concatenate(
        [
            gain_grads.reshape(6, chips, 2, share).transpose(1, 2, 0, 3).reshape(chips, 2, -1),
            of_core(table_grad, 1).reshape(chips, 2, -1),
            of_core(depth_grad.reshape(taps, chips, share).transpose(1, 0, 2), 1).reshape(
                chips, 2, -1
            ),
        ],
        axis=2,
    )
    small_sum = choose(small_grads, core, 1) + swap(choose(small_grads, 1 - core, 1))
    small_sum = small_sum.reshape(grid + (count,))
    small_sum = add(small_sum, send(small_sum, "y", 2), "y", 2)
    small_sum = add(small_sum, send(small_sum, "q", 1), "q", 1)
    one_rows = -(-count // (16 * width)) * 16
    small_sum = jnp.pad(low(small_sum), ((0, 0), (0, one_rows * width - count)))
    small_sum = small_sum.reshape(grid[0], one_rows, width)

    if square:
        far_sum, near_sum = together(jnp.concatenate(far + [small_sum], axis=1), near_sum)
        far_sum = last_sum(far_sum)
        half_units = units // 2
        inner_sum_one = jnp.concatenate([near_sum[:half_units], far_sum[:half_units]])
        outer_sum_one = jnp.concatenate([near_sum[half_units:], far_sum[half_units:units]])
        small_sum = far_sum[units:]
    else:
        one_sum = last_sum(jnp.concatenate([inner_sum_one, outer_sum_one, small_sum], axis=1))
        inner_sum_one, outer_sum_one = one_sum[:units], one_sum[units : 2 * units]
        small_sum = one_sum[2 * units :]

    def whole_columns(values, shape, dim):
        parts = values.reshape(2, share, -1)
        mine = choose(parts, core, 0)
        other = swap(choose(parts, 1 - core, 0))
        joined = ordered(
            jnp.expand_dims(mine.reshape((share,) + shape), dim),
            jnp.expand_dims(other.reshape((share,) + shape), dim),
            core,
            dim,
        )
        return joined.reshape(share, -1).astype(f32)

    attend_out = whole_columns(attend_sum, (3, half), 2)
    glu_out = whole_columns(glu_sum, (2, chips, share), 3)
    point_out = mixed_sum[:share].astype(f32)
    merge_out = mixed_sum[share : 2 * share].astype(f32)
    inner_out = jnp.stack([inner_sum_one.T, inner_sum_two.T]).astype(f32)
    outer_out = jnp.stack([outer_sum_one, outer_sum_two]).astype(f32)
    small_out = small_sum.reshape(-1)[:count].astype(f32)
    gains_out = small_out[:gain_size].reshape(norm_gains.shape)
    position_out = small_out[gain_size : gain_size + position_bias.size]
    depth_out = small_out[gain_size + position_bias.size :].reshape(taps, share)
    return (
        result,
        input_grad,
        gains_out,
        position_out,
        attend_out,
        merge_out,
        glu_out,
        depth_out,
        point_out,
        inner_out,
        outer_out,
    )


def solution(mesh):
    across, along = mesh.shape["dp"], mesh.shape["head"]
    fine = Mesh(mesh.devices.reshape(4, across // 4, along // 2, 2), ("p", "q", "y", "c"))
    every = ("p", "q", "y", "c")
    in_specs = (
        P(every, None),
        P(every, None),
        P(("p", "q"), None),
        P(None, every),
        P(every),
        P(every, None),
        P(every, None),
        P(every, None),
        P(None, every),
        P(every, None),
        P(None, None, every),
        P(None, every, None),
    )
    out_specs = (
        P(every, None),
        P(every, None),
        P(None, every),
        P(every),
        P(every, None),
        P(every, None),
        P(every, None),
        P(None, every),
        P(every, None),
        P(None, None, every),
        P(None, every, None),
    )
    return jax.shard_map(
        on_device, mesh=fine, in_specs=in_specs, out_specs=out_specs, check_vma=False
    )
```

```python
import jax
import jax.numpy as jnp
from jax import lax
from jax.experimental import pallas as pl
from jax.experimental.pallas import tpu as pltpu
from jax.sharding import Mesh
from jax.sharding import PartitionSpec as P

HEADS = 16
HD = 64
NB = 64
ROWS = 128
VMEM = 50 * 1024 * 1024


def matmul_in(left, right, dims):
    return lax.dot_general(left, right, (dims, ((), ())), preferred_element_type=jnp.float32)


def spread_of(bias):
    row = jnp.broadcast_to(bias, (ROWS, bias.shape[1]))
    return pltpu.roll(row, 0, 1, stride=1, stride_axis=0)


def half_mask(rows, half):
    lane = lax.broadcasted_iota(jnp.int32, (rows, 2 * HD), 1)
    return lane < HD if half == 0 else lane >= HD


def segment_at(position, first_end, second_end):
    return (position >= first_end).astype(jnp.int32) + (position >= second_end).astype(jnp.int32)


def weights_of(info_ref, spread_ref, raw, number):
    group = raw.shape[1]
    first_end, second_end, start = info_ref[0], info_ref[1], info_ref[2]
    shift = pl.multiple_of(group - start - number * ROWS, ROWS)
    bias = spread_ref[:, pl.ds(shift, group)]
    row = start + number * ROWS + lax.broadcasted_iota(jnp.int32, (ROWS, 1), 0)
    column = lax.broadcasted_iota(jnp.int32, (1, group), 1)
    same = segment_at(row, first_end, second_end) == segment_at(column, first_end, second_end)
    scores = jnp.where(same, raw * 0.125 + bias, -1e30)
    raised = jnp.exp(scores - jnp.max(scores, axis=1, keepdims=True))
    return raised * (1.0 / jnp.sum(raised, axis=1, keepdims=True))


def attend_kernel(info_ref, bias_ref, query_ref, key_ref, value_ref, out_ref, spread_ref, raw_ref, weight_ref):
    outs = []
    for half in range(2):
        mask = half_mask(query_ref.shape[0], half)
        query = jnp.where(mask, query_ref[...], jnp.bfloat16(0))
        raw_ref[half] = matmul_in(query, key_ref[...], ((1,), (1,)))
        spread_ref[half] = spread_of(bias_ref[0, half : half + 1])
    for half in range(2):
        for number in range(query_ref.shape[0] // ROWS):
            rows = pl.ds(number * ROWS, ROWS)
            weights = weights_of(info_ref, spread_ref.at[half], raw_ref[half, rows, :], number)
            weight_ref[half, rows, :] = weights.astype(jnp.bfloat16)
        outs.append(matmul_in(weight_ref[half], value_ref[...], ((1,), (0,))).astype(jnp.bfloat16))
    out_ref[...] = jnp.where(half_mask(query_ref.shape[0], 0), outs[0], outs[1])


def attend_back_kernel(
    info_ref,
    bias_ref,
    query_ref,
    key_ref,
    value_ref,
    grad_ref,
    query_grad_ref,
    key_grad_ref,
    value_grad_ref,
    sums_ref,
    spread_ref,
    diag_ref,
    weight_ref,
    score_ref,
    raw_ref,
    weight_grad_ref,
):
    group, width = key_ref.shape[0], spread_ref.shape[2]
    outs, key_grads, value_grads = [], [], []
    for half in range(2):
        mask = half_mask(query_ref.shape[0], half)
        query = jnp.where(mask, query_ref[...], jnp.bfloat16(0))
        grad = jnp.where(mask, grad_ref[...], jnp.bfloat16(0))
        raw_ref[half] = matmul_in(query, key_ref[...], ((1,), (1,)))
        weight_grad_ref[half] = matmul_in(grad, value_ref[...], ((1,), (1,)))
        spread_ref[half] = spread_of(bias_ref[0, half : half + 1])
    diag_ref[...] = jnp.zeros(diag_ref.shape, jnp.float32)
    for half in range(2):
        mask = half_mask(query_ref.shape[0], half)
        query = jnp.where(mask, query_ref[...], jnp.bfloat16(0))
        grad = jnp.where(mask, grad_ref[...], jnp.bfloat16(0))
        for number in range(query_ref.shape[0] // ROWS):
            rows = pl.ds(number * ROWS, ROWS)
            weights = weights_of(info_ref, spread_ref.at[half], raw_ref[half, rows, :], number)
            weight_ref[half, rows, :] = weights.astype(jnp.bfloat16)
            weight_grad = weight_grad_ref[half, rows, :]
            inner = jnp.sum(weights * weight_grad, axis=1, keepdims=True)
            score_grad = weights * (weight_grad - inner)
            shift = pl.multiple_of(group - info_ref[2] - number * ROWS, ROWS)
            diag_ref[half, :, pl.ds(shift, group)] += score_grad
            score_ref[half, rows, :] = (score_grad * 0.125).astype(jnp.bfloat16)
        outs.append(matmul_in(score_ref[half], key_ref[...], ((1,), (0,))).astype(jnp.bfloat16))
        key_grads.append(matmul_in(score_ref[half], query, ((0,), (0,))))
        value_grads.append(matmul_in(weight_ref[half], grad, ((0,), (0,))))
        total = diag_ref[half]
        size = ROWS // 2
        while size >= 8:
            total = total[:size] + pltpu.roll(total[size:], width - size, 1)
            size //= 2
        for size in (4, 2, 1):
            total = total + pltpu.roll(pltpu.roll(total, 8 - size, 0), width - size, 1)
        sums_ref[0, half : half + 1] = total[0:1]
    query_grad_ref[...] = jnp.where(half_mask(query_ref.shape[0], 0), outs[0], outs[1])
    key_grad_ref[...] = key_grads[0] + key_grads[1]
    value_grad_ref[...] = value_grads[0] + value_grads[1]


def attend_specs(rows, group, width, pairs):
    return [
        pl.BlockSpec(memory_space=pltpu.SMEM),
        pl.BlockSpec((1, 2, width), lambda h: (h, 0, 0)),
        pl.BlockSpec((rows, 2 * HD), lambda h: (0, h)),
        pl.BlockSpec((group, 2 * HD), lambda h: (0, h)),
        pl.BlockSpec((group, 2 * HD), lambda h: (0, pairs + h)),
    ]


def cost_of(heads, rows, group, products):
    return pl.CostEstimate(
        flops=2 * products * heads * rows * group * HD,
        bytes_accessed=4 * heads * HD * (rows + group),
        transcendentals=heads * rows * group,
    )


def attend(info, bias, query, both):
    pairs, _, width = bias.shape
    heads = 2 * pairs
    rows, group = query.shape[0], both.shape[0]
    return pl.pallas_call(
        attend_kernel,
        grid=(pairs,),
        in_specs=attend_specs(rows, group, width, pairs),
        out_specs=pl.BlockSpec((rows, 2 * HD), lambda h: (0, h)),
        out_shape=jax.ShapeDtypeStruct((rows, heads * HD), jnp.bfloat16),
        scratch_shapes=[
            pltpu.VMEM((2, ROWS, width), jnp.float32),
            pltpu.VMEM((2, rows, group), jnp.float32),
            pltpu.VMEM((2, rows, group), jnp.bfloat16),
        ],
        compiler_params=pltpu.CompilerParams(vmem_limit_bytes=VMEM),
        cost_estimate=cost_of(heads, rows, group, 2),
        name="attend",
    )(info, bias, query, both, both)


def attend_back(info, bias, query, both, grad):
    pairs, _, width = bias.shape
    heads = 2 * pairs
    rows, group = query.shape[0], both.shape[0]
    pair_block = pl.BlockSpec((rows, 2 * HD), lambda h: (0, h))
    group_block = pl.BlockSpec((group, 2 * HD), lambda h: (0, h))
    return pl.pallas_call(
        attend_back_kernel,
        grid=(pairs,),
        in_specs=attend_specs(rows, group, width, pairs) + [pair_block],
        out_specs=[pair_block, group_block, group_block, pl.BlockSpec((1, 2, width), lambda h: (h, 0, 0))],
        out_shape=[
            jax.ShapeDtypeStruct((rows, heads * HD), jnp.bfloat16),
            jax.ShapeDtypeStruct((group, heads * HD), jnp.float32),
            jax.ShapeDtypeStruct((group, heads * HD), jnp.float32),
            jax.ShapeDtypeStruct((pairs, 2, width), jnp.float32),
        ],
        scratch_shapes=[
            pltpu.VMEM((2, ROWS, width), jnp.float32),
            pltpu.VMEM((2, ROWS, width), jnp.float32),
            pltpu.VMEM((2, rows, group), jnp.bfloat16),
            pltpu.VMEM((2, rows, group), jnp.bfloat16),
            pltpu.VMEM((2, rows, group), jnp.float32),
            pltpu.VMEM((2, rows, group), jnp.float32),
        ],
        compiler_params=pltpu.CompilerParams(vmem_limit_bytes=VMEM),
        cost_estimate=cost_of(heads, rows, group, 5),
        name="attend_back",
    )(info, bias, query, both, both, grad)


LANES = 128
EDGE = 16


def reach_of(info_ref, rows, group):
    position = info_ref[2] + lax.broadcasted_iota(jnp.int32, (rows, LANES), 0)
    first_end, second_end = info_ref[0], info_ref[1]
    low = jnp.where(position >= second_end, second_end, jnp.where(position >= first_end, first_end, 0))
    high = jnp.where(position < first_end, first_end, jnp.where(position < second_end, second_end, group))
    return (low - position, high - position)


def within(reach, shift):
    if shift < 0:
        return reach[0] <= shift
    return reach[1] > shift


def fill(pad_ref, low_ref, mid_ref, high_ref):
    rows = mid_ref.shape[0]
    pad_ref[0:EDGE, :] = low_ref[...].astype(jnp.float32)
    pad_ref[EDGE : EDGE + rows, :] = mid_ref[...].astype(jnp.float32)
    pad_ref[EDGE + rows :, :] = high_ref[...].astype(jnp.float32)


def taps_of(pad_ref, depth_ref, reach, base, rows, taps, mirror):
    margin = (taps - 1) // 2
    total = jnp.zeros((rows, LANES), jnp.float32)
    for tap in range(taps):
        shift = margin - tap if mirror else tap - margin
        piece = pad_ref[EDGE + base + shift : EDGE + base + shift + rows, :] * depth_ref[tap : tap + 1, :]
        if shift:
            piece = jnp.where(within(reach, shift), piece, 0.0)
        total = total + piece
    return total


def conv_kernel(group, taps, info_ref, low_ref, mid_ref, high_ref, depth_ref, out_ref, pad_ref):
    fill(pad_ref, low_ref, mid_ref, high_ref)
    low, high = reach_of(info_ref, mid_ref.shape[0], group)
    for base in range(0, mid_ref.shape[0], STEP):
        reach = (low[base : base + STEP], high[base : base + STEP])
        out_ref[base : base + STEP, :] = taps_of(pad_ref, depth_ref, reach, base, STEP, taps, False)


STEP = 64


def conv_back_kernel(
    group,
    taps,
    info_ref,
    low_ref,
    mid_ref,
    high_ref,
    grad_low_ref,
    grad_mid_ref,
    grad_high_ref,
    depth_ref,
    out_ref,
    depth_grad_ref,
    pad_ref,
    grad_pad_ref,
    sum_ref,
):
    fill(pad_ref, low_ref, mid_ref, high_ref)
    fill(grad_pad_ref, grad_low_ref, grad_mid_ref, grad_high_ref)
    low, high = reach_of(info_ref, mid_ref.shape[0], group)
    margin = (taps - 1) // 2
    sum_ref[...] = jnp.zeros(sum_ref.shape, jnp.float32)
    for base in range(0, mid_ref.shape[0], STEP):
        reach = (low[base : base + STEP], high[base : base + STEP])
        out_ref[base : base + STEP, :] = taps_of(grad_pad_ref, depth_ref, reach, base, STEP, taps, True)
        grad = grad_pad_ref[EDGE + base : EDGE + base + STEP, :]
        for tap in range(taps):
            shift = tap - margin
            piece = pad_ref[EDGE + base + shift : EDGE + base + shift + STEP, :] * grad
            if shift:
                piece = jnp.where(within(reach, shift), piece, 0.0)
            sum_ref[8 * tap : 8 * tap + 8, :] += jnp.sum(piece.reshape(STEP // 8, 8, LANES), axis=0)
    for tap in range(taps):
        depth_grad_ref[tap : tap + 1, :] = jnp.sum(sum_ref[8 * tap : 8 * tap + 8, :], axis=0, keepdims=True)


def lane_block(rows):
    return pl.BlockSpec((rows, LANES), lambda i: (0, i))


def conv(info, low, mid, high, depth, group):
    rows, width = mid.shape
    taps = depth.shape[0]
    return pl.pallas_call(
        lambda *refs: conv_kernel(group, taps, *refs),
        grid=(width // LANES,),
        in_specs=[pl.BlockSpec(memory_space=pltpu.SMEM)]
        + [lane_block(EDGE), lane_block(rows), lane_block(EDGE), lane_block(taps)],
        out_specs=lane_block(rows),
        out_shape=jax.ShapeDtypeStruct((rows, width), jnp.float32),
        scratch_shapes=[pltpu.VMEM((rows + 2 * EDGE, LANES), jnp.float32)],
        compiler_params=pltpu.CompilerParams(vmem_limit_bytes=VMEM),
        cost_estimate=pl.CostEstimate(
            flops=2 * taps * rows * width, bytes_accessed=6 * rows * width, transcendentals=0
        ),
        name="conv",
    )(info, low, mid, high, depth)


def conv_back(info, low, mid, high, grad_low, grad_mid, grad_high, depth, group):
    rows, width = mid.shape
    taps = depth.shape[0]
    return pl.pallas_call(
        lambda *refs: conv_back_kernel(group, taps, *refs),
        grid=(width // LANES,),
        in_specs=[pl.BlockSpec(memory_space=pltpu.SMEM)]
        + [lane_block(EDGE), lane_block(rows), lane_block(EDGE)] * 2
        + [lane_block(taps)],
        out_specs=[lane_block(rows), lane_block(taps)],
        out_shape=[
            jax.ShapeDtypeStruct((rows, width), jnp.float32),
            jax.ShapeDtypeStruct((taps, width), jnp.float32),
        ],
        scratch_shapes=[
            pltpu.VMEM((rows + 2 * EDGE, LANES), jnp.float32),
            pltpu.VMEM((rows + 2 * EDGE, LANES), jnp.float32),
            pltpu.VMEM((8 * taps, LANES), jnp.float32),
        ],
        compiler_params=pltpu.CompilerParams(vmem_limit_bytes=VMEM),
        cost_estimate=pl.CostEstimate(
            flops=4 * taps * rows * width, bytes_accessed=8 * rows * width, transcendentals=0
        ),
        name="conv_back",
    )(info, low, mid, high, grad_low, grad_mid, grad_high, depth)


EPS = 1e-05
CORES = [(0, 1), (1, 0)]


def low(values):
    return values.astype(jnp.bfloat16)


def product(left_in, right_in):
    return jnp.dot(left_in, right_in, preferred_element_type=jnp.float32)


def left_product(left_in, right_in):
    return jnp.einsum("nd,nf->df", left_in, right_in, preferred_element_type=jnp.float32)


def right_product(left_in, right_in):
    return jnp.einsum("nf,df->nd", left_in, right_in, preferred_element_type=jnp.float32)


def swap(values, axis="c"):
    return lax.ppermute(values, axis, CORES)


def ordered(mine, other, place, dim=0):
    first = place == 0
    return jnp.concatenate([jnp.where(first, mine, other), jnp.where(first, other, mine)], axis=dim)


def choose(values, place, dim):
    return lax.dynamic_index_in_dim(values, place, dim, keepdims=False)


def pair_rows(values):
    return ordered(values, swap(values), lax.axis_index("c"))


def pair_sum(partial):
    place = lax.axis_index("c")
    halves = partial.reshape(2, partial.shape[0] // 2, partial.shape[1])
    received = swap(low(choose(halves, 1 - place, 0)))
    return choose(halves, place, 0) + received.astype(jnp.float32)


def gather_axis(values, axis):
    if lax.axis_size(axis) == 2:
        return ordered(values, swap(values, axis), lax.axis_index(axis))
    return lax.all_gather(values, axis, axis=0, tiled=True)


def pick(values, axis, dim):
    return choose(values, 1 - lax.axis_index(axis), dim)


def send(values, axis, dim):
    if lax.axis_size(axis) == 2:
        return swap(pick(values, axis, dim), axis)
    return lax.psum_scatter(values, axis, scatter_dimension=dim, tiled=False)


def add(values, received, axis, dim):
    if lax.axis_size(axis) != 2:
        return received
    kept = choose(values, lax.axis_index(axis), dim)
    return (kept.astype(jnp.float32) + received.astype(jnp.float32)).astype(values.dtype)


def together(*values):
    return lax.optimization_barrier(values)


def placed(parts):
    own, across, both, along = parts
    q, y = lax.axis_index("q"), lax.axis_index("y")
    result = jnp.zeros((own.shape[0], 2, 2) + own.shape[1:], own.dtype)
    for part, at_q, at_y in ((own, q, y), (across, 1 - q, y), (both, 1 - q, 1 - y), (along, q, 1 - y)):
        at = (0, at_q, at_y) + (0,) * (own.ndim - 1)
        result = lax.dynamic_update_slice(result, part[:, None, None], at)
    return result


def normalize(values):
    average = jnp.mean(values, axis=-1, keepdims=True)
    centred = values - average
    inverse = lax.rsqrt(jnp.mean(centred * centred, axis=-1, keepdims=True) + EPS)
    return (centred * inverse, inverse)


def norm_back(upstream, normed, inverse, gain):
    gain_grad = jnp.sum(upstream * normed, axis=0)
    scaled = upstream * gain
    back = inverse * (
        scaled
        - jnp.mean(scaled, axis=-1, keepdims=True)
        - normed * jnp.mean(scaled * normed, axis=-1, keepdims=True)
    )
    return (back, gain_grad)


def silu_slope(values):
    sigma = jax.nn.sigmoid(values)
    return sigma * (1.0 + values * (1.0 - sigma))


def split_normalize(values):
    width = values.shape[1]
    average = jnp.mean(values, axis=1)
    centred = values - average[:, None]
    spread = jnp.sum(centred * centred, axis=1)
    other = swap(jnp.stack([average, spread]))
    gap = average - other[0]
    whole = spread + other[1] + (0.5 * width) * gap * gap
    inverse = lax.rsqrt(whole / (2 * width) + EPS)
    middle = 0.5 * (average + other[0])
    return ((values - middle[:, None]) * inverse[:, None], inverse[:, None])


def split_norm_back(upstream, normed, inverse, gain):
    gain_grad = jnp.sum(upstream * normed, axis=0)
    scaled = upstream * gain
    sums = jnp.stack([jnp.sum(scaled, axis=1), jnp.sum(scaled * normed, axis=1)])
    means = (sums + swap(sums)) / (2 * scaled.shape[1])
    back = inverse * (scaled - means[0][:, None] - normed * means[1][:, None])
    return (back, gain_grad)


def feed_forward(hidden, gain, inner, outer):
    rows = hidden.shape[0]
    normed, inverse = normalize(hidden)
    entry = low(normed * gain)
    both = jnp.concatenate([entry, swap(entry)], axis=0)
    middle = right_product(both, inner)
    activated = low(jax.nn.silu(middle))
    partial = product(activated, outer)
    received = swap(low(partial[rows:]))
    result = hidden + 0.5 * (partial[:rows] + received.astype(jnp.float32))
    return (result, (normed, inverse, both, middle, activated))


def feed_back(upstream, gain, inner, outer, kept):
    normed, inverse, both, middle, activated = kept
    rows = upstream.shape[0]
    half = low(0.5 * upstream)
    half_both = jnp.concatenate([half, swap(half)], axis=0)
    active_grad = right_product(half_both, outer)
    middle_grad = low(active_grad * silu_slope(middle))
    partial = product(middle_grad, inner)
    received = swap(low(partial[rows:]))
    entry_grad = partial[:rows] + received.astype(jnp.float32)
    back, gain_grad = norm_back(entry_grad, normed, inverse, gain)

    eighth = middle.shape[1] // 8

    def inner_grad(first, end):
        return left_product(middle_grad[:, first * eighth : end * eighth], both)

    def outer_grad(first, end):
        return left_product(activated[:, first * eighth : end * eighth], half_both)

    return (upstream + back, gain_grad, inner_grad, outer_grad)


def bucket_hits(group):
    offset = group - jnp.arange(2 * group, dtype=jnp.int32)
    distance = jnp.abs(offset)
    level = jnp.zeros_like(distance)
    for power in range(1, 14):
        level = level + (distance >= 2**power).astype(jnp.int32)
    plain = jnp.where(distance < 16, distance, jnp.minimum(12 + level, 31))
    bucket = plain + 32 * (offset < 0).astype(jnp.int32)
    return bucket[:, None] == jnp.arange(NB, dtype=jnp.int32)[None, :]


def halos(values):
    count = lax.axis_size("y")
    forward = [(i, i + 1) for i in range(count - 1)]
    backward = [(target, source) for source, target in forward]
    return (
        lax.ppermute(values[-EDGE:], "y", forward),
        lax.ppermute(values[:EDGE], "y", backward),
    )


CHIPS = ("p", "q", "y")


def on_device(
    frames,
    cotangent,
    lengths,
    norm_gains,
    position_bias,
    attend_weight,
    merge_weight,
    glu_weight,
    depth_weight,
    point_weight,
    inner_weight,
    outer_weight,
):
    core = lax.axis_index("c")
    grid = tuple(lax.axis_size(axis) for axis in CHIPS)
    chips = grid[0] * grid[1] * grid[2]
    rows, width = frames.shape
    pair = 2 * rows
    group = pair * grid[2]
    half = width // 2
    share = attend_weight.shape[0]
    units = inner_weight.shape[2]
    taps = depth_weight.shape[0]
    heads = HEADS // 2
    f32 = jnp.float32

    small = jnp.concatenate([norm_gains.reshape(-1), position_bias, depth_weight.reshape(-1)])
    count = small.shape[0]
    small_rows = -(-2 * count // (16 * width)) * 16
    small_both = ordered(small[None], swap(small[None]), core).reshape(-1)
    small_both = jnp.pad(small_both, (0, small_rows * width - 2 * count)).reshape(small_rows, width)

    inner_pack = inner_weight[0].T
    outer_pack = jnp.concatenate([outer_weight[0], small_both], axis=0)
    pack_two = jnp.concatenate([inner_weight[1].T, outer_weight[1]], axis=0)
    attend_weight, glu_weight = together(attend_weight, glu_weight, outer_pack)[:2]

    def own_columns(weight, shape, dim):
        parts = weight.reshape((share,) + shape)
        mine = choose(parts, core, dim).reshape(share, -1)
        other = swap(choose(parts, 1 - core, dim).reshape(share, -1))
        return ordered(mine, other, core)

    attend_part = own_columns(attend_weight, (3, 2, half), 2)
    glu_part = own_columns(glu_weight, (2, chips, 2, share), 3)
    mixed_pack = jnp.concatenate(
        [attend_part.reshape(-1, width), glu_part, merge_weight, point_weight], axis=0
    )

    square = grid[1] == 2 and grid[2] == 2
    marks = [0]
    for size in (3 * share, 2 * share, share, share):
        marks.append(marks[-1] + size)

    def gather_p(values):
        return lax.all_gather(values, "p", axis=0)

    def in_halves(*parts):
        parts = [part.reshape(grid[0], units, width) for part in parts]
        near = [part[:, : units // 2].reshape(-1, width) for part in parts]
        far = [part[:, units // 2 :].reshape(-1, width) for part in parts]
        return jnp.concatenate(near + far, axis=0)

    if square:
        inner = gather_p(inner_pack)
        two_x, two_y = together(swap(pack_two, "q"), swap(pack_two, "y"))
        pack_two = jnp.stack([pack_two, two_x, swap(two_x, "y"), two_y])
        whole_one = gather_p(outer_pack)
        inner, pack_two = together(inner.reshape(-1, width), pack_two)
        inner_x, inner_y = together(swap(inner, "q"), swap(inner, "y"))
        mixed_pack, inner_x, inner_y = together(mixed_pack, inner_x, inner_y)
        mixed = gather_p(mixed_pack)
        inner_xy = swap(inner_y, "q")
        outer = whole_one[:, :units].reshape(-1, width)
        tiny = whole_one[:, units:]
        outer, tiny = together(outer, tiny)
        across = [(0, 3), (3, 0), (1, 2), (2, 1)]
        tiny_xy = lax.ppermute(tiny, ("q", "y"), across)
        outer_x, outer_y, tiny_x, tiny_y, tiny_xy = together(
            swap(outer, "q"), swap(outer, "y"), swap(tiny, "q"), swap(tiny, "y"), tiny_xy
        )
        small_full = placed((tiny, tiny_x, tiny_xy, tiny_y)).reshape(chips, -1)
        outer_xy = swap(outer_x, "y")
        whole_two = gather_p(pack_two).reshape(chips, 2 * units, width)
        attend_part = mixed[:, : marks[1]].reshape(grid[0], 2 * share, 3 * half)
        rest_part = mixed[:, marks[1] :]
        attend_part, rest_part = together(attend_part, rest_part)
        attend_x = swap(attend_part, "q")
        inner_xy, outer_xy, attend_x, attend_part, rest_part = together(
            inner_xy, outer_xy, attend_x, attend_part, rest_part
        )
        inner_one = in_halves(inner, inner_x, inner_xy, inner_y)
        outer_one = in_halves(outer, outer_x, outer_xy, outer_y)
        attend_y, rest_x = swap(attend_part, "y"), swap(rest_part, "q")
    else:
        inner_one = lax.all_gather(inner_pack, CHIPS, axis=0, tiled=True)
        whole_one = lax.all_gather(outer_pack, CHIPS, axis=0)
        mixed = lax.all_gather(mixed_pack, CHIPS, axis=0)
        whole_two = lax.all_gather(pack_two, CHIPS, axis=0)
        outer_one = whole_one[:, :units].reshape(chips * units, width)
        small_full = whole_one[:, units:].reshape(chips, -1)

    small_full = small_full[:, : 2 * count].reshape(chips, 2, count)
    gain_size = norm_gains.size
    gains = small_full[..., :gain_size].reshape(chips, 2, 6, -1).astype(f32)
    gain_table = gains.transpose(2, 0, 1, 3).reshape(6, width)
    gain_mid = choose(gains[:, :, 3], core, 1).reshape(half)
    bias_table = small_full[..., gain_size : gain_size + position_bias.size].reshape(NB, 2, heads)
    bias_table = choose(bias_table, core, 1)
    depth = choose(small_full[..., gain_size + position_bias.size :], core, 1)
    depth = depth.reshape(chips, taps, share).transpose(1, 0, 2).reshape(taps, half).astype(f32)

    start = lax.axis_index("y") * pair
    info = jnp.stack([lengths[0, 0], lengths[0, 0] + lengths[0, 1], start.astype(jnp.int32)])
    hits = bucket_hits(group)
    bias = jnp.einsum("bh,wb->hw", bias_table, hits.astype(jnp.bfloat16), preferred_element_type=f32)
    bias = bias.reshape(heads // 2, 2, -1)

    hidden = frames.astype(f32)
    first, first_kept = feed_forward(hidden, gain_table[0], inner_one, outer_one)
    if square:
        first, attend_y, rest_part = together(first, attend_y, rest_part)
        rest_y = swap(rest_part, "y")
        attend_full = placed((attend_part, attend_x, swap(attend_y, "q"), attend_y))
    else:
        attend_full = mixed[:, : marks[1]]
    attend_full = attend_full.reshape(width, 3 * half)
    normed_att, inverse_att = normalize(first)
    att_entry = pair_rows(low(normed_att * gain_table[1]))
    triple = low(product(att_entry, attend_full))
    query = triple[:, :half]
    key_value = triple[:, half:]
    if square:
        key_value, rest_x, rest_y = together(key_value, rest_x, rest_y)
        rest_xy = swap(rest_y, "q")
    both = gather_axis(key_value, "y")
    attended = attend(info, bias, query, both)
    if square:
        attended, rest_xy = together(attended, rest_xy)
        rest = placed((rest_part, rest_x, rest_xy, rest_y)).reshape(chips, -1, width)
    else:
        rest = mixed[:, marks[1] :]
    marks = [mark - marks[1] for mark in marks]
    glu_full = rest[:, : marks[2]].reshape(width, width)
    merge_half = rest[:, marks[2] : marks[3]]
    point_full = rest[:, marks[3] : marks[4]].reshape(half, width)
    sides = merge_half.reshape(2, chips // 2, share, width)
    merge_full = ordered(
        choose(sides, core, 0)[:, None], swap(choose(sides, 1 - core, 0))[:, None], core, 1
    ).reshape(half, width)
    second = first + pair_sum(product(attended, merge_full))
    normed_conv, inverse_conv = normalize(second)
    conv_entry = pair_rows(low(normed_conv * gain_table[2]))
    gate_up = product(conv_entry, glu_full)
    gate_sig = jax.nn.sigmoid(gate_up[:, half:])
    glu_rows = low(gate_up[:, :half] * gate_sig)
    glu_low, glu_high = halos(glu_rows)
    mixed_rows = conv(info, glu_low, glu_rows, glu_high, depth, group)
    normed_mid, inverse_mid = split_normalize(mixed_rows)
    activated = normed_mid * gain_mid
    swish = low(jax.nn.silu(activated))
    third = second + pair_sum(product(swish, point_full))
    inner_two = whole_two[:, :units].reshape(chips * units, width)
    outer_two = whole_two[:, units:].reshape(chips * units, width)
    fourth, fourth_kept = feed_forward(third, gain_table[4], inner_two, outer_two)
    normed_last, inverse_last = normalize(fourth)
    result = low(normed_last * gain_table[5])

    def by_chip(values):
        return values.reshape(grid + (values.shape[0] // chips, values.shape[1]))

    def last_sum(values):
        return lax.psum_scatter(values, "p", scatter_dimension=0, tiled=False)

    size = grid[0] * units // 2

    def early_sum(grad):
        shape = (grid[0], 4) if square else grid
        return last_sum(low(grad).reshape(shape + (units, width)))

    grad_fourth, gain_five = norm_back(
        cotangent.astype(f32), normed_last, inverse_last, gain_table[5]
    )
    grad_third, gain_four, inner_two_grad, outer_two_grad = feed_back(
        grad_fourth, gain_table[4], inner_two, outer_two, fourth_kept
    )

    outer_two_sum = early_sum(outer_two_grad(0, 8))

    conv_out_grad = pair_rows(low(grad_third))
    swish_grad = right_product(conv_out_grad, point_full)
    act_grad = swish_grad * silu_slope(activated)
    mixed_grad, gain_three = split_norm_back(act_grad, normed_mid, inverse_mid, gain_mid)
    mixed_low = low(mixed_grad)
    grad_low, grad_high = halos(mixed_low)
    if square:
        inner_two = low(inner_two_grad(0, 8)).reshape(grid[0], 4, units, width)
        inner_two_a, mixed_low = together(inner_two[:, 1:3], mixed_low)
        inner_two_a = swap(inner_two_a, "q")
    glu_back, depth_grad = conv_back(
        info, glu_low, glu_rows, glu_high, grad_low, mixed_low, grad_high, depth, group
    )
    value_part = gate_up[:, :half]
    gate_grad = low(
        jnp.concatenate(
            [glu_back * gate_sig, glu_back * value_part * gate_sig * (1.0 - gate_sig)], axis=1
        )
    )
    conv_entry_grad = pair_sum(right_product(gate_grad, glu_full))
    point_grad = by_chip(low(left_product(swish, conv_out_grad)))
    glu_grad = by_chip(low(left_product(conv_entry, gate_grad)))
    back_conv, gain_two = norm_back(conv_entry_grad, normed_conv, inverse_conv, gain_table[2])
    grad_second = grad_third + back_conv

    att_out_grad = pair_rows(low(grad_second))
    glu_a = send(glu_grad, "y", 2)
    point_a = send(point_grad, "y", 2)
    attended_grad = low(right_product(att_out_grad, merge_full))
    query_grad, key_grad, value_grad, table_sums = attend_back(info, bias, query, both, attended_grad)
    query_grad, key_grad, value_grad, glu_a, point_a = together(
        query_grad, key_grad, value_grad, glu_a, point_a
    )
    att_out_grad, query_grad = together(att_out_grad, query_grad)
    merge_grad = low(left_product(attended, att_out_grad)).reshape(chips // 2, 2, share, width)
    merge_grad = ordered(
        choose(merge_grad, core, 1)[None], swap(choose(merge_grad, 1 - core, 1))[None], core
    )
    merge_grad = by_chip(merge_grad.reshape(chips * share, width))
    glu_half = add(glu_grad, glu_a, "y", 2)
    point_half = add(point_grad, point_a, "y", 2)
    both_grad = jnp.concatenate([key_grad, value_grad], axis=1).reshape(grid[2], pair, width)
    if grid[2] == 2:
        place = lax.axis_index("y")
        both_received = swap(low(choose(both_grad, 1 - place, 0)), "y")
        both_grad = low(choose(both_grad, place, 0) + both_received.astype(f32))
    else:
        both_received = low(lax.psum_scatter(both_grad, "y", scatter_dimension=0, tiled=False))
        both_grad = both_received
    if square:
        glu_b, point_b, merge_a, outer_two_a, inner_two_a, both_grad = together(
            pick(glu_half, "q", 1),
            pick(point_half, "q", 1),
            pick(merge_grad, "q", 1),
            outer_two_sum[1:3],
            inner_two_a,
            both_grad,
        )
        inner_two_b = low(inner_two[:, 3].astype(f32) + inner_two_a[:, 1].astype(f32))
        inner_two_b = swap(inner_two_b, "y")
        glu_b, point_b, merge_a, outer_two_a = [
            swap(part, "q") for part in (glu_b, point_b, merge_a, outer_two_a)
        ]
    else:
        glu_b, point_b, merge_a = [send(part, "q", 1) for part in (glu_half, point_half, merge_grad)]
        inner_two_sum = early_sum(inner_two_grad(0, 8))
    triple_grad = jnp.concatenate([query_grad, both_grad], axis=1)
    attend_grad = low(left_product(att_entry, triple_grad))
    attend_grad = attend_grad.reshape(grid + (2 * share, 3 * half))
    att_entry_grad = pair_sum(right_product(triple_grad, attend_full))
    back_att, gain_one = norm_back(att_entry_grad, normed_att, inverse_att, gain_table[1])
    grad_first = grad_second + back_att
    attend_sum = last_sum(attend_grad)
    if square:
        inner_two_sum = inner_two[:, 0].astype(f32) + inner_two_a[:, 0].astype(f32)
    input_grad, gain_zero, inner_one_grad, outer_one_grad = feed_back(
        grad_first, gain_table[0], inner_one, outer_one, first_kept
    )
    if square:
        near_o, near_i, glu_b, point_b, merge_a, inner_two_b = together(
            low(outer_one_grad(1, 3)),
            low(inner_one_grad(2, 4)),
            glu_b,
            point_b,
            merge_a,
            inner_two_b,
        )
        near_o, near_i = swap(near_o, "q"), swap(near_i, "y")
        inner_two_sum = low(inner_two_sum + inner_two_b.astype(f32))
    merge_half = add(merge_grad, merge_a, "q", 1)
    merge_b = send(merge_half, "y", 1)
    mixed_sum = jnp.concatenate(
        [
            add(glu_half, glu_b, "q", 1),
            add(point_half, point_b, "q", 1),
            add(merge_half, merge_b, "y", 1),
        ]
        + ([inner_two_sum] if square else []),
        axis=1,
    )
    if square:
        near_o, near_i, far_o, far_i, mixed_sum, outer_two_a, attend_sum = together(
            near_o,
            near_i,
            low(outer_one_grad(5, 7)),
            low(inner_one_grad(6, 8)),
            mixed_sum,
            outer_two_a,
            attend_sum,
        )
        far_o, far_i = swap(far_o, "q"), swap(far_i, "y")
        mixed_sum = last_sum(mixed_sum)

        def second(first, got_o, got_i):
            return together(
                low(outer_one_grad(first + 3, first + 4) + got_o[size:].astype(f32)),
                low(inner_one_grad(first + 1, first + 2) + got_i[:size].astype(f32)),
            )

        def third(first, got_o, got_i, end_o, end_i):
            sum_o = outer_one_grad(first, first + 1) + got_o[:size].astype(f32)
            sum_i = inner_one_grad(first, first + 1) + got_i[size:].astype(f32)
            sums = [low(sum_i + end_i.astype(f32)), low(sum_o + end_o.astype(f32))]
            return [part.reshape(grid[0], units // 2, width) for part in sums]

        near = second(0, near_o, near_i)
        *near, far_o, far_i = together(swap(near[0], "y"), swap(near[1], "q"), far_o, far_i)
        near = jnp.concatenate(third(0, near_o, near_i, *near), axis=1)
        near, mixed_sum = together(near, mixed_sum)
        near_sum = last_sum(near)
        far_o, attend_sum = together(far_o, attend_sum)
        far = second(4, far_o, far_i)
        *far, table_sums, depth_grad, gain_one, gain_two, gain_three, gain_four, gain_five = together(
            *far, table_sums, depth_grad, gain_one, gain_two, gain_three, gain_four, gain_five
        )
        far = together(swap(far[0], "y"), swap(far[1], "q"))
        far = third(4, far_o, far_i, *far)
        outer_two_b = swap(low(outer_two_sum[3].astype(f32) + outer_two_a[1].astype(f32)), "y")
        outer_sum_two = outer_two_sum[0].astype(f32) + outer_two_a[0].astype(f32)
        outer_sum_two = low(outer_sum_two + outer_two_b.astype(f32))
        inner_sum_two = mixed_sum[4 * share :]
    else:
        mixed_sum = last_sum(mixed_sum)
        inner_sum_one = by_chip(low(inner_one_grad(0, 8)))
        outer_sum_one = by_chip(low(outer_one_grad(0, 8)))
        inner_sum_one = send(send(inner_sum_one, "y", 2), "q", 1)
        outer_sum_one = send(send(outer_sum_one, "y", 2), "q", 1)
        inner_sum_two = send(send(inner_two_sum, "y", 1), "q", 0)
        outer_sum_two = send(send(outer_two_sum, "y", 1), "q", 0)
    attend_half = add(attend_sum, send(attend_sum, "q", 0), "q", 0)
    attend_sum = add(attend_half, send(attend_half, "y", 0), "y", 0)

    table_grad = jnp.einsum(
        "hw,wb->bh", table_sums.reshape(heads, -1), hits.astype(f32), precision=lax.Precision.HIGHEST
    )

    def of_core(values, dim):
        empty = jnp.zeros_like(values)
        return jnp.stack(
            [jnp.where(core == 0, values, empty), jnp.where(core == 1, values, empty)], axis=dim
        )

    gain_three = of_core(gain_three.reshape(chips, share), 1).reshape(width)
    gain_grads = jnp.stack([gain_zero, gain_one, gain_two, gain_three, gain_four, gain_five])
    small_grads = jnp.concatenate(
        [
            gain_grads.reshape(6, chips, 2, share).transpose(1, 2, 0, 3).reshape(chips, 2, -1),
            of_core(table_grad, 1).reshape(chips, 2, -1),
            of_core(depth_grad.reshape(taps, chips, share).transpose(1, 0, 2), 1).reshape(
                chips, 2, -1
            ),
        ],
        axis=2,
    )
    small_sum = choose(small_grads, core, 1) + swap(choose(small_grads, 1 - core, 1))
    small_sum = small_sum.reshape(grid + (count,))
    if square:
        at_q, at_y = lax.axis_index("q"), lax.axis_index("y")
        here = [choose(small_sum, at_q, 1), choose(small_sum, 1 - at_q, 1)]
        across = [(0, 3), (3, 0), (1, 2), (2, 1)]
        small_sum = (
            choose(here[0], at_y, 1)
            + swap(choose(here[0], 1 - at_y, 1), "y")
            + swap(choose(here[1], at_y, 1), "q")
            + lax.ppermute(choose(here[1], 1 - at_y, 1), ("q", "y"), across)
        )
    else:
        small_sum = add(small_sum, send(small_sum, "y", 2), "y", 2)
        small_sum = add(small_sum, send(small_sum, "q", 1), "q", 1)
    one_rows = -(-count // (16 * width)) * 16
    small_sum = jnp.pad(low(small_sum), ((0, 0), (0, one_rows * width - count)))
    small_sum = small_sum.reshape(grid[0], one_rows, width)

    if square:
        far_sum, near_sum = together(jnp.concatenate(far + [small_sum], axis=1), near_sum)
        far_sum = last_sum(far_sum)
        half_units = units // 2
        inner_sum_one = jnp.concatenate([near_sum[:half_units], far_sum[:half_units]])
        outer_sum_one = jnp.concatenate([near_sum[half_units:], far_sum[half_units:units]])
        small_sum = far_sum[units:]
    else:
        one_sum = last_sum(jnp.concatenate([inner_sum_one, outer_sum_one, small_sum], axis=1))
        inner_sum_one, outer_sum_one = one_sum[:units], one_sum[units : 2 * units]
        small_sum = one_sum[2 * units :]

    def whole_columns(values, shape, dim):
        parts = values.reshape(2, share, -1)
        mine = choose(parts, core, 0)
        other = swap(choose(parts, 1 - core, 0))
        joined = ordered(
            jnp.expand_dims(mine.reshape((share,) + shape), dim),
            jnp.expand_dims(other.reshape((share,) + shape), dim),
            core,
            dim,
        )
        return joined.reshape(share, -1).astype(f32)

    attend_out = whole_columns(attend_sum, (3, half), 2)
    glu_out = whole_columns(mixed_sum[: 2 * share], (2, chips, share), 3)
    point_out = mixed_sum[2 * share : 3 * share].astype(f32)
    merge_out = mixed_sum[3 * share : 4 * share].astype(f32)
    inner_out = jnp.stack([inner_sum_one.T, inner_sum_two.T]).astype(f32)
    outer_out = jnp.stack([outer_sum_one, outer_sum_two]).astype(f32)
    small_out = small_sum.reshape(-1)[:count].astype(f32)
    gains_out = small_out[:gain_size].reshape(norm_gains.shape)
    position_out = small_out[gain_size : gain_size + position_bias.size]
    depth_out = small_out[gain_size + position_bias.size :].reshape(taps, share)
    return (
        result,
        input_grad,
        gains_out,
        position_out,
        attend_out,
        merge_out,
        glu_out,
        depth_out,
        point_out,
        inner_out,
        outer_out,
    )


def solution(mesh):
    across, along = mesh.shape["dp"], mesh.shape["head"]
    fine = Mesh(mesh.devices.reshape(4, across // 4, along // 2, 2), ("p", "q", "y", "c"))
    every = ("p", "q", "y", "c")
    in_specs = (
        P(every, None),
        P(every, None),
        P(("p", "q"), None),
        P(None, every),
        P(every),
        P(every, None),
        P(every, None),
        P(every, None),
        P(None, every),
        P(every, None),
        P(None, None, every),
        P(None, every, None),
    )
    out_specs = (
        P(every, None),
        P(every, None),
        P(None, every),
        P(every),
        P(every, None),
        P(every, None),
        P(every, None),
        P(None, every),
        P(every, None),
        P(None, None, every),
        P(None, every, None),
    )
    return jax.shard_map(
        on_device, mesh=fine, in_specs=in_specs, out_specs=out_specs, check_vma=False
    )
```

```python
import jax
import jax.numpy as jnp
from jax import lax
from jax.experimental import pallas as pl
from jax.experimental.pallas import tpu as pltpu
from jax.sharding import Mesh
from jax.sharding import PartitionSpec as P

HEADS = 16
HD = 64
NB = 64
ROWS = 128
VMEM = 50 * 1024 * 1024


def matmul_in(left, right, dims):
    return lax.dot_general(left, right, (dims, ((), ())), preferred_element_type=jnp.float32)


def spread_of(bias):
    row = jnp.broadcast_to(bias, (ROWS, bias.shape[1]))
    return pltpu.roll(row, 0, 1, stride=1, stride_axis=0)


def half_mask(rows, half):
    lane = lax.broadcasted_iota(jnp.int32, (rows, 2 * HD), 1)
    return lane < HD if half == 0 else lane >= HD


def segment_at(position, first_end, second_end):
    return (position >= first_end).astype(jnp.int32) + (position >= second_end).astype(jnp.int32)


def weights_of(info_ref, spread_ref, raw, number):
    group = raw.shape[1]
    first_end, second_end, start = info_ref[0], info_ref[1], info_ref[2]
    shift = pl.multiple_of(group - start - number * ROWS, ROWS)
    bias = spread_ref[:, pl.ds(shift, group)]
    row = start + number * ROWS + lax.broadcasted_iota(jnp.int32, (ROWS, 1), 0)
    column = lax.broadcasted_iota(jnp.int32, (1, group), 1)
    same = segment_at(row, first_end, second_end) == segment_at(column, first_end, second_end)
    scores = jnp.where(same, raw * 0.125 + bias, -1e30)
    raised = jnp.exp(scores - jnp.max(scores, axis=1, keepdims=True))
    return raised * (1.0 / jnp.sum(raised, axis=1, keepdims=True))


def attend_kernel(info_ref, bias_ref, query_ref, key_ref, value_ref, out_ref, spread_ref, raw_ref, weight_ref):
    outs = []
    for half in range(2):
        mask = half_mask(query_ref.shape[0], half)
        query = jnp.where(mask, query_ref[...], jnp.bfloat16(0))
        raw_ref[half] = matmul_in(query, key_ref[...], ((1,), (1,)))
        spread_ref[half] = spread_of(bias_ref[0, half : half + 1])
    for half in range(2):
        for number in range(query_ref.shape[0] // ROWS):
            rows = pl.ds(number * ROWS, ROWS)
            weights = weights_of(info_ref, spread_ref.at[half], raw_ref[half, rows, :], number)
            weight_ref[half, rows, :] = weights.astype(jnp.bfloat16)
        outs.append(matmul_in(weight_ref[half], value_ref[...], ((1,), (0,))).astype(jnp.bfloat16))
    out_ref[...] = jnp.where(half_mask(query_ref.shape[0], 0), outs[0], outs[1])


def attend_back_kernel(
    info_ref,
    bias_ref,
    query_ref,
    key_ref,
    value_ref,
    grad_ref,
    query_grad_ref,
    key_grad_ref,
    value_grad_ref,
    sums_ref,
    spread_ref,
    diag_ref,
    weight_ref,
    score_ref,
    raw_ref,
    weight_grad_ref,
):
    group, width = key_ref.shape[0], spread_ref.shape[2]
    outs, key_grads, value_grads = [], [], []
    for half in range(2):
        mask = half_mask(query_ref.shape[0], half)
        query = jnp.where(mask, query_ref[...], jnp.bfloat16(0))
        grad = jnp.where(mask, grad_ref[...], jnp.bfloat16(0))
        raw_ref[half] = matmul_in(query, key_ref[...], ((1,), (1,)))
        weight_grad_ref[half] = matmul_in(grad, value_ref[...], ((1,), (1,)))
        spread_ref[half] = spread_of(bias_ref[0, half : half + 1])
    diag_ref[...] = jnp.zeros(diag_ref.shape, jnp.float32)
    for half in range(2):
        mask = half_mask(query_ref.shape[0], half)
        query = jnp.where(mask, query_ref[...], jnp.bfloat16(0))
        grad = jnp.where(mask, grad_ref[...], jnp.bfloat16(0))
        for number in range(query_ref.shape[0] // ROWS):
            rows = pl.ds(number * ROWS, ROWS)
            weights = weights_of(info_ref, spread_ref.at[half], raw_ref[half, rows, :], number)
            weight_ref[half, rows, :] = weights.astype(jnp.bfloat16)
            weight_grad = weight_grad_ref[half, rows, :]
            inner = jnp.sum(weights * weight_grad, axis=1, keepdims=True)
            score_grad = weights * (weight_grad - inner)
            shift = pl.multiple_of(group - info_ref[2] - number * ROWS, ROWS)
            diag_ref[half, :, pl.ds(shift, group)] += score_grad
            score_ref[half, rows, :] = (score_grad * 0.125).astype(jnp.bfloat16)
        outs.append(matmul_in(score_ref[half], key_ref[...], ((1,), (0,))).astype(jnp.bfloat16))
        key_grads.append(matmul_in(score_ref[half], query, ((0,), (0,))))
        value_grads.append(matmul_in(weight_ref[half], grad, ((0,), (0,))))
        total = diag_ref[half]
        size = ROWS // 2
        while size >= 8:
            total = total[:size] + pltpu.roll(total[size:], width - size, 1)
            size //= 2
        for size in (4, 2, 1):
            total = total + pltpu.roll(pltpu.roll(total, 8 - size, 0), width - size, 1)
        sums_ref[0, half : half + 1] = total[0:1]
    query_grad_ref[...] = jnp.where(half_mask(query_ref.shape[0], 0), outs[0], outs[1])
    key_grad_ref[...] = key_grads[0] + key_grads[1]
    value_grad_ref[...] = value_grads[0] + value_grads[1]


def attend_specs(rows, group, width, pairs):
    return [
        pl.BlockSpec(memory_space=pltpu.SMEM),
        pl.BlockSpec((1, 2, width), lambda h: (h, 0, 0)),
        pl.BlockSpec((rows, 2 * HD), lambda h: (0, h)),
        pl.BlockSpec((group, 2 * HD), lambda h: (0, h)),
        pl.BlockSpec((group, 2 * HD), lambda h: (0, pairs + h)),
    ]


def cost_of(heads, rows, group, products):
    return pl.CostEstimate(
        flops=2 * products * heads * rows * group * HD,
        bytes_accessed=4 * heads * HD * (rows + group),
        transcendentals=heads * rows * group,
    )


def attend(info, bias, query, both):
    pairs, _, width = bias.shape
    heads = 2 * pairs
    rows, group = query.shape[0], both.shape[0]
    return pl.pallas_call(
        attend_kernel,
        grid=(pairs,),
        in_specs=attend_specs(rows, group, width, pairs),
        out_specs=pl.BlockSpec((rows, 2 * HD), lambda h: (0, h)),
        out_shape=jax.ShapeDtypeStruct((rows, heads * HD), jnp.bfloat16),
        scratch_shapes=[
            pltpu.VMEM((2, ROWS, width), jnp.float32),
            pltpu.VMEM((2, rows, group), jnp.float32),
            pltpu.VMEM((2, rows, group), jnp.bfloat16),
        ],
        compiler_params=pltpu.CompilerParams(vmem_limit_bytes=VMEM),
        cost_estimate=cost_of(heads, rows, group, 2),
        name="attend",
    )(info, bias, query, both, both)


def attend_back(info, bias, query, both, grad):
    pairs, _, width = bias.shape
    heads = 2 * pairs
    rows, group = query.shape[0], both.shape[0]
    pair_block = pl.BlockSpec((rows, 2 * HD), lambda h: (0, h))
    group_block = pl.BlockSpec((group, 2 * HD), lambda h: (0, h))
    return pl.pallas_call(
        attend_back_kernel,
        grid=(pairs,),
        in_specs=attend_specs(rows, group, width, pairs) + [pair_block],
        out_specs=[pair_block, group_block, group_block, pl.BlockSpec((1, 2, width), lambda h: (h, 0, 0))],
        out_shape=[
            jax.ShapeDtypeStruct((rows, heads * HD), jnp.bfloat16),
            jax.ShapeDtypeStruct((group, heads * HD), jnp.float32),
            jax.ShapeDtypeStruct((group, heads * HD), jnp.float32),
            jax.ShapeDtypeStruct((pairs, 2, width), jnp.float32),
        ],
        scratch_shapes=[
            pltpu.VMEM((2, ROWS, width), jnp.float32),
            pltpu.VMEM((2, ROWS, width), jnp.float32),
            pltpu.VMEM((2, rows, group), jnp.bfloat16),
            pltpu.VMEM((2, rows, group), jnp.bfloat16),
            pltpu.VMEM((2, rows, group), jnp.float32),
            pltpu.VMEM((2, rows, group), jnp.float32),
        ],
        compiler_params=pltpu.CompilerParams(vmem_limit_bytes=VMEM),
        cost_estimate=cost_of(heads, rows, group, 5),
        name="attend_back",
    )(info, bias, query, both, both, grad)


LANES = 128
EDGE = 16


def reach_of(info_ref, rows, group):
    position = info_ref[2] + lax.broadcasted_iota(jnp.int32, (rows, LANES), 0)
    first_end, second_end = info_ref[0], info_ref[1]
    low = jnp.where(position >= second_end, second_end, jnp.where(position >= first_end, first_end, 0))
    high = jnp.where(position < first_end, first_end, jnp.where(position < second_end, second_end, group))
    return (low - position, high - position)


def within(reach, shift):
    if shift < 0:
        return reach[0] <= shift
    return reach[1] > shift


def fill(pad_ref, low_ref, mid_ref, high_ref):
    rows = mid_ref.shape[0]
    pad_ref[0:EDGE, :] = low_ref[...].astype(jnp.float32)
    pad_ref[EDGE : EDGE + rows, :] = mid_ref[...].astype(jnp.float32)
    pad_ref[EDGE + rows :, :] = high_ref[...].astype(jnp.float32)


def taps_of(pad_ref, depth_ref, reach, base, rows, taps, mirror):
    margin = (taps - 1) // 2
    total = jnp.zeros((rows, LANES), jnp.float32)
    for tap in range(taps):
        shift = margin - tap if mirror else tap - margin
        piece = pad_ref[EDGE + base + shift : EDGE + base + shift + rows, :] * depth_ref[tap : tap + 1, :]
        if shift:
            piece = jnp.where(within(reach, shift), piece, 0.0)
        total = total + piece
    return total


def conv_kernel(group, taps, info_ref, low_ref, mid_ref, high_ref, depth_ref, out_ref, pad_ref):
    fill(pad_ref, low_ref, mid_ref, high_ref)
    low, high = reach_of(info_ref, mid_ref.shape[0], group)
    for base in range(0, mid_ref.shape[0], STEP):
        reach = (low[base : base + STEP], high[base : base + STEP])
        out_ref[base : base + STEP, :] = taps_of(pad_ref, depth_ref, reach, base, STEP, taps, False)


STEP = 64


def conv_back_kernel(
    group,
    taps,
    info_ref,
    low_ref,
    mid_ref,
    high_ref,
    grad_low_ref,
    grad_mid_ref,
    grad_high_ref,
    depth_ref,
    out_ref,
    depth_grad_ref,
    pad_ref,
    grad_pad_ref,
    sum_ref,
):
    fill(pad_ref, low_ref, mid_ref, high_ref)
    fill(grad_pad_ref, grad_low_ref, grad_mid_ref, grad_high_ref)
    low, high = reach_of(info_ref, mid_ref.shape[0], group)
    margin = (taps - 1) // 2
    sum_ref[...] = jnp.zeros(sum_ref.shape, jnp.float32)
    for base in range(0, mid_ref.shape[0], STEP):
        reach = (low[base : base + STEP], high[base : base + STEP])
        out_ref[base : base + STEP, :] = taps_of(grad_pad_ref, depth_ref, reach, base, STEP, taps, True)
        grad = grad_pad_ref[EDGE + base : EDGE + base + STEP, :]
        for tap in range(taps):
            shift = tap - margin
            piece = pad_ref[EDGE + base + shift : EDGE + base + shift + STEP, :] * grad
            if shift:
                piece = jnp.where(within(reach, shift), piece, 0.0)
            sum_ref[8 * tap : 8 * tap + 8, :] += jnp.sum(piece.reshape(STEP // 8, 8, LANES), axis=0)
    for tap in range(taps):
        depth_grad_ref[tap : tap + 1, :] = jnp.sum(sum_ref[8 * tap : 8 * tap + 8, :], axis=0, keepdims=True)


def lane_block(rows):
    return pl.BlockSpec((rows, LANES), lambda i: (0, i))


def conv(info, low, mid, high, depth, group):
    rows, width = mid.shape
    taps = depth.shape[0]
    return pl.pallas_call(
        lambda *refs: conv_kernel(group, taps, *refs),
        grid=(width // LANES,),
        in_specs=[pl.BlockSpec(memory_space=pltpu.SMEM)]
        + [lane_block(EDGE), lane_block(rows), lane_block(EDGE), lane_block(taps)],
        out_specs=lane_block(rows),
        out_shape=jax.ShapeDtypeStruct((rows, width), jnp.float32),
        scratch_shapes=[pltpu.VMEM((rows + 2 * EDGE, LANES), jnp.float32)],
        compiler_params=pltpu.CompilerParams(vmem_limit_bytes=VMEM),
        cost_estimate=pl.CostEstimate(
            flops=2 * taps * rows * width, bytes_accessed=6 * rows * width, transcendentals=0
        ),
        name="conv",
    )(info, low, mid, high, depth)


def conv_back(info, low, mid, high, grad_low, grad_mid, grad_high, depth, group):
    rows, width = mid.shape
    taps = depth.shape[0]
    return pl.pallas_call(
        lambda *refs: conv_back_kernel(group, taps, *refs),
        grid=(width // LANES,),
        in_specs=[pl.BlockSpec(memory_space=pltpu.SMEM)]
        + [lane_block(EDGE), lane_block(rows), lane_block(EDGE)] * 2
        + [lane_block(taps)],
        out_specs=[lane_block(rows), lane_block(taps)],
        out_shape=[
            jax.ShapeDtypeStruct((rows, width), jnp.float32),
            jax.ShapeDtypeStruct((taps, width), jnp.float32),
        ],
        scratch_shapes=[
            pltpu.VMEM((rows + 2 * EDGE, LANES), jnp.float32),
            pltpu.VMEM((rows + 2 * EDGE, LANES), jnp.float32),
            pltpu.VMEM((8 * taps, LANES), jnp.float32),
        ],
        compiler_params=pltpu.CompilerParams(vmem_limit_bytes=VMEM),
        cost_estimate=pl.CostEstimate(
            flops=4 * taps * rows * width, bytes_accessed=8 * rows * width, transcendentals=0
        ),
        name="conv_back",
    )(info, low, mid, high, grad_low, grad_mid, grad_high, depth)


EPS = 1e-05
CORES = [(0, 1), (1, 0)]


def low(values):
    return values.astype(jnp.bfloat16)


def product(left_in, right_in):
    return jnp.dot(left_in, right_in, preferred_element_type=jnp.float32)


def left_product(left_in, right_in):
    return jnp.einsum("nd,nf->df", left_in, right_in, preferred_element_type=jnp.float32)


def right_product(left_in, right_in):
    return jnp.einsum("nf,df->nd", left_in, right_in, preferred_element_type=jnp.float32)


def swap(values, axis="c"):
    return lax.ppermute(values, axis, CORES)


def ordered(mine, other, place, dim=0):
    first = place == 0
    return jnp.concatenate([jnp.where(first, mine, other), jnp.where(first, other, mine)], axis=dim)


def choose(values, place, dim):
    return lax.dynamic_index_in_dim(values, place, dim, keepdims=False)


def pair_rows(values):
    return ordered(values, swap(values), lax.axis_index("c"))


def pair_sum(partial):
    place = lax.axis_index("c")
    halves = partial.reshape(2, partial.shape[0] // 2, partial.shape[1])
    received = swap(low(choose(halves, 1 - place, 0)))
    return choose(halves, place, 0) + received.astype(jnp.float32)


def gather_axis(values, axis):
    if lax.axis_size(axis) == 2:
        return ordered(values, swap(values, axis), lax.axis_index(axis))
    return lax.all_gather(values, axis, axis=0, tiled=True)


def pick(values, axis, dim):
    return choose(values, 1 - lax.axis_index(axis), dim)


def send(values, axis, dim):
    if lax.axis_size(axis) == 2:
        return swap(pick(values, axis, dim), axis)
    return lax.psum_scatter(values, axis, scatter_dimension=dim, tiled=False)


def add(values, received, axis, dim):
    if lax.axis_size(axis) != 2:
        return received
    kept = choose(values, lax.axis_index(axis), dim)
    return (kept.astype(jnp.float32) + received.astype(jnp.float32)).astype(values.dtype)


def together(*values):
    return lax.optimization_barrier(values)


def placed(parts):
    own, across, both, along = parts
    q, y = lax.axis_index("q"), lax.axis_index("y")
    result = jnp.zeros((own.shape[0], 2, 2) + own.shape[1:], own.dtype)
    for part, at_q, at_y in ((own, q, y), (across, 1 - q, y), (both, 1 - q, 1 - y), (along, q, 1 - y)):
        at = (0, at_q, at_y) + (0,) * (own.ndim - 1)
        result = lax.dynamic_update_slice(result, part[:, None, None], at)
    return result


def normalize(values):
    average = jnp.mean(values, axis=-1, keepdims=True)
    centred = values - average
    inverse = lax.rsqrt(jnp.mean(centred * centred, axis=-1, keepdims=True) + EPS)
    return (centred * inverse, inverse)


def norm_back(upstream, normed, inverse, gain):
    gain_grad = jnp.sum(upstream * normed, axis=0)
    scaled = upstream * gain
    back = inverse * (
        scaled
        - jnp.mean(scaled, axis=-1, keepdims=True)
        - normed * jnp.mean(scaled * normed, axis=-1, keepdims=True)
    )
    return (back, gain_grad)


def silu_slope(values):
    sigma = jax.nn.sigmoid(values)
    return sigma * (1.0 + values * (1.0 - sigma))


def split_normalize(values):
    width = values.shape[1]
    average = jnp.mean(values, axis=1)
    centred = values - average[:, None]
    spread = jnp.sum(centred * centred, axis=1)
    other = swap(jnp.stack([average, spread]))
    gap = average - other[0]
    whole = spread + other[1] + (0.5 * width) * gap * gap
    inverse = lax.rsqrt(whole / (2 * width) + EPS)
    middle = 0.5 * (average + other[0])
    return ((values - middle[:, None]) * inverse[:, None], inverse[:, None])


def split_norm_back(upstream, normed, inverse, gain):
    gain_grad = jnp.sum(upstream * normed, axis=0)
    scaled = upstream * gain
    sums = jnp.stack([jnp.sum(scaled, axis=1), jnp.sum(scaled * normed, axis=1)])
    means = (sums + swap(sums)) / (2 * scaled.shape[1])
    back = inverse * (scaled - means[0][:, None] - normed * means[1][:, None])
    return (back, gain_grad)


def feed_forward(hidden, gain, inner, outer):
    rows = hidden.shape[0]
    normed, inverse = normalize(hidden)
    entry = low(normed * gain)
    both = jnp.concatenate([entry, swap(entry)], axis=0)
    middle = right_product(both, inner)
    activated = low(jax.nn.silu(middle))
    partial = product(activated, outer)
    received = swap(low(partial[rows:]))
    result = hidden + 0.5 * (partial[:rows] + received.astype(jnp.float32))
    return (result, (normed, inverse, both, middle, activated))


def feed_back(upstream, gain, inner, outer, kept, *held):
    normed, inverse, both, middle, activated = kept
    rows = upstream.shape[0]
    half = low(0.5 * upstream)
    half_both = jnp.concatenate([half, swap(half)], axis=0)
    active_grad = right_product(half_both, outer)
    middle_grad = low(active_grad * silu_slope(middle))
    if held:
        middle_grad, *held = together(middle_grad, *held)
    partial = product(middle_grad, inner)
    received = swap(low(partial[rows:]))
    entry_grad = partial[:rows] + received.astype(jnp.float32)
    back, gain_grad = norm_back(entry_grad, normed, inverse, gain)

    eighth = middle.shape[1] // 8

    def inner_grad(first, end):
        return left_product(middle_grad[:, first * eighth : end * eighth], both)

    def outer_grad(first, end):
        return left_product(activated[:, first * eighth : end * eighth], half_both)

    return (upstream + back, gain_grad, inner_grad, outer_grad, *held)


def bucket_hits(group):
    offset = group - jnp.arange(2 * group, dtype=jnp.int32)
    distance = jnp.abs(offset)
    level = jnp.zeros_like(distance)
    for power in range(1, 14):
        level = level + (distance >= 2**power).astype(jnp.int32)
    plain = jnp.where(distance < 16, distance, jnp.minimum(12 + level, 31))
    bucket = plain + 32 * (offset < 0).astype(jnp.int32)
    return bucket[:, None] == jnp.arange(NB, dtype=jnp.int32)[None, :]


def halos(values):
    count = lax.axis_size("y")
    forward = [(i, i + 1) for i in range(count - 1)]
    backward = [(target, source) for source, target in forward]
    return (
        lax.ppermute(values[-EDGE:], "y", forward),
        lax.ppermute(values[:EDGE], "y", backward),
    )


CHIPS = ("p", "q", "y")


def on_device(
    frames,
    cotangent,
    lengths,
    norm_gains,
    position_bias,
    attend_weight,
    merge_weight,
    glu_weight,
    depth_weight,
    point_weight,
    inner_weight,
    outer_weight,
):
    core = lax.axis_index("c")
    grid = tuple(lax.axis_size(axis) for axis in CHIPS)
    chips = grid[0] * grid[1] * grid[2]
    rows, width = frames.shape
    pair = 2 * rows
    group = pair * grid[2]
    half = width // 2
    share = attend_weight.shape[0]
    units = inner_weight.shape[2]
    taps = depth_weight.shape[0]
    heads = HEADS // 2
    f32 = jnp.float32

    small = jnp.concatenate([norm_gains.reshape(-1), position_bias, depth_weight.reshape(-1)])
    count = small.shape[0]
    small_rows = -(-2 * count // (16 * width)) * 16
    small_both = ordered(small[None], swap(small[None]), core).reshape(-1)
    small_both = jnp.pad(small_both, (0, small_rows * width - 2 * count)).reshape(small_rows, width)

    inner_pack = inner_weight[0].T
    outer_pack = jnp.concatenate([outer_weight[0], small_both], axis=0)
    pack_two = jnp.concatenate([inner_weight[1].T, outer_weight[1]], axis=0)
    attend_weight, glu_weight = together(attend_weight, glu_weight, outer_pack)[:2]

    def own_columns(weight, shape, dim):
        parts = weight.reshape((share,) + shape)
        mine = choose(parts, core, dim).reshape(share, -1)
        other = swap(choose(parts, 1 - core, dim).reshape(share, -1))
        return ordered(mine, other, core)

    attend_part = own_columns(attend_weight, (3, 2, half), 2)
    glu_part = own_columns(glu_weight, (2, chips, 2, share), 3)
    mixed_pack = jnp.concatenate(
        [attend_part.reshape(-1, width), glu_part, merge_weight, point_weight], axis=0
    )

    square = grid[1] == 2 and grid[2] == 2
    marks = [0]
    for size in (3 * share, 2 * share, share, share):
        marks.append(marks[-1] + size)

    def gather_p(values):
        return lax.all_gather(values, "p", axis=0)

    def in_halves(*parts):
        parts = [part.reshape(grid[0], units, width) for part in parts]
        near = [part[:, : units // 2].reshape(-1, width) for part in parts]
        far = [part[:, units // 2 :].reshape(-1, width) for part in parts]
        return jnp.concatenate(near + far, axis=0)

    if square:
        inner = gather_p(inner_pack)
        two_x, two_y = together(swap(pack_two, "q"), swap(pack_two, "y"))
        pack_two = jnp.stack([pack_two, two_x, swap(two_x, "y"), two_y])
        whole_one = gather_p(outer_pack)
        inner, pack_two = together(inner.reshape(-1, width), pack_two)
        inner_x, inner_y = together(swap(inner, "q"), swap(inner, "y"))
        mixed_pack, inner_x, inner_y = together(mixed_pack, inner_x, inner_y)
        mixed = gather_p(mixed_pack)
        inner_xy = swap(inner_y, "q")
        outer = whole_one[:, :units].reshape(-1, width)
        tiny = whole_one[:, units:]
        outer, tiny = together(outer, tiny)
        across = [(0, 3), (3, 0), (1, 2), (2, 1)]
        tiny_xy = lax.ppermute(tiny, ("q", "y"), across)
        outer_x, outer_y, tiny_x, tiny_y, tiny_xy = together(
            swap(outer, "q"), swap(outer, "y"), swap(tiny, "q"), swap(tiny, "y"), tiny_xy
        )
        small_full = placed((tiny, tiny_x, tiny_xy, tiny_y)).reshape(chips, -1)
        outer_xy = swap(outer_x, "y")
        whole_two = gather_p(pack_two).reshape(chips, 2 * units, width)
        attend_part = mixed[:, : marks[1]].reshape(grid[0], 2 * share, 3 * half)
        rest_part = mixed[:, marks[1] :]
        attend_part, rest_part = together(attend_part, rest_part)
        attend_x = swap(attend_part, "q")
        inner_xy, outer_xy, attend_x, attend_part, rest_part = together(
            inner_xy, outer_xy, attend_x, attend_part, rest_part
        )
        inner_one = in_halves(inner, inner_x, inner_xy, inner_y)
        outer_one = in_halves(outer, outer_x, outer_xy, outer_y)
        attend_y, rest_x = swap(attend_part, "y"), swap(rest_part, "q")
    else:
        inner_one = lax.all_gather(inner_pack, CHIPS, axis=0, tiled=True)
        whole_one = lax.all_gather(outer_pack, CHIPS, axis=0)
        mixed = lax.all_gather(mixed_pack, CHIPS, axis=0)
        whole_two = lax.all_gather(pack_two, CHIPS, axis=0)
        outer_one = whole_one[:, :units].reshape(chips * units, width)
        small_full = whole_one[:, units:].reshape(chips, -1)

    small_full = small_full[:, : 2 * count].reshape(chips, 2, count)
    gain_size = norm_gains.size
    gains = small_full[..., :gain_size].reshape(chips, 2, 6, -1).astype(f32)
    gain_table = gains.transpose(2, 0, 1, 3).reshape(6, width)
    gain_mid = choose(gains[:, :, 3], core, 1).reshape(half)
    bias_table = small_full[..., gain_size : gain_size + position_bias.size].reshape(NB, 2, heads)
    bias_table = choose(bias_table, core, 1)
    depth = choose(small_full[..., gain_size + position_bias.size :], core, 1)
    depth = depth.reshape(chips, taps, share).transpose(1, 0, 2).reshape(taps, half).astype(f32)

    start = lax.axis_index("y") * pair
    info = jnp.stack([lengths[0, 0], lengths[0, 0] + lengths[0, 1], start.astype(jnp.int32)])
    hits = bucket_hits(group)
    bias = jnp.einsum("bh,wb->hw", bias_table, hits.astype(jnp.bfloat16), preferred_element_type=f32)
    bias = bias.reshape(heads // 2, 2, -1)

    hidden = frames.astype(f32)
    first, first_kept = feed_forward(hidden, gain_table[0], inner_one, outer_one)
    if square:
        first, attend_y, rest_part = together(first, attend_y, rest_part)
        rest_y = swap(rest_part, "y")
        attend_full = placed((attend_part, attend_x, swap(attend_y, "q"), attend_y))
    else:
        attend_full = mixed[:, : marks[1]]
    attend_full = attend_full.reshape(width, 3 * half)
    normed_att, inverse_att = normalize(first)
    att_entry = pair_rows(low(normed_att * gain_table[1]))
    triple = low(product(att_entry, attend_full))
    query = triple[:, :half]
    key_value = triple[:, half:]
    if square:
        key_value, rest_x, rest_y = together(key_value, rest_x, rest_y)
        rest_xy = swap(rest_y, "q")
    both = gather_axis(key_value, "y")
    attended = attend(info, bias, query, both)
    if square:
        attended, rest_xy = together(attended, rest_xy)
        rest = placed((rest_part, rest_x, rest_xy, rest_y)).reshape(chips, -1, width)
    else:
        rest = mixed[:, marks[1] :]
    marks = [mark - marks[1] for mark in marks]
    glu_full = rest[:, : marks[2]].reshape(width, width)
    merge_half = rest[:, marks[2] : marks[3]]
    point_full = rest[:, marks[3] : marks[4]].reshape(half, width)
    sides = merge_half.reshape(2, chips // 2, share, width)
    merge_full = ordered(
        choose(sides, core, 0)[:, None], swap(choose(sides, 1 - core, 0))[:, None], core, 1
    ).reshape(half, width)
    second = first + pair_sum(product(attended, merge_full))
    normed_conv, inverse_conv = normalize(second)
    conv_entry = pair_rows(low(normed_conv * gain_table[2]))
    gate_up = product(conv_entry, glu_full)
    gate_sig = jax.nn.sigmoid(gate_up[:, half:])
    glu_rows = low(gate_up[:, :half] * gate_sig)
    glu_low, glu_high = halos(glu_rows)
    mixed_rows = conv(info, glu_low, glu_rows, glu_high, depth, group)
    normed_mid, inverse_mid = split_normalize(mixed_rows)
    activated = normed_mid * gain_mid
    swish = low(jax.nn.silu(activated))
    third = second + pair_sum(product(swish, point_full))
    inner_two = whole_two[:, :units].reshape(chips * units, width)
    outer_two = whole_two[:, units:].reshape(chips * units, width)
    fourth, fourth_kept = feed_forward(third, gain_table[4], inner_two, outer_two)
    normed_last, inverse_last = normalize(fourth)
    result = low(normed_last * gain_table[5])

    def by_chip(values):
        return values.reshape(grid + (values.shape[0] // chips, values.shape[1]))

    def last_sum(values):
        return lax.psum_scatter(values, "p", scatter_dimension=0, tiled=False)

    size = grid[0] * units // 2

    def early_sum(grad):
        shape = (grid[0], 4) if square else grid
        return last_sum(low(grad).reshape(shape + (units, width)))

    def small_of(table_sums, depth_grad, gain_zero, gain_one, gain_two, gain_three, gain_four, gain_five):
        table_grad = jnp.einsum(
            "hw,wb->bh", table_sums.reshape(heads, -1), hits.astype(f32), precision=lax.Precision.HIGHEST
        )

        def of_core(values, dim):
            empty = jnp.zeros_like(values)
            return jnp.stack(
                [jnp.where(core == 0, values, empty), jnp.where(core == 1, values, empty)], axis=dim
            )

        gain_three = of_core(gain_three.reshape(chips, share), 1).reshape(width)
        gain_grads = jnp.stack([gain_zero, gain_one, gain_two, gain_three, gain_four, gain_five])
        small_grads = jnp.concatenate(
            [
                gain_grads.reshape(6, chips, 2, share).transpose(1, 2, 0, 3).reshape(chips, 2, -1),
                of_core(table_grad, 1).reshape(chips, 2, -1),
                of_core(depth_grad.reshape(taps, chips, share).transpose(1, 0, 2), 1).reshape(
                    chips, 2, -1
                ),
            ],
            axis=2,
        )
        small_sum = choose(small_grads, core, 1) + swap(choose(small_grads, 1 - core, 1))
        small_sum = small_sum.reshape(grid + (count,))
        if square:
            at_q, at_y = lax.axis_index("q"), lax.axis_index("y")
            here = [choose(small_sum, at_q, 1), choose(small_sum, 1 - at_q, 1)]
            across = [(0, 3), (3, 0), (1, 2), (2, 1)]
            own = choose(here[0], at_y, 1)
            parts = together(
                choose(here[0], 1 - at_y, 1), choose(here[1], at_y, 1), choose(here[1], 1 - at_y, 1)
            )
            parts = together(
                swap(parts[0], "y"), swap(parts[1], "q"), lax.ppermute(parts[2], ("q", "y"), across)
            )
            small_sum = own + parts[0] + parts[1] + parts[2]
        else:
            small_sum = add(small_sum, send(small_sum, "y", 2), "y", 2)
            small_sum = add(small_sum, send(small_sum, "q", 1), "q", 1)
        one_rows = -(-count // (16 * width)) * 16
        small_sum = jnp.pad(low(small_sum), ((0, 0), (0, one_rows * width - count)))
        small_sum = small_sum.reshape(grid[0], one_rows, width)
        return small_sum

    grad_fourth, gain_five = norm_back(
        cotangent.astype(f32), normed_last, inverse_last, gain_table[5]
    )
    grad_third, gain_four, inner_two_grad, outer_two_grad = feed_back(
        grad_fourth, gain_table[4], inner_two, outer_two, fourth_kept
    )

    if square:
        outer_two_rows = low(outer_two_grad(0, 8)).reshape(grid[0], 4, units, width)
        outer_two_a, grad_third = together(outer_two_rows[:, 1:3], grad_third)
        outer_two_a = swap(outer_two_a, "q")
    else:
        outer_two_sum = early_sum(outer_two_grad(0, 8))

    conv_out_grad = pair_rows(low(grad_third))
    swish_grad = right_product(conv_out_grad, point_full)
    act_grad = swish_grad * silu_slope(activated)
    mixed_grad, gain_three = split_norm_back(act_grad, normed_mid, inverse_mid, gain_mid)
    mixed_low = low(mixed_grad)
    grad_low, grad_high = halos(mixed_low)
    point_grad = by_chip(low(left_product(swish, conv_out_grad)))
    point_a = send(point_grad, "q", 1)
    if square:
        mixed_low, point_a = together(mixed_low, point_a)
    point_half = add(point_grad, point_a, "q", 1)
    point_b = send(point_half, "y", 1)
    inner_two_sum = early_sum(inner_two_grad(0, 8))
    glu_back, depth_grad = conv_back(
        info, glu_low, glu_rows, glu_high, grad_low, mixed_low, grad_high, depth, group
    )
    value_part = gate_up[:, :half]
    gate_grad = low(
        jnp.concatenate(
            [glu_back * gate_sig, glu_back * value_part * gate_sig * (1.0 - gate_sig)], axis=1
        )
    )
    conv_entry_grad = pair_sum(right_product(gate_grad, glu_full))
    glu_grad = by_chip(low(left_product(conv_entry, gate_grad)))
    back_conv, gain_two = norm_back(conv_entry_grad, normed_conv, inverse_conv, gain_table[2])
    grad_second = grad_third + back_conv

    att_out_grad = pair_rows(low(grad_second))
    glu_a = send(glu_grad, "y", 2)
    attended_grad = low(right_product(att_out_grad, merge_full))
    query_grad, key_grad, value_grad, table_sums = attend_back(info, bias, query, both, attended_grad)
    query_grad, key_grad, value_grad, glu_a = together(query_grad, key_grad, value_grad, glu_a)
    if square:
        query_grad, outer_two_a, point_b = together(query_grad, outer_two_a, point_b)
    att_out_grad, query_grad = together(att_out_grad, query_grad)
    merge_grad = low(left_product(attended, att_out_grad)).reshape(chips // 2, 2, share, width)
    merge_grad = ordered(
        choose(merge_grad, core, 1)[None], swap(choose(merge_grad, 1 - core, 1))[None], core
    )
    merge_grad = by_chip(merge_grad.reshape(chips * share, width))
    glu_half = add(glu_grad, glu_a, "y", 2)
    both_grad = jnp.concatenate([key_grad, value_grad], axis=1).reshape(grid[2], pair, width)
    if grid[2] == 2:
        place = lax.axis_index("y")
        both_received = swap(low(choose(both_grad, 1 - place, 0)), "y")
        both_grad = low(choose(both_grad, place, 0) + both_received.astype(f32))
    else:
        both_received = low(lax.psum_scatter(both_grad, "y", scatter_dimension=0, tiled=False))
        both_grad = both_received
    if square:
        outer_two_b = low(outer_two_rows[:, 3].astype(f32) + outer_two_a[:, 1].astype(f32))
        glu_b, merge_a, outer_two_b, both_grad = together(
            pick(glu_half, "q", 1),
            pick(merge_grad, "q", 1),
            outer_two_b,
            both_grad,
        )
        glu_b, merge_a = swap(glu_b, "q"), swap(merge_a, "q")
        outer_two_b = swap(outer_two_b, "y")
    else:
        glu_b, merge_a = send(glu_half, "q", 1), send(merge_grad, "q", 1)
    triple_grad = jnp.concatenate([query_grad, both_grad], axis=1)
    attend_grad = low(left_product(att_entry, triple_grad))
    attend_grad = attend_grad.reshape(grid + (2 * share, 3 * half))
    att_entry_grad = pair_sum(right_product(triple_grad, attend_full))
    back_att, gain_one = norm_back(att_entry_grad, normed_att, inverse_att, gain_table[1])
    grad_first = grad_second + back_att
    attend_sum = last_sum(attend_grad)
    if square:
        outer_two_sum = outer_two_rows[:, 0].astype(f32) + outer_two_a[:, 0].astype(f32)
    input_grad, gain_zero, inner_one_grad, outer_one_grad, glu_b = feed_back(
        grad_first, gain_table[0], inner_one, outer_one, first_kept, glu_b
    )
    if square:
        near_o, near_i = together(low(outer_one_grad(1, 3)), low(inner_one_grad(2, 4)))
        near_o, near_i = swap(near_o, "q"), swap(near_i, "y")
    if square:
        near_o, near_i, glu_b, outer_two_b, far_o, far_i, merge_a, attend_sum, inner_two_sum = together(
            near_o,
            near_i,
            glu_b,
            outer_two_b,
            low(outer_one_grad(5, 7)),
            low(inner_one_grad(6, 8)),
            merge_a,
            attend_sum,
            inner_two_sum,
        )
    edge_half = add(merge_grad, merge_a, "q", 1)
    edge_b = send(edge_half, "y", 1)
    edge_b, table_sums, depth_grad, gain_one, gain_two, gain_three, gain_four, gain_five = together(
        edge_b, table_sums, depth_grad, gain_one, gain_two, gain_three, gain_four, gain_five
    )
    mixed_sum = [add(glu_half, glu_b, "q", 1), add(point_half, point_b, "y", 1)]
    if square:
        outer_two_sum = low(outer_two_sum + outer_two_b.astype(f32))
        mixed_sum += [outer_two_sum, add(edge_half, edge_b, "y", 1)]
    mixed_sum = jnp.concatenate(mixed_sum, axis=1)
    if square:
        mixed_sum = last_sum(mixed_sum)

        def second(first, got_o, got_i):
            return together(
                low(outer_one_grad(first + 3, first + 4) + got_o[size:].astype(f32)),
                low(inner_one_grad(first + 1, first + 2) + got_i[:size].astype(f32)),
            )

        def third(first, got_o, got_i, end_o, end_i):
            sum_o = outer_one_grad(first, first + 1) + got_o[:size].astype(f32)
            sum_i = inner_one_grad(first, first + 1) + got_i[size:].astype(f32)
            sums = [low(sum_i + end_i.astype(f32)), low(sum_o + end_o.astype(f32))]
            return [part.reshape(grid[0], units // 2, width) for part in sums]

        near = second(0, near_o, near_i)
        across_q = jnp.concatenate([far_o, near[1]], axis=0)
        across_y = jnp.concatenate([far_i, near[0]], axis=0)
        across_q, across_y = together(across_q, across_y)
        across_q, across_y = swap(across_q, "q"), swap(across_y, "y")
        small_sum = small_of(
            table_sums, depth_grad, gain_zero, gain_one, gain_two, gain_three, gain_four, gain_five
        )
        across_q, across_y, small_sum = together(across_q, across_y, small_sum)
        far_o, far_i = across_q[: 2 * size], across_y[: 2 * size]
        near = [across_y[2 * size :], across_q[2 * size :]]
        near = third(0, near_o, near_i, *near)
        far_o, attend_sum = together(far_o, attend_sum)
        far = second(4, far_o, far_i)
        far = together(swap(far[0], "y"), swap(far[1], "q"))
        far = third(4, far_o, far_i, *far)
    else:
        mixed_sum = last_sum(mixed_sum)
        edge_sum = last_sum(edge_b)
        small_sum = small_of(
            table_sums, depth_grad, gain_zero, gain_one, gain_two, gain_three, gain_four, gain_five
        )
        inner_sum_one = by_chip(low(inner_one_grad(0, 8)))
        outer_sum_one = by_chip(low(outer_one_grad(0, 8)))
        inner_sum_one = send(send(inner_sum_one, "y", 2), "q", 1)
        outer_sum_one = send(send(outer_sum_one, "y", 2), "q", 1)
        inner_sum_two = send(send(inner_two_sum, "y", 1), "q", 0)
        outer_sum_two = send(send(outer_two_sum, "y", 1), "q", 0)
    attend_half = add(attend_sum, send(attend_sum, "q", 0), "q", 0)
    attend_sum = add(attend_half, send(attend_half, "y", 0), "y", 0)

    if square:
        one_sum = jnp.concatenate(near + far + [small_sum], axis=1)
        one_sum, mixed_sum, inner_two_sum = together(one_sum, mixed_sum, inner_two_sum)
        one_sum = last_sum(one_sum)
        inner_two_a = swap(inner_two_sum[2:], "y")
        inner_two_b = swap(low(inner_two_sum[1].astype(f32) + inner_two_a[0].astype(f32)), "q")
        inner_sum_two = inner_two_sum[0].astype(f32) + inner_two_a[1].astype(f32)
        inner_sum_two = low(inner_sum_two + inner_two_b.astype(f32))
        quarters = [one_sum[at * (units // 2) : (at + 1) * (units // 2)] for at in range(4)]
        inner_sum_one = jnp.concatenate([quarters[0], quarters[2]])
        outer_sum_one = jnp.concatenate([quarters[1], quarters[3]])
        small_sum = one_sum[2 * units :]
        outer_sum_two = mixed_sum[3 * share : 3 * share + units]
        edge_sum = mixed_sum[3 * share + units :]
    else:
        one_sum = last_sum(jnp.concatenate([inner_sum_one, outer_sum_one, small_sum], axis=1))
        inner_sum_one, outer_sum_one = one_sum[:units], one_sum[units : 2 * units]
        small_sum = one_sum[2 * units :]

    def whole_columns(values, shape, dim):
        parts = values.reshape(2, share, -1)
        mine = choose(parts, core, 0)
        other = swap(choose(parts, 1 - core, 0))
        joined = ordered(
            jnp.expand_dims(mine.reshape((share,) + shape), dim),
            jnp.expand_dims(other.reshape((share,) + shape), dim),
            core,
            dim,
        )
        return joined.reshape(share, -1).astype(f32)

    attend_out = whole_columns(attend_sum, (3, half), 2)
    glu_out = whole_columns(mixed_sum[: 2 * share], (2, chips, share), 3)
    point_out = mixed_sum[2 * share : 3 * share].astype(f32)
    merge_out = edge_sum.astype(f32)
    inner_out = jnp.stack([inner_sum_one.T, inner_sum_two.T]).astype(f32)
    outer_out = jnp.stack([outer_sum_one, outer_sum_two]).astype(f32)
    small_out = small_sum.reshape(-1)[:count].astype(f32)
    gains_out = small_out[:gain_size].reshape(norm_gains.shape)
    position_out = small_out[gain_size : gain_size + position_bias.size]
    depth_out = small_out[gain_size + position_bias.size :].reshape(taps, share)
    return (
        result,
        input_grad,
        gains_out,
        position_out,
        attend_out,
        merge_out,
        glu_out,
        depth_out,
        point_out,
        inner_out,
        outer_out,
    )


def solution(mesh):
    across, along = mesh.shape["dp"], mesh.shape["head"]
    fine = Mesh(mesh.devices.reshape(4, across // 4, along // 2, 2), ("p", "q", "y", "c"))
    every = ("p", "q", "y", "c")
    in_specs = (
        P(every, None),
        P(every, None),
        P(("p", "q"), None),
        P(None, every),
        P(every),
        P(every, None),
        P(every, None),
        P(every, None),
        P(None, every),
        P(every, None),
        P(None, None, every),
        P(None, every, None),
    )
    out_specs = (
        P(every, None),
        P(every, None),
        P(None, every),
        P(every),
        P(every, None),
        P(every, None),
        P(every, None),
        P(None, every),
        P(every, None),
        P(None, None, every),
        P(None, every, None),
    )
    return jax.shard_map(
        on_device, mesh=fine, in_specs=in_specs, out_specs=out_specs, check_vma=False
    )
```

```python
import jax
import jax.numpy as jnp
from jax import lax
from jax.experimental import pallas as pl
from jax.experimental.pallas import tpu as pltpu
from jax.sharding import Mesh
from jax.sharding import PartitionSpec as P

HEADS = 16
HD = 64
NB = 64
ROWS = 128
VMEM = 50 * 1024 * 1024


def matmul_in(left, right, dims):
    return lax.dot_general(left, right, (dims, ((), ())), preferred_element_type=jnp.float32)


def spread_of(bias):
    row = jnp.broadcast_to(bias, (ROWS, bias.shape[1]))
    return pltpu.roll(row, 0, 1, stride=1, stride_axis=0)


def half_mask(rows, half):
    lane = lax.broadcasted_iota(jnp.int32, (rows, 2 * HD), 1)
    return lane < HD if half == 0 else lane >= HD


def segment_at(position, first_end, second_end):
    return (position >= first_end).astype(jnp.int32) + (position >= second_end).astype(jnp.int32)


def weights_of(info_ref, spread_ref, raw, number):
    group = raw.shape[1]
    first_end, second_end, start = info_ref[0], info_ref[1], info_ref[2]
    shift = pl.multiple_of(group - start - number * ROWS, ROWS)
    bias = spread_ref[:, pl.ds(shift, group)]
    row = start + number * ROWS + lax.broadcasted_iota(jnp.int32, (ROWS, 1), 0)
    column = lax.broadcasted_iota(jnp.int32, (1, group), 1)
    same = segment_at(row, first_end, second_end) == segment_at(column, first_end, second_end)
    scores = jnp.where(same, raw * 0.125 + bias, -1e30)
    raised = jnp.exp(scores - jnp.max(scores, axis=1, keepdims=True))
    return raised * (1.0 / jnp.sum(raised, axis=1, keepdims=True))


def attend_kernel(info_ref, bias_ref, query_ref, key_ref, value_ref, out_ref, spread_ref, raw_ref, weight_ref):
    outs = []
    for half in range(2):
        mask = half_mask(query_ref.shape[0], half)
        query = jnp.where(mask, query_ref[...], jnp.bfloat16(0))
        raw_ref[half] = matmul_in(query, key_ref[...], ((1,), (1,)))
        spread_ref[half] = spread_of(bias_ref[0, half : half + 1])
    for half in range(2):
        for number in range(query_ref.shape[0] // ROWS):
            rows = pl.ds(number * ROWS, ROWS)
            weights = weights_of(info_ref, spread_ref.at[half], raw_ref[half, rows, :], number)
            weight_ref[half, rows, :] = weights.astype(jnp.bfloat16)
        outs.append(matmul_in(weight_ref[half], value_ref[...], ((1,), (0,))).astype(jnp.bfloat16))
    out_ref[...] = jnp.where(half_mask(query_ref.shape[0], 0), outs[0], outs[1])


def attend_back_kernel(
    info_ref,
    bias_ref,
    query_ref,
    key_ref,
    value_ref,
    grad_ref,
    query_grad_ref,
    key_grad_ref,
    value_grad_ref,
    sums_ref,
    spread_ref,
    diag_ref,
    weight_ref,
    score_ref,
    raw_ref,
    weight_grad_ref,
):
    group, width = key_ref.shape[0], spread_ref.shape[2]
    outs, key_grads, value_grads = [], [], []
    for half in range(2):
        mask = half_mask(query_ref.shape[0], half)
        query = jnp.where(mask, query_ref[...], jnp.bfloat16(0))
        grad = jnp.where(mask, grad_ref[...], jnp.bfloat16(0))
        raw_ref[half] = matmul_in(query, key_ref[...], ((1,), (1,)))
        weight_grad_ref[half] = matmul_in(grad, value_ref[...], ((1,), (1,)))
        spread_ref[half] = spread_of(bias_ref[0, half : half + 1])
    diag_ref[...] = jnp.zeros(diag_ref.shape, jnp.float32)
    for half in range(2):
        mask = half_mask(query_ref.shape[0], half)
        query = jnp.where(mask, query_ref[...], jnp.bfloat16(0))
        grad = jnp.where(mask, grad_ref[...], jnp.bfloat16(0))
        for number in range(query_ref.shape[0] // ROWS):
            rows = pl.ds(number * ROWS, ROWS)
            weights = weights_of(info_ref, spread_ref.at[half], raw_ref[half, rows, :], number)
            weight_ref[half, rows, :] = weights.astype(jnp.bfloat16)
            weight_grad = weight_grad_ref[half, rows, :]
            inner = jnp.sum(weights * weight_grad, axis=1, keepdims=True)
            score_grad = weights * (weight_grad - inner)
            shift = pl.multiple_of(group - info_ref[2] - number * ROWS, ROWS)
            diag_ref[half, :, pl.ds(shift, group)] += score_grad
            score_ref[half, rows, :] = (score_grad * 0.125).astype(jnp.bfloat16)
        outs.append(matmul_in(score_ref[half], key_ref[...], ((1,), (0,))).astype(jnp.bfloat16))
        key_grads.append(matmul_in(score_ref[half], query, ((0,), (0,))))
        value_grads.append(matmul_in(weight_ref[half], grad, ((0,), (0,))))
        total = diag_ref[half]
        size = ROWS // 2
        while size >= 8:
            total = total[:size] + pltpu.roll(total[size:], width - size, 1)
            size //= 2
        for size in (4, 2, 1):
            total = total + pltpu.roll(pltpu.roll(total, 8 - size, 0), width - size, 1)
        sums_ref[0, half : half + 1] = total[0:1]
    query_grad_ref[...] = jnp.where(half_mask(query_ref.shape[0], 0), outs[0], outs[1])
    key_grad_ref[...] = key_grads[0] + key_grads[1]
    value_grad_ref[...] = value_grads[0] + value_grads[1]


def attend_specs(rows, group, width, pairs):
    return [
        pl.BlockSpec(memory_space=pltpu.SMEM),
        pl.BlockSpec((1, 2, width), lambda h: (h, 0, 0)),
        pl.BlockSpec((rows, 2 * HD), lambda h: (0, h)),
        pl.BlockSpec((group, 2 * HD), lambda h: (0, h)),
        pl.BlockSpec((group, 2 * HD), lambda h: (0, pairs + h)),
    ]


def cost_of(heads, rows, group, products):
    return pl.CostEstimate(
        flops=2 * products * heads * rows * group * HD,
        bytes_accessed=4 * heads * HD * (rows + group),
        transcendentals=heads * rows * group,
    )


def attend(info, bias, query, both):
    pairs, _, width = bias.shape
    heads = 2 * pairs
    rows, group = query.shape[0], both.shape[0]
    return pl.pallas_call(
        attend_kernel,
        grid=(pairs,),
        in_specs=attend_specs(rows, group, width, pairs),
        out_specs=pl.BlockSpec((rows, 2 * HD), lambda h: (0, h)),
        out_shape=jax.ShapeDtypeStruct((rows, heads * HD), jnp.bfloat16),
        scratch_shapes=[
            pltpu.VMEM((2, ROWS, width), jnp.float32),
            pltpu.VMEM((2, rows, group), jnp.float32),
            pltpu.VMEM((2, rows, group), jnp.bfloat16),
        ],
        compiler_params=pltpu.CompilerParams(vmem_limit_bytes=VMEM),
        cost_estimate=cost_of(heads, rows, group, 2),
        name="attend",
    )(info, bias, query, both, both)


def attend_back(info, bias, query, both, grad):
    pairs, _, width = bias.shape
    heads = 2 * pairs
    rows, group = query.shape[0], both.shape[0]
    pair_block = pl.BlockSpec((rows, 2 * HD), lambda h: (0, h))
    group_block = pl.BlockSpec((group, 2 * HD), lambda h: (0, h))
    return pl.pallas_call(
        attend_back_kernel,
        grid=(pairs,),
        in_specs=attend_specs(rows, group, width, pairs) + [pair_block],
        out_specs=[pair_block, group_block, group_block, pl.BlockSpec((1, 2, width), lambda h: (h, 0, 0))],
        out_shape=[
            jax.ShapeDtypeStruct((rows, heads * HD), jnp.bfloat16),
            jax.ShapeDtypeStruct((group, heads * HD), jnp.float32),
            jax.ShapeDtypeStruct((group, heads * HD), jnp.float32),
            jax.ShapeDtypeStruct((pairs, 2, width), jnp.float32),
        ],
        scratch_shapes=[
            pltpu.VMEM((2, ROWS, width), jnp.float32),
            pltpu.VMEM((2, ROWS, width), jnp.float32),
            pltpu.VMEM((2, rows, group), jnp.bfloat16),
            pltpu.VMEM((2, rows, group), jnp.bfloat16),
            pltpu.VMEM((2, rows, group), jnp.float32),
            pltpu.VMEM((2, rows, group), jnp.float32),
        ],
        compiler_params=pltpu.CompilerParams(vmem_limit_bytes=VMEM),
        cost_estimate=cost_of(heads, rows, group, 5),
        name="attend_back",
    )(info, bias, query, both, both, grad)


LANES = 128
EDGE = 16


def reach_of(info_ref, rows, group):
    position = info_ref[2] + lax.broadcasted_iota(jnp.int32, (rows, LANES), 0)
    first_end, second_end = info_ref[0], info_ref[1]
    low = jnp.where(position >= second_end, second_end, jnp.where(position >= first_end, first_end, 0))
    high = jnp.where(position < first_end, first_end, jnp.where(position < second_end, second_end, group))
    return (low - position, high - position)


def within(reach, shift):
    if shift < 0:
        return reach[0] <= shift
    return reach[1] > shift


def fill(pad_ref, low_ref, mid_ref, high_ref):
    rows = mid_ref.shape[0]
    pad_ref[0:EDGE, :] = low_ref[...].astype(jnp.float32)
    pad_ref[EDGE : EDGE + rows, :] = mid_ref[...].astype(jnp.float32)
    pad_ref[EDGE + rows :, :] = high_ref[...].astype(jnp.float32)


def taps_of(pad_ref, depth_ref, reach, base, rows, taps, mirror):
    margin = (taps - 1) // 2
    total = jnp.zeros((rows, LANES), jnp.float32)
    for tap in range(taps):
        shift = margin - tap if mirror else tap - margin
        piece = pad_ref[EDGE + base + shift : EDGE + base + shift + rows, :] * depth_ref[tap : tap + 1, :]
        if shift:
            piece = jnp.where(within(reach, shift), piece, 0.0)
        total = total + piece
    return total


def conv_kernel(group, taps, info_ref, low_ref, mid_ref, high_ref, depth_ref, out_ref, pad_ref):
    fill(pad_ref, low_ref, mid_ref, high_ref)
    low, high = reach_of(info_ref, mid_ref.shape[0], group)
    for base in range(0, mid_ref.shape[0], STEP):
        reach = (low[base : base + STEP], high[base : base + STEP])
        out_ref[base : base + STEP, :] = taps_of(pad_ref, depth_ref, reach, base, STEP, taps, False)


STEP = 64


def conv_back_kernel(
    group,
    taps,
    info_ref,
    low_ref,
    mid_ref,
    high_ref,
    grad_low_ref,
    grad_mid_ref,
    grad_high_ref,
    depth_ref,
    out_ref,
    depth_grad_ref,
    pad_ref,
    grad_pad_ref,
    sum_ref,
):
    fill(pad_ref, low_ref, mid_ref, high_ref)
    fill(grad_pad_ref, grad_low_ref, grad_mid_ref, grad_high_ref)
    low, high = reach_of(info_ref, mid_ref.shape[0], group)
    margin = (taps - 1) // 2
    sum_ref[...] = jnp.zeros(sum_ref.shape, jnp.float32)
    for base in range(0, mid_ref.shape[0], STEP):
        reach = (low[base : base + STEP], high[base : base + STEP])
        out_ref[base : base + STEP, :] = taps_of(grad_pad_ref, depth_ref, reach, base, STEP, taps, True)
        grad = grad_pad_ref[EDGE + base : EDGE + base + STEP, :]
        for tap in range(taps):
            shift = tap - margin
            piece = pad_ref[EDGE + base + shift : EDGE + base + shift + STEP, :] * grad
            if shift:
                piece = jnp.where(within(reach, shift), piece, 0.0)
            sum_ref[8 * tap : 8 * tap + 8, :] += jnp.sum(piece.reshape(STEP // 8, 8, LANES), axis=0)
    for tap in range(taps):
        depth_grad_ref[tap : tap + 1, :] = jnp.sum(sum_ref[8 * tap : 8 * tap + 8, :], axis=0, keepdims=True)


def lane_block(rows):
    return pl.BlockSpec((rows, LANES), lambda i: (0, i))


def conv(info, low, mid, high, depth, group):
    rows, width = mid.shape
    taps = depth.shape[0]
    return pl.pallas_call(
        lambda *refs: conv_kernel(group, taps, *refs),
        grid=(width // LANES,),
        in_specs=[pl.BlockSpec(memory_space=pltpu.SMEM)]
        + [lane_block(EDGE), lane_block(rows), lane_block(EDGE), lane_block(taps)],
        out_specs=lane_block(rows),
        out_shape=jax.ShapeDtypeStruct((rows, width), jnp.float32),
        scratch_shapes=[pltpu.VMEM((rows + 2 * EDGE, LANES), jnp.float32)],
        compiler_params=pltpu.CompilerParams(vmem_limit_bytes=VMEM),
        cost_estimate=pl.CostEstimate(
            flops=2 * taps * rows * width, bytes_accessed=6 * rows * width, transcendentals=0
        ),
        name="conv",
    )(info, low, mid, high, depth)


def conv_back(info, low, mid, high, grad_low, grad_mid, grad_high, depth, group):
    rows, width = mid.shape
    taps = depth.shape[0]
    return pl.pallas_call(
        lambda *refs: conv_back_kernel(group, taps, *refs),
        grid=(width // LANES,),
        in_specs=[pl.BlockSpec(memory_space=pltpu.SMEM)]
        + [lane_block(EDGE), lane_block(rows), lane_block(EDGE)] * 2
        + [lane_block(taps)],
        out_specs=[lane_block(rows), lane_block(taps)],
        out_shape=[
            jax.ShapeDtypeStruct((rows, width), jnp.float32),
            jax.ShapeDtypeStruct((taps, width), jnp.float32),
        ],
        scratch_shapes=[
            pltpu.VMEM((rows + 2 * EDGE, LANES), jnp.float32),
            pltpu.VMEM((rows + 2 * EDGE, LANES), jnp.float32),
            pltpu.VMEM((8 * taps, LANES), jnp.float32),
        ],
        compiler_params=pltpu.CompilerParams(vmem_limit_bytes=VMEM),
        cost_estimate=pl.CostEstimate(
            flops=4 * taps * rows * width, bytes_accessed=8 * rows * width, transcendentals=0
        ),
        name="conv_back",
    )(info, low, mid, high, grad_low, grad_mid, grad_high, depth)


EPS = 1e-05
CORES = [(0, 1), (1, 0)]


def low(values):
    return values.astype(jnp.bfloat16)


def product(left_in, right_in):
    return jnp.dot(left_in, right_in, preferred_element_type=jnp.float32)


def left_product(left_in, right_in):
    return jnp.einsum("nd,nf->df", left_in, right_in, preferred_element_type=jnp.float32)


def right_product(left_in, right_in):
    return jnp.einsum("nf,df->nd", left_in, right_in, preferred_element_type=jnp.float32)


def swap(values, axis="c"):
    return lax.ppermute(values, axis, CORES)


def ordered(mine, other, place, dim=0):
    first = place == 0
    return jnp.concatenate([jnp.where(first, mine, other), jnp.where(first, other, mine)], axis=dim)


def choose(values, place, dim):
    return lax.dynamic_index_in_dim(values, place, dim, keepdims=False)


def pair_rows(values):
    return ordered(values, swap(values), lax.axis_index("c"))


def pair_sum(partial):
    place = lax.axis_index("c")
    halves = partial.reshape(2, partial.shape[0] // 2, partial.shape[1])
    received = swap(low(choose(halves, 1 - place, 0)))
    return choose(halves, place, 0) + received.astype(jnp.float32)


def gather_axis(values, axis):
    if lax.axis_size(axis) == 2:
        return ordered(values, swap(values, axis), lax.axis_index(axis))
    return lax.all_gather(values, axis, axis=0, tiled=True)


def pick(values, axis, dim):
    return choose(values, 1 - lax.axis_index(axis), dim)


def send(values, axis, dim):
    if lax.axis_size(axis) == 2:
        return swap(pick(values, axis, dim), axis)
    return lax.psum_scatter(values, axis, scatter_dimension=dim, tiled=False)


def add(values, received, axis, dim):
    if lax.axis_size(axis) != 2:
        return received
    kept = choose(values, lax.axis_index(axis), dim)
    return (kept.astype(jnp.float32) + received.astype(jnp.float32)).astype(values.dtype)


def together(*values):
    return lax.optimization_barrier(values)


def placed(parts):
    own, across, both, along = parts
    q, y = lax.axis_index("q"), lax.axis_index("y")
    result = jnp.zeros((own.shape[0], 2, 2) + own.shape[1:], own.dtype)
    for part, at_q, at_y in ((own, q, y), (across, 1 - q, y), (both, 1 - q, 1 - y), (along, q, 1 - y)):
        at = (0, at_q, at_y) + (0,) * (own.ndim - 1)
        result = lax.dynamic_update_slice(result, part[:, None, None], at)
    return result


def normalize(values):
    average = jnp.mean(values, axis=-1, keepdims=True)
    centred = values - average
    inverse = lax.rsqrt(jnp.mean(centred * centred, axis=-1, keepdims=True) + EPS)
    return (centred * inverse, inverse)


def norm_back(upstream, normed, inverse, gain):
    gain_grad = jnp.sum(upstream * normed, axis=0)
    scaled = upstream * gain
    back = inverse * (
        scaled
        - jnp.mean(scaled, axis=-1, keepdims=True)
        - normed * jnp.mean(scaled * normed, axis=-1, keepdims=True)
    )
    return (back, gain_grad)


def silu_slope(values):
    sigma = jax.nn.sigmoid(values)
    return sigma * (1.0 + values * (1.0 - sigma))


def split_normalize(values):
    width = values.shape[1]
    average = jnp.mean(values, axis=1)
    centred = values - average[:, None]
    spread = jnp.sum(centred * centred, axis=1)
    other = swap(jnp.stack([average, spread]))
    gap = average - other[0]
    whole = spread + other[1] + (0.5 * width) * gap * gap
    inverse = lax.rsqrt(whole / (2 * width) + EPS)
    middle = 0.5 * (average + other[0])
    return ((values - middle[:, None]) * inverse[:, None], inverse[:, None])


def split_norm_back(upstream, normed, inverse, gain):
    gain_grad = jnp.sum(upstream * normed, axis=0)
    scaled = upstream * gain
    sums = jnp.stack([jnp.sum(scaled, axis=1), jnp.sum(scaled * normed, axis=1)])
    means = (sums + swap(sums)) / (2 * scaled.shape[1])
    back = inverse * (scaled - means[0][:, None] - normed * means[1][:, None])
    return (back, gain_grad)


def feed_forward(hidden, gain, inner, outer):
    rows = hidden.shape[0]
    normed, inverse = normalize(hidden)
    entry = low(normed * gain)
    both = jnp.concatenate([entry, swap(entry)], axis=0)
    middle = right_product(both, inner)
    activated = low(jax.nn.silu(middle))
    partial = product(activated, outer)
    received = swap(low(partial[rows:]))
    result = hidden + 0.5 * (partial[:rows] + received.astype(jnp.float32))
    return (result, (normed, inverse, both, middle, activated))


def feed_back(upstream, gain, inner, outer, kept, *held):
    normed, inverse, both, middle, activated = kept
    rows = upstream.shape[0]
    half = low(0.5 * upstream)
    half_both = jnp.concatenate([half, swap(half)], axis=0)
    active_grad = right_product(half_both, outer)
    middle_grad = low(active_grad * silu_slope(middle))
    if held:
        middle_grad, *held = together(middle_grad, *held)
    partial = product(middle_grad, inner)
    received = swap(low(partial[rows:]))
    entry_grad = partial[:rows] + received.astype(jnp.float32)
    back, gain_grad = norm_back(entry_grad, normed, inverse, gain)

    eighth = middle.shape[1] // 8

    def inner_grad(first, end, tie=None):
        columns = middle_grad[:, first * eighth : end * eighth]
        if tie is None:
            return left_product(columns, both)
        columns, tie = together(columns, tie)
        return (left_product(columns, both), tie)

    def outer_grad(first, end):
        return left_product(activated[:, first * eighth : end * eighth], half_both)

    return (upstream + back, gain_grad, inner_grad, outer_grad, *held)


def bucket_hits(group):
    offset = group - jnp.arange(2 * group, dtype=jnp.int32)
    distance = jnp.abs(offset)
    level = jnp.zeros_like(distance)
    for power in range(1, 14):
        level = level + (distance >= 2**power).astype(jnp.int32)
    plain = jnp.where(distance < 16, distance, jnp.minimum(12 + level, 31))
    bucket = plain + 32 * (offset < 0).astype(jnp.int32)
    return bucket[:, None] == jnp.arange(NB, dtype=jnp.int32)[None, :]


def halos(values):
    count = lax.axis_size("y")
    forward = [(i, i + 1) for i in range(count - 1)]
    backward = [(target, source) for source, target in forward]
    return (
        lax.ppermute(values[-EDGE:], "y", forward),
        lax.ppermute(values[:EDGE], "y", backward),
    )


CHIPS = ("p", "q", "y")


def on_device(
    frames,
    cotangent,
    lengths,
    norm_gains,
    position_bias,
    attend_weight,
    merge_weight,
    glu_weight,
    depth_weight,
    point_weight,
    inner_weight,
    outer_weight,
):
    core = lax.axis_index("c")
    grid = tuple(lax.axis_size(axis) for axis in CHIPS)
    chips = grid[0] * grid[1] * grid[2]
    rows, width = frames.shape
    pair = 2 * rows
    group = pair * grid[2]
    half = width // 2
    share = attend_weight.shape[0]
    units = inner_weight.shape[2]
    taps = depth_weight.shape[0]
    heads = HEADS // 2
    f32 = jnp.float32

    small = jnp.concatenate([norm_gains.reshape(-1), position_bias, depth_weight.reshape(-1)])
    count = small.shape[0]
    small_rows = -(-2 * count // (16 * width)) * 16
    small_both = ordered(small[None], swap(small[None]), core).reshape(-1)
    small_both = jnp.pad(small_both, (0, small_rows * width - 2 * count)).reshape(small_rows, width)

    inner_pack = inner_weight[0].T
    outer_pack = jnp.concatenate([outer_weight[0], small_both], axis=0)
    pack_two = jnp.concatenate([inner_weight[1].T, outer_weight[1]], axis=0)
    attend_weight, glu_weight = together(attend_weight, glu_weight, outer_pack)[:2]

    def own_columns(weight, shape, dim):
        parts = weight.reshape((share,) + shape)
        mine = choose(parts, core, dim).reshape(share, -1)
        other = swap(choose(parts, 1 - core, dim).reshape(share, -1))
        return ordered(mine, other, core)

    attend_part = own_columns(attend_weight, (3, 2, half), 2)
    glu_part = own_columns(glu_weight, (2, chips, 2, share), 3)
    mixed_pack = jnp.concatenate(
        [attend_part.reshape(-1, width), glu_part, merge_weight, point_weight], axis=0
    )

    square = grid[1] == 2 and grid[2] == 2
    marks = [0]
    for size in (3 * share, 2 * share, share, share):
        marks.append(marks[-1] + size)

    def gather_p(values):
        return lax.all_gather(values, "p", axis=0)

    def in_halves(*parts):
        parts = [part.reshape(grid[0], units, width) for part in parts]
        near = [part[:, : units // 2].reshape(-1, width) for part in parts]
        far = [part[:, units // 2 :].reshape(-1, width) for part in parts]
        return jnp.concatenate(near + far, axis=0)

    if square:
        inner = gather_p(inner_pack)
        two_x, two_y = together(swap(pack_two, "q"), swap(pack_two, "y"))
        pack_two = jnp.stack([pack_two, two_x, swap(two_x, "y"), two_y])
        whole_one = gather_p(outer_pack)
        inner, pack_two = together(inner.reshape(-1, width), pack_two)
        inner_x, inner_y = together(swap(inner, "q"), swap(inner, "y"))
        mixed_pack, inner_x, inner_y = together(mixed_pack, inner_x, inner_y)
        mixed = gather_p(mixed_pack)
        inner_xy = swap(inner_y, "q")
        outer = whole_one[:, :units].reshape(-1, width)
        tiny = whole_one[:, units:]
        outer, tiny = together(outer, tiny)
        across = [(0, 3), (3, 0), (1, 2), (2, 1)]
        tiny_xy = lax.ppermute(tiny, ("q", "y"), across)
        outer_x, outer_y, tiny_x, tiny_y, tiny_xy = together(
            swap(outer, "q"), swap(outer, "y"), swap(tiny, "q"), swap(tiny, "y"), tiny_xy
        )
        small_full = placed((tiny, tiny_x, tiny_xy, tiny_y)).reshape(chips, -1)
        outer_xy = swap(outer_x, "y")
        whole_two = gather_p(pack_two).reshape(chips, 2 * units, width)
        attend_part = mixed[:, : marks[1]].reshape(grid[0], 2 * share, 3 * half)
        rest_part = mixed[:, marks[1] :]
        attend_part, rest_part = together(attend_part, rest_part)
        attend_x = swap(attend_part, "q")
        inner_xy, outer_xy, attend_x, attend_part, rest_part = together(
            inner_xy, outer_xy, attend_x, attend_part, rest_part
        )
        inner_one = in_halves(inner, inner_x, inner_xy, inner_y)
        outer_one = in_halves(outer, outer_x, outer_xy, outer_y)
        attend_y, rest_x = swap(attend_part, "y"), swap(rest_part, "q")
    else:
        inner_one = lax.all_gather(inner_pack, CHIPS, axis=0, tiled=True)
        whole_one = lax.all_gather(outer_pack, CHIPS, axis=0)
        mixed = lax.all_gather(mixed_pack, CHIPS, axis=0)
        whole_two = lax.all_gather(pack_two, CHIPS, axis=0)
        outer_one = whole_one[:, :units].reshape(chips * units, width)
        small_full = whole_one[:, units:].reshape(chips, -1)

    small_full = small_full[:, : 2 * count].reshape(chips, 2, count)
    gain_size = norm_gains.size
    gains = small_full[..., :gain_size].reshape(chips, 2, 6, -1).astype(f32)
    gain_table = gains.transpose(2, 0, 1, 3).reshape(6, width)
    gain_mid = choose(gains[:, :, 3], core, 1).reshape(half)
    bias_table = small_full[..., gain_size : gain_size + position_bias.size].reshape(NB, 2, heads)
    bias_table = choose(bias_table, core, 1)
    depth = choose(small_full[..., gain_size + position_bias.size :], core, 1)
    depth = depth.reshape(chips, taps, share).transpose(1, 0, 2).reshape(taps, half).astype(f32)

    start = lax.axis_index("y") * pair
    info = jnp.stack([lengths[0, 0], lengths[0, 0] + lengths[0, 1], start.astype(jnp.int32)])
    hits = bucket_hits(group)
    bias = jnp.einsum("bh,wb->hw", bias_table, hits.astype(jnp.bfloat16), preferred_element_type=f32)
    bias = bias.reshape(heads // 2, 2, -1)

    hidden = frames.astype(f32)
    first, first_kept = feed_forward(hidden, gain_table[0], inner_one, outer_one)
    if square:
        first, attend_y, rest_part = together(first, attend_y, rest_part)
        rest_y = swap(rest_part, "y")
        attend_full = placed((attend_part, attend_x, swap(attend_y, "q"), attend_y))
    else:
        attend_full = mixed[:, : marks[1]]
    attend_full = attend_full.reshape(width, 3 * half)
    normed_att, inverse_att = normalize(first)
    att_entry = pair_rows(low(normed_att * gain_table[1]))
    triple = low(product(att_entry, attend_full))
    query = triple[:, :half]
    key_value = triple[:, half:]
    if square:
        key_value, rest_x, rest_y = together(key_value, rest_x, rest_y)
        rest_xy = swap(rest_y, "q")
    both = gather_axis(key_value, "y")
    attended = attend(info, bias, query, both)
    if square:
        attended, rest_xy = together(attended, rest_xy)
        rest = placed((rest_part, rest_x, rest_xy, rest_y)).reshape(chips, -1, width)
    else:
        rest = mixed[:, marks[1] :]
    marks = [mark - marks[1] for mark in marks]
    glu_full = rest[:, : marks[2]].reshape(width, width)
    merge_half = rest[:, marks[2] : marks[3]]
    point_full = rest[:, marks[3] : marks[4]].reshape(half, width)
    sides = merge_half.reshape(2, chips // 2, share, width)
    merge_full = ordered(
        choose(sides, core, 0)[:, None], swap(choose(sides, 1 - core, 0))[:, None], core, 1
    ).reshape(half, width)
    second = first + pair_sum(product(attended, merge_full))
    normed_conv, inverse_conv = normalize(second)
    conv_entry = pair_rows(low(normed_conv * gain_table[2]))
    gate_up = product(conv_entry, glu_full)
    gate_sig = jax.nn.sigmoid(gate_up[:, half:])
    glu_rows = low(gate_up[:, :half] * gate_sig)
    glu_low, glu_high = halos(glu_rows)
    mixed_rows = conv(info, glu_low, glu_rows, glu_high, depth, group)
    normed_mid, inverse_mid = split_normalize(mixed_rows)
    activated = normed_mid * gain_mid
    swish = low(jax.nn.silu(activated))
    third = second + pair_sum(product(swish, point_full))
    inner_two = whole_two[:, :units].reshape(chips * units, width)
    outer_two = whole_two[:, units:].reshape(chips * units, width)
    fourth, fourth_kept = feed_forward(third, gain_table[4], inner_two, outer_two)
    normed_last, inverse_last = normalize(fourth)
    result = low(normed_last * gain_table[5])

    def by_chip(values):
        return values.reshape(grid + (values.shape[0] // chips, values.shape[1]))

    def last_sum(values):
        return lax.psum_scatter(values, "p", scatter_dimension=0, tiled=False)

    size = grid[0] * units // 2

    def early_sum(grad):
        shape = (grid[0], 4) if square else grid
        return last_sum(low(grad).reshape(shape + (units, width)))

    def small_of(table_sums, depth_grad, gain_zero, gain_one, gain_two, gain_three, gain_four, gain_five):
        table_grad = jnp.einsum(
            "hw,wb->bh", table_sums.reshape(heads, -1), hits.astype(f32), precision=lax.Precision.HIGHEST
        )

        def of_core(values, dim):
            empty = jnp.zeros_like(values)
            return jnp.stack(
                [jnp.where(core == 0, values, empty), jnp.where(core == 1, values, empty)], axis=dim
            )

        gain_three = of_core(gain_three.reshape(chips, share), 1).reshape(width)
        gain_grads = jnp.stack([gain_zero, gain_one, gain_two, gain_three, gain_four, gain_five])
        small_grads = jnp.concatenate(
            [
                gain_grads.reshape(6, chips, 2, share).transpose(1, 2, 0, 3).reshape(chips, 2, -1),
                of_core(table_grad, 1).reshape(chips, 2, -1),
                of_core(depth_grad.reshape(taps, chips, share).transpose(1, 0, 2), 1).reshape(
                    chips, 2, -1
                ),
            ],
            axis=2,
        )
        small_sum = choose(small_grads, core, 1) + swap(choose(small_grads, 1 - core, 1))
        small_sum = small_sum.reshape(grid + (count,))
        if square:
            at_q, at_y = lax.axis_index("q"), lax.axis_index("y")
            here = [choose(small_sum, at_q, 1), choose(small_sum, 1 - at_q, 1)]
            across = [(0, 3), (3, 0), (1, 2), (2, 1)]
            own = choose(here[0], at_y, 1)
            parts = together(
                choose(here[0], 1 - at_y, 1), choose(here[1], at_y, 1), choose(here[1], 1 - at_y, 1)
            )
            parts = together(
                swap(parts[0], "y"), swap(parts[1], "q"), lax.ppermute(parts[2], ("q", "y"), across)
            )
            small_sum = own + parts[0] + parts[1] + parts[2]
        else:
            small_sum = add(small_sum, send(small_sum, "y", 2), "y", 2)
            small_sum = add(small_sum, send(small_sum, "q", 1), "q", 1)
        one_rows = -(-count // (16 * width)) * 16
        small_sum = jnp.pad(low(small_sum), ((0, 0), (0, one_rows * width - count)))
        small_sum = small_sum.reshape(grid[0], one_rows, width)
        return small_sum

    grad_fourth, gain_five = norm_back(
        cotangent.astype(f32), normed_last, inverse_last, gain_table[5]
    )
    grad_third, gain_four, inner_two_grad, outer_two_grad = feed_back(
        grad_fourth, gain_table[4], inner_two, outer_two, fourth_kept
    )

    if square:
        outer_two_rows = low(outer_two_grad(0, 8)).reshape(grid[0], 4, units, width)
        outer_two_a, grad_third = together(outer_two_rows[:, 1:3], grad_third)
        outer_two_a = swap(outer_two_a, "q")
    else:
        outer_two_sum = early_sum(outer_two_grad(0, 8))

    conv_out_grad = pair_rows(low(grad_third))
    swish_grad = right_product(conv_out_grad, point_full)
    act_grad = swish_grad * silu_slope(activated)
    mixed_grad, gain_three = split_norm_back(act_grad, normed_mid, inverse_mid, gain_mid)
    mixed_low = low(mixed_grad)
    grad_low, grad_high = halos(mixed_low)
    inner_two_rows, mixed_low = inner_two_grad(0, 8, mixed_low)
    point_grad = by_chip(low(left_product(swish, conv_out_grad)))
    point_a = send(point_grad, "q", 1)
    if square:
        mixed_low, point_a = together(mixed_low, point_a)
    point_half = add(point_grad, point_a, "q", 1)
    point_b = send(point_half, "y", 1)
    inner_two_sum = early_sum(inner_two_rows)
    glu_back, depth_grad = conv_back(
        info, glu_low, glu_rows, glu_high, grad_low, mixed_low, grad_high, depth, group
    )
    value_part = gate_up[:, :half]
    gate_grad = low(
        jnp.concatenate(
            [glu_back * gate_sig, glu_back * value_part * gate_sig * (1.0 - gate_sig)], axis=1
        )
    )
    conv_entry_grad = pair_sum(right_product(gate_grad, glu_full))
    glu_grad = by_chip(low(left_product(conv_entry, gate_grad)))
    back_conv, gain_two = norm_back(conv_entry_grad, normed_conv, inverse_conv, gain_table[2])
    grad_second = grad_third + back_conv

    att_out_grad = pair_rows(low(grad_second))
    glu_a = send(glu_grad, "y", 2)
    attended_grad = low(right_product(att_out_grad, merge_full))
    query_grad, key_grad, value_grad, table_sums = attend_back(info, bias, query, both, attended_grad)
    query_grad, key_grad, value_grad, glu_a = together(query_grad, key_grad, value_grad, glu_a)
    if square:
        query_grad, outer_two_a, point_b = together(query_grad, outer_two_a, point_b)
    att_out_grad, query_grad = together(att_out_grad, query_grad)
    merge_grad = low(left_product(attended, att_out_grad)).reshape(chips // 2, 2, share, width)
    merge_grad = ordered(
        choose(merge_grad, core, 1)[None], swap(choose(merge_grad, 1 - core, 1))[None], core
    )
    merge_grad = by_chip(merge_grad.reshape(chips * share, width))
    glu_half = add(glu_grad, glu_a, "y", 2)
    both_grad = jnp.concatenate([key_grad, value_grad], axis=1).reshape(grid[2], pair, width)
    if grid[2] == 2:
        place = lax.axis_index("y")
        both_received = swap(low(choose(both_grad, 1 - place, 0)), "y")
        both_grad = low(choose(both_grad, place, 0) + both_received.astype(f32))
    else:
        both_received = low(lax.psum_scatter(both_grad, "y", scatter_dimension=0, tiled=False))
        both_grad = both_received
    if square:
        outer_two_b = low(outer_two_rows[:, 3].astype(f32) + outer_two_a[:, 1].astype(f32))
        glu_b, merge_a, outer_two_b, both_grad = together(
            pick(glu_half, "q", 1),
            pick(merge_grad, "q", 1),
            outer_two_b,
            both_grad,
        )
        glu_b, merge_a = swap(glu_b, "q"), swap(merge_a, "q")
        outer_two_b = swap(outer_two_b, "y")
    else:
        glu_b, merge_a = send(glu_half, "q", 1), send(merge_grad, "q", 1)
    triple_grad = jnp.concatenate([query_grad, both_grad], axis=1)
    attend_grad = low(left_product(att_entry, triple_grad))
    attend_grad = attend_grad.reshape(grid + (2 * share, 3 * half))
    att_entry_grad = pair_sum(right_product(triple_grad, attend_full))
    back_att, gain_one = norm_back(att_entry_grad, normed_att, inverse_att, gain_table[1])
    grad_first = grad_second + back_att
    attend_sum = last_sum(attend_grad)
    if square:
        outer_two_sum = outer_two_rows[:, 0].astype(f32) + outer_two_a[:, 0].astype(f32)
    input_grad, gain_zero, inner_one_grad, outer_one_grad, glu_b = feed_back(
        grad_first, gain_table[0], inner_one, outer_one, first_kept, glu_b
    )
    if square:
        near_o, near_i, inner_two_sum = together(
            low(outer_one_grad(1, 3)), low(inner_one_grad(2, 4)), inner_two_sum
        )
        near_o, near_i = swap(near_o, "q"), swap(near_i, "y")
    if square:
        near_o, near_i, glu_b, outer_two_b, far_o, far_i, merge_a = together(
            near_o,
            near_i,
            glu_b,
            outer_two_b,
            low(outer_one_grad(5, 7)),
            low(inner_one_grad(6, 8)),
            merge_a,
        )
    edge_half = add(merge_grad, merge_a, "q", 1)
    edge_b = send(edge_half, "y", 1)
    edge_b, table_sums, depth_grad, gain_one, gain_two, gain_three, gain_four, gain_five = together(
        edge_b, table_sums, depth_grad, gain_one, gain_two, gain_three, gain_four, gain_five
    )
    mixed_sum = [add(glu_half, glu_b, "q", 1), add(point_half, point_b, "y", 1)]
    if square:
        outer_two_sum = low(outer_two_sum + outer_two_b.astype(f32))
        mixed_sum += [outer_two_sum, add(edge_half, edge_b, "y", 1)]
    mixed_sum = jnp.concatenate(mixed_sum, axis=1)
    if square:
        mixed_sum = last_sum(mixed_sum)

        def second(first, got_o, got_i):
            return together(
                low(outer_one_grad(first + 3, first + 4) + got_o[size:].astype(f32)),
                low(inner_one_grad(first + 1, first + 2) + got_i[:size].astype(f32)),
            )

        def third(first, got_o, got_i, end_o, end_i):
            sum_o = outer_one_grad(first, first + 1) + got_o[:size].astype(f32)
            sum_i = inner_one_grad(first, first + 1) + got_i[size:].astype(f32)
            sums = [low(sum_i + end_i.astype(f32)), low(sum_o + end_o.astype(f32))]
            return [part.reshape(grid[0], units // 2, width) for part in sums]

        near = second(0, near_o, near_i)
        across_q = jnp.concatenate([far_o, near[1]], axis=0)
        across_y = jnp.concatenate([far_i, near[0]], axis=0)
        across_q, across_y = together(across_q, across_y)
        across_q, across_y = swap(across_q, "q"), swap(across_y, "y")
        small_sum = small_of(
            table_sums, depth_grad, gain_zero, gain_one, gain_two, gain_three, gain_four, gain_five
        )
        across_q, across_y, small_sum, attend_sum = together(across_q, across_y, small_sum, attend_sum)
        far_o, far_i = across_q[: 2 * size], across_y[: 2 * size]
        near = [across_y[2 * size :], across_q[2 * size :]]
        near = third(0, near_o, near_i, *near)
        far_o, attend_sum = together(far_o, attend_sum)
        far = second(4, far_o, far_i)
        far = together(swap(far[0], "y"), swap(far[1], "q"))
        far = third(4, far_o, far_i, *far)
    else:
        mixed_sum = last_sum(mixed_sum)
        edge_sum = last_sum(edge_b)
        small_sum = small_of(
            table_sums, depth_grad, gain_zero, gain_one, gain_two, gain_three, gain_four, gain_five
        )
        inner_sum_one = by_chip(low(inner_one_grad(0, 8)))
        outer_sum_one = by_chip(low(outer_one_grad(0, 8)))
        inner_sum_one = send(send(inner_sum_one, "y", 2), "q", 1)
        outer_sum_one = send(send(outer_sum_one, "y", 2), "q", 1)
        inner_sum_two = send(send(inner_two_sum, "y", 1), "q", 0)
        outer_sum_two = send(send(outer_two_sum, "y", 1), "q", 0)
    attend_half = add(attend_sum, send(attend_sum, "q", 0), "q", 0)
    attend_sum = add(attend_half, send(attend_half, "y", 0), "y", 0)

    if square:
        one_sum = jnp.concatenate(near + far + [small_sum], axis=1)
        one_sum, mixed_sum, inner_two_sum = together(one_sum, mixed_sum, inner_two_sum)
        one_sum = last_sum(one_sum)
        inner_two_a = swap(inner_two_sum[2:], "y")
        inner_two_b = swap(low(inner_two_sum[1].astype(f32) + inner_two_a[0].astype(f32)), "q")
        inner_sum_two = inner_two_sum[0].astype(f32) + inner_two_a[1].astype(f32)
        inner_sum_two = low(inner_sum_two + inner_two_b.astype(f32))
        quarters = [one_sum[at * (units // 2) : (at + 1) * (units // 2)] for at in range(4)]
        inner_sum_one = jnp.concatenate([quarters[0], quarters[2]])
        outer_sum_one = jnp.concatenate([quarters[1], quarters[3]])
        small_sum = one_sum[2 * units :]
        outer_sum_two = mixed_sum[3 * share : 3 * share + units]
        edge_sum = mixed_sum[3 * share + units :]
    else:
        one_sum = last_sum(jnp.concatenate([inner_sum_one, outer_sum_one, small_sum], axis=1))
        inner_sum_one, outer_sum_one = one_sum[:units], one_sum[units : 2 * units]
        small_sum = one_sum[2 * units :]

    def whole_columns(values, shape, dim):
        parts = values.reshape(2, share, -1)
        mine = choose(parts, core, 0)
        other = swap(choose(parts, 1 - core, 0))
        joined = ordered(
            jnp.expand_dims(mine.reshape((share,) + shape), dim),
            jnp.expand_dims(other.reshape((share,) + shape), dim),
            core,
            dim,
        )
        return joined.reshape(share, -1).astype(f32)

    attend_out = whole_columns(attend_sum, (3, half), 2)
    glu_out = whole_columns(mixed_sum[: 2 * share], (2, chips, share), 3)
    point_out = mixed_sum[2 * share : 3 * share].astype(f32)
    merge_out = edge_sum.astype(f32)
    inner_out = jnp.stack([inner_sum_one.T, inner_sum_two.T]).astype(f32)
    outer_out = jnp.stack([outer_sum_one, outer_sum_two]).astype(f32)
    small_out = small_sum.reshape(-1)[:count].astype(f32)
    gains_out = small_out[:gain_size].reshape(norm_gains.shape)
    position_out = small_out[gain_size : gain_size + position_bias.size]
    depth_out = small_out[gain_size + position_bias.size :].reshape(taps, share)
    return (
        result,
        input_grad,
        gains_out,
        position_out,
        attend_out,
        merge_out,
        glu_out,
        depth_out,
        point_out,
        inner_out,
        outer_out,
    )


def solution(mesh):
    across, along = mesh.shape["dp"], mesh.shape["head"]
    fine = Mesh(mesh.devices.reshape(4, across // 4, along // 2, 2), ("p", "q", "y", "c"))
    every = ("p", "q", "y", "c")
    in_specs = (
        P(every, None),
        P(every, None),
        P(("p", "q"), None),
        P(None, every),
        P(every),
        P(every, None),
        P(every, None),
        P(every, None),
        P(None, every),
        P(every, None),
        P(None, None, every),
        P(None, every, None),
    )
    out_specs = (
        P(every, None),
        P(every, None),
        P(None, every),
        P(every),
        P(every, None),
        P(every, None),
        P(every, None),
        P(None, every),
        P(every, None),
        P(None, None, every),
        P(None, every, None),
    )
    return jax.shard_map(
        on_device, mesh=fine, in_specs=in_specs, out_specs=out_specs, check_vma=False
    )
```

```python
import jax
import jax.numpy as jnp
from jax import lax
from jax.experimental import pallas as pl
from jax.experimental.pallas import tpu as pltpu
from jax.sharding import Mesh
from jax.sharding import PartitionSpec as P

HEADS = 16
HD = 64
NB = 64
ROWS = 128
VMEM = 50 * 1024 * 1024


def matmul_in(left, right, dims):
    return lax.dot_general(left, right, (dims, ((), ())), preferred_element_type=jnp.float32)


def spread_of(bias):
    row = jnp.broadcast_to(bias, (ROWS, bias.shape[1]))
    return pltpu.roll(row, 0, 1, stride=1, stride_axis=0)


def half_mask(rows, half):
    lane = lax.broadcasted_iota(jnp.int32, (rows, 2 * HD), 1)
    return lane < HD if half == 0 else lane >= HD


def segment_at(position, first_end, second_end):
    return (position >= first_end).astype(jnp.int32) + (position >= second_end).astype(jnp.int32)


def weights_of(info_ref, spread_ref, raw, number):
    group = raw.shape[1]
    first_end, second_end, start = info_ref[0], info_ref[1], info_ref[2]
    shift = pl.multiple_of(group - start - number * ROWS, ROWS)
    bias = spread_ref[:, pl.ds(shift, group)]
    row = start + number * ROWS + lax.broadcasted_iota(jnp.int32, (ROWS, 1), 0)
    column = lax.broadcasted_iota(jnp.int32, (1, group), 1)
    same = segment_at(row, first_end, second_end) == segment_at(column, first_end, second_end)
    scores = jnp.where(same, raw * 0.125 + bias, -1e30)
    raised = jnp.exp(scores - jnp.max(scores, axis=1, keepdims=True))
    return raised * (1.0 / jnp.sum(raised, axis=1, keepdims=True))


def attend_kernel(info_ref, bias_ref, query_ref, key_ref, value_ref, out_ref, spread_ref, raw_ref, weight_ref):
    outs = []
    for half in range(2):
        mask = half_mask(query_ref.shape[0], half)
        query = jnp.where(mask, query_ref[...], jnp.bfloat16(0))
        raw_ref[half] = matmul_in(query, key_ref[...], ((1,), (1,)))
        spread_ref[half] = spread_of(bias_ref[0, half : half + 1])
    for half in range(2):
        for number in range(query_ref.shape[0] // ROWS):
            rows = pl.ds(number * ROWS, ROWS)
            weights = weights_of(info_ref, spread_ref.at[half], raw_ref[half, rows, :], number)
            weight_ref[half, rows, :] = weights.astype(jnp.bfloat16)
        outs.append(matmul_in(weight_ref[half], value_ref[...], ((1,), (0,))).astype(jnp.bfloat16))
    out_ref[...] = jnp.where(half_mask(query_ref.shape[0], 0), outs[0], outs[1])


def attend_back_kernel(
    info_ref,
    bias_ref,
    query_ref,
    key_ref,
    value_ref,
    grad_ref,
    query_grad_ref,
    key_grad_ref,
    value_grad_ref,
    diag_ref,
    spread_ref,
    weight_ref,
    score_ref,
    raw_ref,
    weight_grad_ref,
):
    group = key_ref.shape[0]
    outs, key_grads, value_grads = [], [], []
    for half in range(2):
        mask = half_mask(query_ref.shape[0], half)
        query = jnp.where(mask, query_ref[...], jnp.bfloat16(0))
        grad = jnp.where(mask, grad_ref[...], jnp.bfloat16(0))
        raw_ref[half] = matmul_in(query, key_ref[...], ((1,), (1,)))
        weight_grad_ref[half] = matmul_in(grad, value_ref[...], ((1,), (1,)))
        spread_ref[half] = spread_of(bias_ref[0, half : half + 1])
    diag_ref[...] = jnp.zeros(diag_ref.shape, jnp.float32)
    for half in range(2):
        mask = half_mask(query_ref.shape[0], half)
        query = jnp.where(mask, query_ref[...], jnp.bfloat16(0))
        grad = jnp.where(mask, grad_ref[...], jnp.bfloat16(0))
        for number in range(query_ref.shape[0] // ROWS):
            rows = pl.ds(number * ROWS, ROWS)
            weights = weights_of(info_ref, spread_ref.at[half], raw_ref[half, rows, :], number)
            weight_ref[half, rows, :] = weights.astype(jnp.bfloat16)
            weight_grad = weight_grad_ref[half, rows, :]
            inner = jnp.sum(weights * weight_grad, axis=1, keepdims=True)
            score_grad = weights * (weight_grad - inner)
            shift = pl.multiple_of(group - info_ref[2] - number * ROWS, ROWS)
            diag_ref[0, half, :, pl.ds(shift, group)] += score_grad
            score_ref[half, rows, :] = (score_grad * 0.125).astype(jnp.bfloat16)
        outs.append(matmul_in(score_ref[half], key_ref[...], ((1,), (0,))).astype(jnp.bfloat16))
        key_grads.append(matmul_in(score_ref[half], query, ((0,), (0,))))
        value_grads.append(matmul_in(weight_ref[half], grad, ((0,), (0,))))
    query_grad_ref[...] = jnp.where(half_mask(query_ref.shape[0], 0), outs[0], outs[1])
    key_grad_ref[...] = key_grads[0] + key_grads[1]
    value_grad_ref[...] = value_grads[0] + value_grads[1]


def attend_specs(rows, group, width, pairs):
    return [
        pl.BlockSpec(memory_space=pltpu.SMEM),
        pl.BlockSpec((1, 2, width), lambda h: (h, 0, 0)),
        pl.BlockSpec((rows, 2 * HD), lambda h: (0, h)),
        pl.BlockSpec((group, 2 * HD), lambda h: (0, h)),
        pl.BlockSpec((group, 2 * HD), lambda h: (0, pairs + h)),
    ]


def cost_of(heads, rows, group, products):
    return pl.CostEstimate(
        flops=2 * products * heads * rows * group * HD,
        bytes_accessed=4 * heads * HD * (rows + group),
        transcendentals=heads * rows * group,
    )


def attend(info, bias, query, both):
    pairs, _, width = bias.shape
    heads = 2 * pairs
    rows, group = query.shape[0], both.shape[0]
    return pl.pallas_call(
        attend_kernel,
        grid=(pairs,),
        in_specs=attend_specs(rows, group, width, pairs),
        out_specs=pl.BlockSpec((rows, 2 * HD), lambda h: (0, h)),
        out_shape=jax.ShapeDtypeStruct((rows, heads * HD), jnp.bfloat16),
        scratch_shapes=[
            pltpu.VMEM((2, ROWS, width), jnp.float32),
            pltpu.VMEM((2, rows, group), jnp.float32),
            pltpu.VMEM((2, rows, group), jnp.bfloat16),
        ],
        compiler_params=pltpu.CompilerParams(vmem_limit_bytes=VMEM),
        cost_estimate=cost_of(heads, rows, group, 2),
        name="attend",
    )(info, bias, query, both, both)


def attend_back(info, bias, query, both, grad):
    pairs, _, width = bias.shape
    heads = 2 * pairs
    rows, group = query.shape[0], both.shape[0]
    pair_block = pl.BlockSpec((rows, 2 * HD), lambda h: (0, h))
    group_block = pl.BlockSpec((group, 2 * HD), lambda h: (0, h))
    return pl.pallas_call(
        attend_back_kernel,
        grid=(pairs,),
        in_specs=attend_specs(rows, group, width, pairs) + [pair_block],
        out_specs=[
            pair_block,
            group_block,
            group_block,
            pl.BlockSpec((1, 2, ROWS, width), lambda h: (h, 0, 0, 0)),
        ],
        out_shape=[
            jax.ShapeDtypeStruct((rows, heads * HD), jnp.bfloat16),
            jax.ShapeDtypeStruct((group, heads * HD), jnp.float32),
            jax.ShapeDtypeStruct((group, heads * HD), jnp.float32),
            jax.ShapeDtypeStruct((pairs, 2, ROWS, width), jnp.float32),
        ],
        scratch_shapes=[
            pltpu.VMEM((2, ROWS, width), jnp.float32),
            pltpu.VMEM((2, rows, group), jnp.bfloat16),
            pltpu.VMEM((2, rows, group), jnp.bfloat16),
            pltpu.VMEM((2, rows, group), jnp.float32),
            pltpu.VMEM((2, rows, group), jnp.float32),
        ],
        compiler_params=pltpu.CompilerParams(vmem_limit_bytes=VMEM),
        cost_estimate=cost_of(heads, rows, group, 5),
        name="attend_back",
    )(info, bias, query, both, both, grad)


def diagonal_kernel(diag_ref, sums_ref):
    width = diag_ref.shape[3]
    for half in range(2):
        total = diag_ref[0, half]
        size = ROWS // 2
        while size >= 8:
            total = total[:size] + pltpu.roll(total[size:], width - size, 1)
            size //= 2
        for size in (4, 2, 1):
            total = total + pltpu.roll(pltpu.roll(total, 8 - size, 0), width - size, 1)
        sums_ref[0, half : half + 1] = total[0:1]


def diagonal_sums(diagonals):
    pairs, _, rows, width = diagonals.shape
    return pl.pallas_call(
        diagonal_kernel,
        grid=(pairs,),
        in_specs=[pl.BlockSpec((1, 2, rows, width), lambda h: (h, 0, 0, 0))],
        out_specs=pl.BlockSpec((1, 2, width), lambda h: (h, 0, 0)),
        out_shape=jax.ShapeDtypeStruct((pairs, 2, width), jnp.float32),
        compiler_params=pltpu.CompilerParams(vmem_limit_bytes=VMEM),
        name="diagonal_sums",
    )(diagonals)


LANES = 128
EDGE = 16


def reach_of(info_ref, rows, group):
    position = info_ref[2] + lax.broadcasted_iota(jnp.int32, (rows, LANES), 0)
    first_end, second_end = info_ref[0], info_ref[1]
    low = jnp.where(position >= second_end, second_end, jnp.where(position >= first_end, first_end, 0))
    high = jnp.where(position < first_end, first_end, jnp.where(position < second_end, second_end, group))
    return (low - position, high - position)


def within(reach, shift):
    if shift < 0:
        return reach[0] <= shift
    return reach[1] > shift


def fill(pad_ref, low_ref, mid_ref, high_ref):
    rows = mid_ref.shape[0]
    pad_ref[0:EDGE, :] = low_ref[...].astype(jnp.float32)
    pad_ref[EDGE : EDGE + rows, :] = mid_ref[...].astype(jnp.float32)
    pad_ref[EDGE + rows :, :] = high_ref[...].astype(jnp.float32)


def taps_of(pad_ref, depth_ref, reach, base, rows, taps, mirror):
    margin = (taps - 1) // 2
    total = jnp.zeros((rows, LANES), jnp.float32)
    for tap in range(taps):
        shift = margin - tap if mirror else tap - margin
        piece = pad_ref[EDGE + base + shift : EDGE + base + shift + rows, :] * depth_ref[tap : tap + 1, :]
        if shift:
            piece = jnp.where(within(reach, shift), piece, 0.0)
        total = total + piece
    return total


def conv_kernel(group, taps, info_ref, low_ref, mid_ref, high_ref, depth_ref, out_ref, pad_ref):
    fill(pad_ref, low_ref, mid_ref, high_ref)
    low, high = reach_of(info_ref, mid_ref.shape[0], group)
    for base in range(0, mid_ref.shape[0], STEP):
        reach = (low[base : base + STEP], high[base : base + STEP])
        out_ref[base : base + STEP, :] = taps_of(pad_ref, depth_ref, reach, base, STEP, taps, False)


STEP = 64


def conv_back_kernel(
    group,
    taps,
    info_ref,
    low_ref,
    mid_ref,
    high_ref,
    grad_low_ref,
    grad_mid_ref,
    grad_high_ref,
    depth_ref,
    out_ref,
    depth_grad_ref,
    pad_ref,
    grad_pad_ref,
    sum_ref,
):
    fill(pad_ref, low_ref, mid_ref, high_ref)
    fill(grad_pad_ref, grad_low_ref, grad_mid_ref, grad_high_ref)
    low, high = reach_of(info_ref, mid_ref.shape[0], group)
    margin = (taps - 1) // 2
    sum_ref[...] = jnp.zeros(sum_ref.shape, jnp.float32)
    for base in range(0, mid_ref.shape[0], STEP):
        reach = (low[base : base + STEP], high[base : base + STEP])
        out_ref[base : base + STEP, :] = taps_of(grad_pad_ref, depth_ref, reach, base, STEP, taps, True)
        grad = grad_pad_ref[EDGE + base : EDGE + base + STEP, :]
        for tap in range(taps):
            shift = tap - margin
            piece = pad_ref[EDGE + base + shift : EDGE + base + shift + STEP, :] * grad
            if shift:
                piece = jnp.where(within(reach, shift), piece, 0.0)
            sum_ref[8 * tap : 8 * tap + 8, :] += jnp.sum(piece.reshape(STEP // 8, 8, LANES), axis=0)
    for tap in range(taps):
        depth_grad_ref[tap : tap + 1, :] = jnp.sum(sum_ref[8 * tap : 8 * tap + 8, :], axis=0, keepdims=True)


def lane_block(rows):
    return pl.BlockSpec((rows, LANES), lambda i: (0, i))


def conv(info, low, mid, high, depth, group):
    rows, width = mid.shape
    taps = depth.shape[0]
    return pl.pallas_call(
        lambda *refs: conv_kernel(group, taps, *refs),
        grid=(width // LANES,),
        in_specs=[pl.BlockSpec(memory_space=pltpu.SMEM)]
        + [lane_block(EDGE), lane_block(rows), lane_block(EDGE), lane_block(taps)],
        out_specs=lane_block(rows),
        out_shape=jax.ShapeDtypeStruct((rows, width), jnp.float32),
        scratch_shapes=[pltpu.VMEM((rows + 2 * EDGE, LANES), jnp.float32)],
        compiler_params=pltpu.CompilerParams(vmem_limit_bytes=VMEM),
        cost_estimate=pl.CostEstimate(
            flops=2 * taps * rows * width, bytes_accessed=6 * rows * width, transcendentals=0
        ),
        name="conv",
    )(info, low, mid, high, depth)


def conv_back(info, low, mid, high, grad_low, grad_mid, grad_high, depth, group):
    rows, width = mid.shape
    taps = depth.shape[0]
    return pl.pallas_call(
        lambda *refs: conv_back_kernel(group, taps, *refs),
        grid=(width // LANES,),
        in_specs=[pl.BlockSpec(memory_space=pltpu.SMEM)]
        + [lane_block(EDGE), lane_block(rows), lane_block(EDGE)] * 2
        + [lane_block(taps)],
        out_specs=[lane_block(rows), lane_block(taps)],
        out_shape=[
            jax.ShapeDtypeStruct((rows, width), jnp.float32),
            jax.ShapeDtypeStruct((taps, width), jnp.float32),
        ],
        scratch_shapes=[
            pltpu.VMEM((rows + 2 * EDGE, LANES), jnp.float32),
            pltpu.VMEM((rows + 2 * EDGE, LANES), jnp.float32),
            pltpu.VMEM((8 * taps, LANES), jnp.float32),
        ],
        compiler_params=pltpu.CompilerParams(vmem_limit_bytes=VMEM),
        cost_estimate=pl.CostEstimate(
            flops=4 * taps * rows * width, bytes_accessed=8 * rows * width, transcendentals=0
        ),
        name="conv_back",
    )(info, low, mid, high, grad_low, grad_mid, grad_high, depth)


EPS = 1e-05
CORES = [(0, 1), (1, 0)]


def low(values):
    return values.astype(jnp.bfloat16)


def product(left_in, right_in):
    return jnp.dot(left_in, right_in, preferred_element_type=jnp.float32)


def left_product(left_in, right_in):
    return jnp.einsum("nd,nf->df", left_in, right_in, preferred_element_type=jnp.float32)


def right_product(left_in, right_in):
    return jnp.einsum("nf,df->nd", left_in, right_in, preferred_element_type=jnp.float32)


def swap(values, axis="c"):
    return lax.ppermute(values, axis, CORES)


def ordered(mine, other, place, dim=0):
    first = place == 0
    return jnp.concatenate([jnp.where(first, mine, other), jnp.where(first, other, mine)], axis=dim)


def choose(values, place, dim):
    return lax.dynamic_index_in_dim(values, place, dim, keepdims=False)


def pair_rows(values):
    return ordered(values, swap(values), lax.axis_index("c"))


def pair_sum(partial):
    place = lax.axis_index("c")
    halves = partial.reshape(2, partial.shape[0] // 2, partial.shape[1])
    received = swap(low(choose(halves, 1 - place, 0)))
    return choose(halves, place, 0) + received.astype(jnp.float32)


def gather_axis(values, axis):
    if lax.axis_size(axis) == 2:
        return ordered(values, swap(values, axis), lax.axis_index(axis))
    return lax.all_gather(values, axis, axis=0, tiled=True)


def pick(values, axis, dim):
    return choose(values, 1 - lax.axis_index(axis), dim)


def send(values, axis, dim):
    if lax.axis_size(axis) == 2:
        return swap(pick(values, axis, dim), axis)
    return lax.psum_scatter(values, axis, scatter_dimension=dim, tiled=False)


def add(values, received, axis, dim):
    if lax.axis_size(axis) != 2:
        return received
    kept = choose(values, lax.axis_index(axis), dim)
    return (kept.astype(jnp.float32) + received.astype(jnp.float32)).astype(values.dtype)


def together(*values):
    return lax.optimization_barrier(values)


def placed(parts):
    own, across, both, along = parts
    q, y = lax.axis_index("q"), lax.axis_index("y")
    result = jnp.zeros((own.shape[0], 2, 2) + own.shape[1:], own.dtype)
    for part, at_q, at_y in ((own, q, y), (across, 1 - q, y), (both, 1 - q, 1 - y), (along, q, 1 - y)):
        at = (0, at_q, at_y) + (0,) * (own.ndim - 1)
        result = lax.dynamic_update_slice(result, part[:, None, None], at)
    return result


def normalize(values):
    average = jnp.mean(values, axis=-1, keepdims=True)
    centred = values - average
    inverse = lax.rsqrt(jnp.mean(centred * centred, axis=-1, keepdims=True) + EPS)
    return (centred * inverse, inverse)


def norm_back(upstream, normed, inverse, gain):
    gain_grad = jnp.sum(upstream * normed, axis=0)
    scaled = upstream * gain
    back = inverse * (
        scaled
        - jnp.mean(scaled, axis=-1, keepdims=True)
        - normed * jnp.mean(scaled * normed, axis=-1, keepdims=True)
    )
    return (back, gain_grad)


def silu_slope(values):
    sigma = jax.nn.sigmoid(values)
    return sigma * (1.0 + values * (1.0 - sigma))


def split_normalize(values):
    width = values.shape[1]
    average = jnp.mean(values, axis=1)
    centred = values - average[:, None]
    spread = jnp.sum(centred * centred, axis=1)
    other = swap(jnp.stack([average, spread]))
    gap = average - other[0]
    whole = spread + other[1] + (0.5 * width) * gap * gap
    inverse = lax.rsqrt(whole / (2 * width) + EPS)
    middle = 0.5 * (average + other[0])
    return ((values - middle[:, None]) * inverse[:, None], inverse[:, None])


def split_norm_back(upstream, normed, inverse, gain):
    gain_grad = jnp.sum(upstream * normed, axis=0)
    scaled = upstream * gain
    sums = jnp.stack([jnp.sum(scaled, axis=1), jnp.sum(scaled * normed, axis=1)])
    means = (sums + swap(sums)) / (2 * scaled.shape[1])
    back = inverse * (scaled - means[0][:, None] - normed * means[1][:, None])
    return (back, gain_grad)


def feed_forward(hidden, gain, inner, outer):
    rows = hidden.shape[0]
    normed, inverse = normalize(hidden)
    entry = low(normed * gain)
    both = jnp.concatenate([entry, swap(entry)], axis=0)
    middle = right_product(both, inner)
    activated = low(jax.nn.silu(middle))
    partial = product(activated, outer)
    received = swap(low(partial[rows:]))
    result = hidden + 0.5 * (partial[:rows] + received.astype(jnp.float32))
    return (result, (normed, inverse, both, middle, activated))


def feed_back(upstream, gain, inner, outer, kept, *held):
    normed, inverse, both, middle, activated = kept
    rows = upstream.shape[0]
    half = low(0.5 * upstream)
    half_both = jnp.concatenate([half, swap(half)], axis=0)
    active_grad = right_product(half_both, outer)
    middle_grad = low(active_grad * silu_slope(middle))
    if held:
        middle_grad, *held = together(middle_grad, *held)
    partial = product(middle_grad, inner)
    received = swap(low(partial[rows:]))
    entry_grad = partial[:rows] + received.astype(jnp.float32)
    back, gain_grad = norm_back(entry_grad, normed, inverse, gain)

    eighth = middle.shape[1] // 8

    def inner_grad(first, end, tie=None):
        columns = middle_grad[:, first * eighth : end * eighth]
        if tie is None:
            return left_product(columns, both)
        columns, tie = together(columns, tie)
        return (left_product(columns, both), tie)

    def outer_grad(first, end):
        return left_product(activated[:, first * eighth : end * eighth], half_both)

    return (upstream + back, gain_grad, inner_grad, outer_grad, *held)


def bucket_hits(group):
    offset = group - jnp.arange(2 * group, dtype=jnp.int32)
    distance = jnp.abs(offset)
    level = jnp.zeros_like(distance)
    for power in range(1, 14):
        level = level + (distance >= 2**power).astype(jnp.int32)
    plain = jnp.where(distance < 16, distance, jnp.minimum(12 + level, 31))
    bucket = plain + 32 * (offset < 0).astype(jnp.int32)
    return bucket[:, None] == jnp.arange(NB, dtype=jnp.int32)[None, :]


def halos(values):
    count = lax.axis_size("y")
    forward = [(i, i + 1) for i in range(count - 1)]
    backward = [(target, source) for source, target in forward]
    return (
        lax.ppermute(values[-EDGE:], "y", forward),
        lax.ppermute(values[:EDGE], "y", backward),
    )


CHIPS = ("p", "q", "y")


def on_device(
    frames,
    cotangent,
    lengths,
    norm_gains,
    position_bias,
    attend_weight,
    merge_weight,
    glu_weight,
    depth_weight,
    point_weight,
    inner_weight,
    outer_weight,
):
    core = lax.axis_index("c")
    grid = tuple(lax.axis_size(axis) for axis in CHIPS)
    chips = grid[0] * grid[1] * grid[2]
    rows, width = frames.shape
    pair = 2 * rows
    group = pair * grid[2]
    half = width // 2
    share = attend_weight.shape[0]
    units = inner_weight.shape[2]
    taps = depth_weight.shape[0]
    heads = HEADS // 2
    f32 = jnp.float32

    small = jnp.concatenate([norm_gains.reshape(-1), position_bias, depth_weight.reshape(-1)])
    count = small.shape[0]
    small_rows = -(-2 * count // (16 * width)) * 16
    small_both = ordered(small[None], swap(small[None]), core).reshape(-1)
    small_both = jnp.pad(small_both, (0, small_rows * width - 2 * count)).reshape(small_rows, width)

    inner_pack = inner_weight[0].T
    outer_pack = jnp.concatenate([outer_weight[0], small_both], axis=0)
    pack_two = jnp.concatenate([inner_weight[1].T, outer_weight[1]], axis=0)
    attend_weight, glu_weight = together(attend_weight, glu_weight, outer_pack)[:2]

    def own_columns(weight, shape, dim):
        parts = weight.reshape((share,) + shape)
        mine = choose(parts, core, dim).reshape(share, -1)
        other = swap(choose(parts, 1 - core, dim).reshape(share, -1))
        return ordered(mine, other, core)

    attend_part = own_columns(attend_weight, (3, 2, half), 2)
    glu_part = own_columns(glu_weight, (2, chips, 2, share), 3)
    mixed_pack = jnp.concatenate(
        [attend_part.reshape(-1, width), glu_part, merge_weight, point_weight], axis=0
    )

    square = grid[1] == 2 and grid[2] == 2
    marks = [0]
    for size in (3 * share, 2 * share, share, share):
        marks.append(marks[-1] + size)

    def gather_p(values):
        return lax.all_gather(values, "p", axis=0)

    def in_halves(*parts):
        parts = [part.reshape(grid[0], units, width) for part in parts]
        near = [part[:, : units // 2].reshape(-1, width) for part in parts]
        far = [part[:, units // 2 :].reshape(-1, width) for part in parts]
        return jnp.concatenate(near + far, axis=0)

    if square:
        inner = gather_p(inner_pack)
        two_x, two_y = together(swap(pack_two, "q"), swap(pack_two, "y"))
        pack_two = jnp.stack([pack_two, two_x, swap(two_x, "y"), two_y])
        whole_one = gather_p(outer_pack)
        inner, pack_two = together(inner.reshape(-1, width), pack_two)
        inner_x, inner_y = together(swap(inner, "q"), swap(inner, "y"))
        mixed_pack, inner_x, inner_y = together(mixed_pack, inner_x, inner_y)
        mixed = gather_p(mixed_pack)
        inner_xy = swap(inner_y, "q")
        outer = whole_one[:, :units].reshape(-1, width)
        tiny = whole_one[:, units:]
        outer, tiny = together(outer, tiny)
        across = [(0, 3), (3, 0), (1, 2), (2, 1)]
        tiny_xy = lax.ppermute(tiny, ("q", "y"), across)
        outer_x, outer_y, tiny_x, tiny_y, tiny_xy = together(
            swap(outer, "q"), swap(outer, "y"), swap(tiny, "q"), swap(tiny, "y"), tiny_xy
        )
        small_full = placed((tiny, tiny_x, tiny_xy, tiny_y)).reshape(chips, -1)
        outer_xy = swap(outer_x, "y")
        whole_two = gather_p(pack_two).reshape(chips, 2 * units, width)
        attend_part = mixed[:, : marks[1]].reshape(grid[0], 2 * share, 3 * half)
        rest_part = mixed[:, marks[1] :]
        attend_part, rest_part = together(attend_part, rest_part)
        attend_x = swap(attend_part, "q")
        inner_xy, outer_xy, attend_x, attend_part, rest_part = together(
            inner_xy, outer_xy, attend_x, attend_part, rest_part
        )
        inner_one = in_halves(inner, inner_x, inner_xy, inner_y)
        outer_one = in_halves(outer, outer_x, outer_xy, outer_y)
        attend_y, rest_x = swap(attend_part, "y"), swap(rest_part, "q")
    else:
        inner_one = lax.all_gather(inner_pack, CHIPS, axis=0, tiled=True)
        whole_one = lax.all_gather(outer_pack, CHIPS, axis=0)
        mixed = lax.all_gather(mixed_pack, CHIPS, axis=0)
        whole_two = lax.all_gather(pack_two, CHIPS, axis=0)
        outer_one = whole_one[:, :units].reshape(chips * units, width)
        small_full = whole_one[:, units:].reshape(chips, -1)

    small_full = small_full[:, : 2 * count].reshape(chips, 2, count)
    gain_size = norm_gains.size
    gains = small_full[..., :gain_size].reshape(chips, 2, 6, -1).astype(f32)
    gain_table = gains.transpose(2, 0, 1, 3).reshape(6, width)
    gain_mid = choose(gains[:, :, 3], core, 1).reshape(half)
    bias_table = small_full[..., gain_size : gain_size + position_bias.size].reshape(NB, 2, heads)
    bias_table = choose(bias_table, core, 1)
    depth = choose(small_full[..., gain_size + position_bias.size :], core, 1)
    depth = depth.reshape(chips, taps, share).transpose(1, 0, 2).reshape(taps, half).astype(f32)

    start = lax.axis_index("y") * pair
    info = jnp.stack([lengths[0, 0], lengths[0, 0] + lengths[0, 1], start.astype(jnp.int32)])
    hits = bucket_hits(group)
    bias = jnp.einsum("bh,wb->hw", bias_table, hits.astype(jnp.bfloat16), preferred_element_type=f32)
    bias = bias.reshape(heads // 2, 2, -1)

    hidden = frames.astype(f32)
    first, first_kept = feed_forward(hidden, gain_table[0], inner_one, outer_one)
    if square:
        first, attend_y, rest_part = together(first, attend_y, rest_part)
        rest_y = swap(rest_part, "y")
        attend_full = placed((attend_part, attend_x, swap(attend_y, "q"), attend_y))
    else:
        attend_full = mixed[:, : marks[1]]
    attend_full = attend_full.reshape(width, 3 * half)
    normed_att, inverse_att = normalize(first)
    att_entry = pair_rows(low(normed_att * gain_table[1]))
    triple = low(product(att_entry, attend_full))
    query = triple[:, :half]
    key_value = triple[:, half:]
    if square:
        key_value, rest_x, rest_y = together(key_value, rest_x, rest_y)
        rest_xy = swap(rest_y, "q")
    both = gather_axis(key_value, "y")
    attended = attend(info, bias, query, both)
    if square:
        attended, rest_xy = together(attended, rest_xy)
        rest = placed((rest_part, rest_x, rest_xy, rest_y)).reshape(chips, -1, width)
    else:
        rest = mixed[:, marks[1] :]
    marks = [mark - marks[1] for mark in marks]
    glu_full = rest[:, : marks[2]].reshape(width, width)
    merge_half = rest[:, marks[2] : marks[3]]
    point_full = rest[:, marks[3] : marks[4]].reshape(half, width)
    sides = merge_half.reshape(2, chips // 2, share, width)
    merge_full = ordered(
        choose(sides, core, 0)[:, None], swap(choose(sides, 1 - core, 0))[:, None], core, 1
    ).reshape(half, width)
    second = first + pair_sum(product(attended, merge_full))
    normed_conv, inverse_conv = normalize(second)
    conv_entry = pair_rows(low(normed_conv * gain_table[2]))
    gate_up = product(conv_entry, glu_full)
    gate_sig = jax.nn.sigmoid(gate_up[:, half:])
    glu_rows = low(gate_up[:, :half] * gate_sig)
    glu_low, glu_high = halos(glu_rows)
    mixed_rows = conv(info, glu_low, glu_rows, glu_high, depth, group)
    normed_mid, inverse_mid = split_normalize(mixed_rows)
    activated = normed_mid * gain_mid
    swish = low(jax.nn.silu(activated))
    third = second + pair_sum(product(swish, point_full))
    inner_two = whole_two[:, :units].reshape(chips * units, width)
    outer_two = whole_two[:, units:].reshape(chips * units, width)
    fourth, fourth_kept = feed_forward(third, gain_table[4], inner_two, outer_two)
    normed_last, inverse_last = normalize(fourth)
    result = low(normed_last * gain_table[5])

    def by_chip(values):
        return values.reshape(grid + (values.shape[0] // chips, values.shape[1]))

    def last_sum(values):
        return lax.psum_scatter(values, "p", scatter_dimension=0, tiled=False)

    size = grid[0] * units // 2

    def early_sum(grad):
        shape = (grid[0], 4) if square else grid
        return last_sum(low(grad).reshape(shape + (units, width)))

    def small_of(table_sums, depth_grad, gain_zero, gain_one, gain_two, gain_three, gain_four, gain_five):
        table_grad = jnp.einsum(
            "hw,wb->bh", diagonal_sums(table_sums).reshape(heads, -1), hits.astype(f32), precision=lax.Precision.HIGHEST
        )

        def of_core(values, dim):
            empty = jnp.zeros_like(values)
            return jnp.stack(
                [jnp.where(core == 0, values, empty), jnp.where(core == 1, values, empty)], axis=dim
            )

        gain_three = of_core(gain_three.reshape(chips, share), 1).reshape(width)
        gain_grads = jnp.stack([gain_zero, gain_one, gain_two, gain_three, gain_four, gain_five])
        small_grads = jnp.concatenate(
            [
                gain_grads.reshape(6, chips, 2, share).transpose(1, 2, 0, 3).reshape(chips, 2, -1),
                of_core(table_grad, 1).reshape(chips, 2, -1),
                of_core(depth_grad.reshape(taps, chips, share).transpose(1, 0, 2), 1).reshape(
                    chips, 2, -1
                ),
            ],
            axis=2,
        )
        small_sum = choose(small_grads, core, 1) + swap(choose(small_grads, 1 - core, 1))
        small_sum = small_sum.reshape(grid + (count,))
        if square:
            at_q, at_y = lax.axis_index("q"), lax.axis_index("y")
            here = [choose(small_sum, at_q, 1), choose(small_sum, 1 - at_q, 1)]
            across = [(0, 3), (3, 0), (1, 2), (2, 1)]
            own = choose(here[0], at_y, 1)
            parts = together(
                choose(here[0], 1 - at_y, 1), choose(here[1], at_y, 1), choose(here[1], 1 - at_y, 1)
            )
            parts = together(
                swap(parts[0], "y"), swap(parts[1], "q"), lax.ppermute(parts[2], ("q", "y"), across)
            )
            small_sum = own + parts[0] + parts[1] + parts[2]
        else:
            small_sum = add(small_sum, send(small_sum, "y", 2), "y", 2)
            small_sum = add(small_sum, send(small_sum, "q", 1), "q", 1)
        one_rows = -(-count // (16 * width)) * 16
        small_sum = jnp.pad(low(small_sum), ((0, 0), (0, one_rows * width - count)))
        small_sum = small_sum.reshape(grid[0], one_rows, width)
        return small_sum

    grad_fourth, gain_five = norm_back(
        cotangent.astype(f32), normed_last, inverse_last, gain_table[5]
    )
    grad_third, gain_four, inner_two_grad, outer_two_grad = feed_back(
        grad_fourth, gain_table[4], inner_two, outer_two, fourth_kept
    )

    if square:
        outer_two_rows = low(outer_two_grad(0, 8)).reshape(grid[0], 4, units, width)
        outer_two_a, grad_third = together(outer_two_rows[:, 1:3], grad_third)
        outer_two_a = swap(outer_two_a, "q")
    else:
        outer_two_sum = early_sum(outer_two_grad(0, 8))

    conv_out_grad = pair_rows(low(grad_third))
    swish_grad = right_product(conv_out_grad, point_full)
    act_grad = swish_grad * silu_slope(activated)
    mixed_grad, gain_three = split_norm_back(act_grad, normed_mid, inverse_mid, gain_mid)
    mixed_low = low(mixed_grad)
    grad_low, grad_high = halos(mixed_low)
    inner_two_rows, mixed_low = inner_two_grad(0, 8, mixed_low)
    point_grad = by_chip(low(left_product(swish, conv_out_grad)))
    point_a = send(point_grad, "q", 1)
    if square:
        mixed_low, point_a = together(mixed_low, point_a)
    point_half = add(point_grad, point_a, "q", 1)
    point_b = send(point_half, "y", 1)
    inner_two_sum = early_sum(inner_two_rows)
    glu_back, depth_grad = conv_back(
        info, glu_low, glu_rows, glu_high, grad_low, mixed_low, grad_high, depth, group
    )
    value_part = gate_up[:, :half]
    gate_grad = low(
        jnp.concatenate(
            [glu_back * gate_sig, glu_back * value_part * gate_sig * (1.0 - gate_sig)], axis=1
        )
    )
    conv_entry_grad = pair_sum(right_product(gate_grad, glu_full))
    glu_grad = by_chip(low(left_product(conv_entry, gate_grad)))
    back_conv, gain_two = norm_back(conv_entry_grad, normed_conv, inverse_conv, gain_table[2])
    grad_second = grad_third + back_conv

    att_out_grad = pair_rows(low(grad_second))
    glu_a = send(glu_grad, "y", 2)
    attended_grad = low(right_product(att_out_grad, merge_full))
    query_grad, key_grad, value_grad, table_sums = attend_back(info, bias, query, both, attended_grad)
    query_grad, key_grad, value_grad, glu_a = together(query_grad, key_grad, value_grad, glu_a)
    if square:
        query_grad, outer_two_a, point_b = together(query_grad, outer_two_a, point_b)
    att_out_grad, query_grad = together(att_out_grad, query_grad)
    merge_grad = low(left_product(attended, att_out_grad)).reshape(chips // 2, 2, share, width)
    merge_grad = ordered(
        choose(merge_grad, core, 1)[None], swap(choose(merge_grad, 1 - core, 1))[None], core
    )
    merge_grad = by_chip(merge_grad.reshape(chips * share, width))
    glu_half = add(glu_grad, glu_a, "y", 2)
    both_grad = jnp.concatenate([key_grad, value_grad], axis=1).reshape(grid[2], pair, width)
    if grid[2] == 2:
        place = lax.axis_index("y")
        both_received = swap(low(choose(both_grad, 1 - place, 0)), "y")
        both_grad = low(choose(both_grad, place, 0) + both_received.astype(f32))
    else:
        both_received = low(lax.psum_scatter(both_grad, "y", scatter_dimension=0, tiled=False))
        both_grad = both_received
    if square:
        outer_two_b = low(outer_two_rows[:, 3].astype(f32) + outer_two_a[:, 1].astype(f32))
        glu_b, merge_a, outer_two_b, both_grad = together(
            pick(glu_half, "q", 1),
            pick(merge_grad, "q", 1),
            outer_two_b,
            both_grad,
        )
        glu_b, merge_a = swap(glu_b, "q"), swap(merge_a, "q")
        outer_two_b = swap(outer_two_b, "y")
    else:
        glu_b, merge_a = send(glu_half, "q", 1), send(merge_grad, "q", 1)
    triple_grad = jnp.concatenate([query_grad, both_grad], axis=1)
    attend_grad = low(left_product(att_entry, triple_grad))
    attend_grad = attend_grad.reshape(grid + (2 * share, 3 * half))
    att_entry_grad = pair_sum(right_product(triple_grad, attend_full))
    back_att, gain_one = norm_back(att_entry_grad, normed_att, inverse_att, gain_table[1])
    grad_first = grad_second + back_att
    attend_sum = last_sum(attend_grad)
    if square:
        outer_two_sum = outer_two_rows[:, 0].astype(f32) + outer_two_a[:, 0].astype(f32)
    input_grad, gain_zero, inner_one_grad, outer_one_grad, glu_b = feed_back(
        grad_first, gain_table[0], inner_one, outer_one, first_kept, glu_b
    )
    if square:
        near_o, near_i, inner_two_sum = together(
            low(outer_one_grad(1, 3)), low(inner_one_grad(2, 4)), inner_two_sum
        )
        near_o, near_i = swap(near_o, "q"), swap(near_i, "y")
    if square:
        near_o, near_i, glu_b, outer_two_b, far_o, far_i, merge_a = together(
            near_o,
            near_i,
            glu_b,
            outer_two_b,
            low(outer_one_grad(5, 7)),
            low(inner_one_grad(6, 8)),
            merge_a,
        )
    edge_half = add(merge_grad, merge_a, "q", 1)
    edge_b = send(edge_half, "y", 1)
    edge_b, table_sums, depth_grad, gain_one, gain_two, gain_three, gain_four, gain_five = together(
        edge_b, table_sums, depth_grad, gain_one, gain_two, gain_three, gain_four, gain_five
    )
    mixed_sum = [add(glu_half, glu_b, "q", 1), add(point_half, point_b, "y", 1)]
    if square:
        outer_two_sum = low(outer_two_sum + outer_two_b.astype(f32))
        mixed_sum += [outer_two_sum, add(edge_half, edge_b, "y", 1)]
    mixed_sum = jnp.concatenate(mixed_sum, axis=1)
    if square:
        mixed_sum = last_sum(mixed_sum)

        def second(first, got_o, got_i):
            return together(
                low(outer_one_grad(first + 3, first + 4) + got_o[size:].astype(f32)),
                low(inner_one_grad(first + 1, first + 2) + got_i[:size].astype(f32)),
            )

        def third(first, got_o, got_i, end_o, end_i):
            sum_o = outer_one_grad(first, first + 1) + got_o[:size].astype(f32)
            sum_i = inner_one_grad(first, first + 1) + got_i[size:].astype(f32)
            sums = [low(sum_i + end_i.astype(f32)), low(sum_o + end_o.astype(f32))]
            return [part.reshape(grid[0], units // 2, width) for part in sums]

        near = second(0, near_o, near_i)
        across_q = jnp.concatenate([far_o, near[1]], axis=0)
        across_y = jnp.concatenate([far_i, near[0]], axis=0)
        across_q, across_y = together(across_q, across_y)
        across_q, across_y = swap(across_q, "q"), swap(across_y, "y")
        small_sum = small_of(
            table_sums, depth_grad, gain_zero, gain_one, gain_two, gain_three, gain_four, gain_five
        )
        across_q, across_y, small_sum, attend_sum = together(across_q, across_y, small_sum, attend_sum)
        far_o, far_i = across_q[: 2 * size], across_y[: 2 * size]
        near = [across_y[2 * size :], across_q[2 * size :]]
        near = third(0, near_o, near_i, *near)
        far_o, attend_sum = together(far_o, attend_sum)
        far = second(4, far_o, far_i)
        far = together(swap(far[0], "y"), swap(far[1], "q"))
        far = third(4, far_o, far_i, *far)
    else:
        mixed_sum = last_sum(mixed_sum)
        edge_sum = last_sum(edge_b)
        small_sum = small_of(
            table_sums, depth_grad, gain_zero, gain_one, gain_two, gain_three, gain_four, gain_five
        )
        inner_sum_one = by_chip(low(inner_one_grad(0, 8)))
        outer_sum_one = by_chip(low(outer_one_grad(0, 8)))
        inner_sum_one = send(send(inner_sum_one, "y", 2), "q", 1)
        outer_sum_one = send(send(outer_sum_one, "y", 2), "q", 1)
        inner_sum_two = send(send(inner_two_sum, "y", 1), "q", 0)
        outer_sum_two = send(send(outer_two_sum, "y", 1), "q", 0)
    attend_half = add(attend_sum, send(attend_sum, "q", 0), "q", 0)
    attend_sum = add(attend_half, send(attend_half, "y", 0), "y", 0)

    if square:
        one_sum = jnp.concatenate(near + far + [small_sum], axis=1)
        one_sum, mixed_sum, inner_two_sum = together(one_sum, mixed_sum, inner_two_sum)
        one_sum = last_sum(one_sum)
        inner_two_a = swap(inner_two_sum[2:], "y")
        inner_two_b = swap(low(inner_two_sum[1].astype(f32) + inner_two_a[0].astype(f32)), "q")
        inner_sum_two = inner_two_sum[0].astype(f32) + inner_two_a[1].astype(f32)
        inner_sum_two = low(inner_sum_two + inner_two_b.astype(f32))
        quarters = [one_sum[at * (units // 2) : (at + 1) * (units // 2)] for at in range(4)]
        inner_sum_one = jnp.concatenate([quarters[0], quarters[2]])
        outer_sum_one = jnp.concatenate([quarters[1], quarters[3]])
        small_sum = one_sum[2 * units :]
        outer_sum_two = mixed_sum[3 * share : 3 * share + units]
        edge_sum = mixed_sum[3 * share + units :]
    else:
        one_sum = last_sum(jnp.concatenate([inner_sum_one, outer_sum_one, small_sum], axis=1))
        inner_sum_one, outer_sum_one = one_sum[:units], one_sum[units : 2 * units]
        small_sum = one_sum[2 * units :]

    def whole_columns(values, shape, dim):
        parts = values.reshape(2, share, -1)
        mine = choose(parts, core, 0)
        other = swap(choose(parts, 1 - core, 0))
        joined = ordered(
            jnp.expand_dims(mine.reshape((share,) + shape), dim),
            jnp.expand_dims(other.reshape((share,) + shape), dim),
            core,
            dim,
        )
        return joined.reshape(share, -1).astype(f32)

    attend_out = whole_columns(attend_sum, (3, half), 2)
    glu_out = whole_columns(mixed_sum[: 2 * share], (2, chips, share), 3)
    point_out = mixed_sum[2 * share : 3 * share].astype(f32)
    merge_out = edge_sum.astype(f32)
    inner_out = jnp.stack([inner_sum_one.T, inner_sum_two.T]).astype(f32)
    outer_out = jnp.stack([outer_sum_one, outer_sum_two]).astype(f32)
    small_out = small_sum.reshape(-1)[:count].astype(f32)
    gains_out = small_out[:gain_size].reshape(norm_gains.shape)
    position_out = small_out[gain_size : gain_size + position_bias.size]
    depth_out = small_out[gain_size + position_bias.size :].reshape(taps, share)
    return (
        result,
        input_grad,
        gains_out,
        position_out,
        attend_out,
        merge_out,
        glu_out,
        depth_out,
        point_out,
        inner_out,
        outer_out,
    )


def solution(mesh):
    across, along = mesh.shape["dp"], mesh.shape["head"]
    fine = Mesh(mesh.devices.reshape(4, across // 4, along // 2, 2), ("p", "q", "y", "c"))
    every = ("p", "q", "y", "c")
    in_specs = (
        P(every, None),
        P(every, None),
        P(("p", "q"), None),
        P(None, every),
        P(every),
        P(every, None),
        P(every, None),
        P(every, None),
        P(None, every),
        P(every, None),
        P(None, None, every),
        P(None, every, None),
    )
    out_specs = (
        P(every, None),
        P(every, None),
        P(None, every),
        P(every),
        P(every, None),
        P(every, None),
        P(every, None),
        P(None, every),
        P(every, None),
        P(None, None, every),
        P(None, every, None),
    )
    return jax.shard_map(
        on_device, mesh=fine, in_specs=in_specs, out_specs=out_specs, check_vma=False
    )
```
